256 devices in a mesh: win: 32 (over y, x, core), tile: 8 (over z).
Axes of the slice: x: 4, y: 4, z: 8, core: 2. Of those that a mesh axis runs over, the one named last changes fastest.
Arguments:
- increment: float32 [32, 3, 137, 64, 128], P('win', None, None, 'tile'), may hold values from -4 to 4
- forcing: float32 [32, 3, 137, 64, 128], P('win', None, None, 'tile'), may hold values from -6 to 6
- error_root: float32 [411, 411], replicated, may hold values from -0.09375 to 0.09375
- physics: float32 [32, 411, 411], P('win'), may hold values from -0.3125 to 0.3125
- coefficients: float32 [32, 4, 64, 128], P('win', None, 'tile'), may hold values from 0.04 to 0.24
- obs_index: int32 [3, 32, 4096], P(None, 'win', 'tile'), may hold values from 0 to 409, as said below
- obs_frac: float32 [2, 32, 4096], P(None, 'win', 'tile'), may hold values from 0 to 1
- obs_value: float32 [32, 4096], P('win', 'tile'), may hold values from -6 to 6
- obs_count: int32 [32, 8], P('win', 'tile'), may hold values from 128 to 512, as said below
Outputs:
- summed: float32 [32, 3, 137, 64, 128], P('win', None, None, 'tile')
- departure: float32 [32, 4096], P('win', 'tile')
The draws below stay inside these ranges and needn't reach their ends.
Inputs may be any that keep to these rules, and one draw needn't show every extreme that they name: `obs_index`: x < 64, y <= 126, r mod 137 <= 135. Of each block of 512 slots at most 128 have x // 8 equal to one value; in every sub-window one value of x // 8 takes exactly 128 slots of every block. `obs_count`: every sub-window has one block with all 512 slots live.
All inputs are finite; a program needn't handle non-finite values.
Results may differ from the reference program's by a relative error of at most 0.0001.
Values sent between devices are 32-bit elements; how exact they have to be, the bound alone decides.
No kernel may reach another device: no remote copies, remote signals or barrier semaphores. Data moves between devices by JAX's collectives and lax.ppermute only.
A program may use at most 192 MiB of HBM per device.

```python
import jax
import jax.numpy as jnp
from jax import lax

FIELDS = 3
LEV = 137
STEPS = 6
CX = 8
NY = 128
OBS_DEV = 512
SUBWIN = 32
NX = 64
ROWS = 411
CAP = 128
OBS = 4096
N_TILE = 8


def draw_obs_index(key, part):
    key = jax.random.fold_in(key, 11)
    keys = jax.random.split(key, 6)
    slot_ids = jnp.arange(OBS_DEV)
    offset = jax.random.randint(keys[0], (), 0, N_TILE)
    busy_tile = (jnp.arange(SUBWIN) + offset) % N_TILE
    others = (busy_tile[:, None] + 1 + (slot_ids[None, :] - CAP) % (N_TILE - 1)) % N_TILE
    owner_sorted = jnp.where(slot_ids[None, :] < CAP, busy_tile[:, None], others)
    owner_sorted = jnp.broadcast_to(owner_sorted[:, None, :], (SUBWIN, N_TILE, OBS_DEV))
    scores = jax.random.randint(keys[1], (SUBWIN, N_TILE, OBS_DEV), 0, 1 << 20) * OBS_DEV + slot_ids
    order = jnp.argsort(scores, axis=-1, stable=True)
    owner_ids = jnp.take_along_axis(owner_sorted, order, axis=-1).reshape(SUBWIN, OBS)
    column_x = owner_ids * CX + jax.random.randint(keys[2], (SUBWIN, OBS), 0, CX)
    column_y = jax.random.randint(keys[3], (SUBWIN, OBS), 0, NY - 1)
    level_ids = jax.random.randint(keys[4], (SUBWIN, OBS), 0, LEV - 1)
    field_ids = jax.random.randint(keys[5], (SUBWIN, OBS), 0, FIELDS)
    row_ids = field_ids * LEV + level_ids
    return jnp.stack([column_x, column_y, row_ids], 0).astype(jnp.int32)


def draw_obs_count(key, part):
    key = jax.random.fold_in(key, 23)
    keys = jax.random.split(key, 2)
    counts = jax.random.randint(keys[0], (SUBWIN, N_TILE), OBS_DEV // 4, OBS_DEV + 1)
    full_block = jax.random.randint(keys[1], (SUBWIN, 1), 0, N_TILE)
    counts = jnp.where(jnp.arange(N_TILE)[None, :] == full_block, OBS_DEV, counts)
    return counts.astype(jnp.int32)


def steps_of(rng, dims, shards, least, high):
    def one(dim, blocks):
        steps = jax.random.uniform(jax.random.fold_in(jax.random.fold_in(rng, 6), dim), (blocks,), jnp.float32, least / len(shards), high / len(shards))
        return jnp.repeat(jnp.exp(steps), dims[dim] // blocks).reshape((-1,) + (1,) * (len(dims) - dim - 1))

    level = one(*shards[0])
    for cut in shards[1:]:
        level = level * one(*cut)
    return level


def noise(own_key, dims, scale, bound, cuts=(), dtype=jnp.bfloat16):
    result = scale * jax.random.normal(own_key, dims, jnp.float32)
    if cuts:
        result = result * steps_of(own_key, dims, cuts, -0.22, 0.18)
    return jnp.clip(result, -bound, bound).astype(dtype)


def setup_inputs(seed: int = 0) -> dict:
    splits = jax.random.split(jax.random.key(seed), 10)
    increment = noise(splits[0], (SUBWIN, FIELDS, LEV, NX, NY), 0.5, 4.0, ((0, 32), (3, 8)), jnp.float32)
    forcing = noise(splits[1], (SUBWIN, FIELDS, LEV, NX, NY), 1.0, 6.0, ((0, 32), (3, 8)), jnp.float32)
    error_root = noise(splits[2], (ROWS, ROWS), (9 * ROWS) ** -0.5, 0.09375, (), jnp.float32)
    physics = noise(splits[3], (SUBWIN, ROWS, ROWS), ROWS ** -0.5, 0.3125, ((0, 32),), jnp.float32)
    coefficients = jnp.clip(0.04 + 0.19999999552965164 * jax.random.uniform(splits[4], (SUBWIN, 4, NX, NY), jnp.float32) ** steps_of(splits[4], (SUBWIN, 4, NX, NY), ((0, 32), (2, 8)), -0.2, 0.2), 0.04, 0.24)
    obs_index = draw_obs_index(jax.random.fold_in(splits[9], 71), 0)
    obs_frac = jnp.clip(1.0 * jax.random.uniform(splits[6], (2, SUBWIN, OBS), jnp.float32) ** steps_of(splits[6], (2, SUBWIN, OBS), ((1, 32), (2, 8)), -0.2, 0.2), 0.0, 1.0)
    obs_value = noise(splits[7], (SUBWIN, OBS), 1.0, 6.0, ((0, 32), (1, 8)), jnp.float32)
    obs_count = draw_obs_count(jax.random.fold_in(splits[9], 71), 0)
    return dict(increment=increment, forcing=forcing, error_root=error_root, physics=physics, coefficients=coefficients, obs_index=obs_index, obs_frac=obs_frac, obs_value=obs_value, obs_count=obs_count)


def model_step(field_state, stencil_rates, jacobian):
    padded = jnp.pad(field_state, ((0, 0), (1, 1), (1, 1)))
    smooth = field_state + stencil_rates[0] * (padded[:, 2:, 1:-1] - field_state)
    smooth = smooth + stencil_rates[1] * (padded[:, :-2, 1:-1] - field_state)
    smooth = smooth + stencil_rates[2] * (padded[:, 1:-1, 2:] - field_state)
    smooth = smooth + stencil_rates[3] * (padded[:, 1:-1, :-2] - field_state)
    flat_state = smooth.reshape(smooth.shape[0], -1)
    column_mixed = flat_state + 0.2 * jnp.dot(jacobian, flat_state, precision=lax.Precision.HIGHEST, preferred_element_type=jnp.float32)
    return column_mixed.reshape(smooth.shape)


def reference(increment, forcing, error_root, physics, coefficients, obs_index, obs_frac, obs_value, obs_count):
    row_count = FIELDS * LEV
    plane_size = NX * NY

    def window(operands):
        start_state, drive_field, jacobian, stencil_rates, places, fractions, observed = operands
        field_state = start_state.reshape(row_count, NX, NY)
        for step_index in range(STEPS):
            field_state = model_step(field_state, stencil_rates, jacobian)
        forced = jnp.dot(error_root, drive_field.reshape(row_count, plane_size), precision=lax.Precision.HIGHEST, preferred_element_type=jnp.float32)
        base_cells = start_state.reshape(row_count, plane_size) - forced
        flat_state = field_state.reshape(-1)
        anchor = places[2] * plane_size + places[0] * NY + places[1]
        frac_y = fractions[0]
        upward = fractions[1]
        evolved = (1.0 - upward) * (1.0 - frac_y) * flat_state[anchor]
        evolved = evolved + (1.0 - upward) * frac_y * flat_state[anchor + 1]
        evolved = evolved + upward * (1.0 - frac_y) * flat_state[anchor + plane_size]
        evolved = evolved + upward * frac_y * flat_state[anchor + plane_size + 1]
        return field_state.reshape(row_count, plane_size), base_cells, observed - evolved

    end_states, base_cells, misfit = lax.map(window, (increment, forcing, physics, coefficients, jnp.transpose(obs_index, (1, 0, 2)), jnp.transpose(obs_frac, (1, 0, 2)), obs_value))
    previous = jnp.concatenate([jnp.zeros_like(end_states[:1]), end_states[:-1]], 0)
    residual = base_cells - previous
    summed = jnp.cumsum(residual, axis=0)
    slot_ids = jnp.arange(OBS)
    live_slots = (slot_ids % OBS_DEV)[None, :] < obs_count[:, slot_ids // OBS_DEV]
    departure = jnp.where(live_slots, misfit, jnp.zeros_like(misfit))
    return summed.reshape(increment.shape), departure
```

```python
import jax
import jax.numpy as jnp
from jax import lax
from jax.experimental import pallas as pl
from jax.experimental.pallas import tpu as pltpu
from jax.sharding import Mesh, PartitionSpec as P

STEPS = 6
ROWS = 411
PAD = 416
COLS = 8
LANES = 128
GRID_Y = 4
GRID_X = 4
CORES = 2
PARTS = 16
PART = 104
TILES = 8
SLOTS = 512
CAP = 128
FIELDS = 8

F32 = jnp.float32
BF16 = jnp.bfloat16
HIGHEST = lax.Precision.HIGHEST
MIB = 1 << 20


def call(body, outs, ins, mib, scratch=(), flops=0, moved=0, smem=(), unread=()):
    specs = [
        pl.BlockSpec(memory_space=pltpu.SMEM if at in smem else pl.ANY if at in unread else pltpu.VMEM)
        for at in range(len(ins))
    ]
    many = isinstance(outs, (list, tuple))
    out_specs = [pl.BlockSpec(memory_space=pltpu.VMEM)] * len(outs) if many else pl.BlockSpec(memory_space=pltpu.VMEM)
    return pl.pallas_call(
        body,
        out_shape=outs,
        in_specs=specs,
        out_specs=out_specs,
        scratch_shapes=list(scratch),
        compiler_params=pltpu.CompilerParams(vmem_limit_bytes=mib * MIB),
        cost_estimate=pl.CostEstimate(flops=flops, bytes_accessed=moved, transcendentals=0),
    )(*ins)


def shape(*dims, dtype=F32):
    return jax.ShapeDtypeStruct(dims, dtype)


def two_parts(value):
    high = value.astype(BF16)
    low = (value - high.astype(F32)).astype(BF16)
    return high, low


def product(left_high, left_low, right):
    high, low = two_parts(right)
    total = jnp.dot(left_high, high, preferred_element_type=F32)
    total = total + jnp.dot(left_high, low, preferred_element_type=F32)
    return total + jnp.dot(left_low, high, preferred_element_type=F32)


def pack_kernel(inc_ref, rate_ref, west_ref, east_ref, sent_ref):
    block = pl.program_id(0)
    flat = inc_ref.reshape(PART * COLS, LANES)
    for c in range(COLS):
        column = flat[pl.ds(c, PART, stride=COLS), :]
        if c < STEPS:
            west_ref[c] = column
        if c >= COLS - STEPS:
            east_ref[c - COLS + STEPS] = column

    sent_ref[...] = jnp.zeros((8, LANES), F32)

    @pl.when(block == pl.num_programs(0) - 1)
    def _():
        last = ROWS % PART
        for c in range(COLS):
            rates = jnp.concatenate([rate_ref[i, c : c + 1, :] for i in range(4)] + [jnp.zeros((1, LANES), F32)], 0)
            if c < STEPS:
                west_ref[c, last:, :] = rates
            if c >= COLS - STEPS:
                east_ref[c - COLS + STEPS, last:, :] = rates


def pack(state, rates):
    halo = shape(STEPS, PAD, LANES)
    field = PAD * COLS * LANES * 4
    return pl.pallas_call(
        pack_kernel,
        grid=(PAD // PART,),
        out_shape=[halo, halo, shape(8, LANES)],
        in_specs=[
            pl.BlockSpec((PART, COLS, LANES), lambda i: (i, 0, 0)),
            pl.BlockSpec((4, COLS, LANES), lambda i: (0, 0, 0)),
        ],
        out_specs=[pl.BlockSpec((STEPS, PART, LANES), lambda i: (0, i, 0))] * 2
        + [pl.BlockSpec((8, LANES), lambda i: (0, 0))],
        compiler_params=pltpu.CompilerParams(vmem_limit_bytes=8 * MIB),
        cost_estimate=pl.CostEstimate(flops=0, bytes_accessed=3 * field, transcendentals=0),
    )(state, rates)


def prepare_kernel(inc_ref, forcing_ref, root_ref, physics_ref, base_ref, high_ref, low_ref, square, drive):
    square[...] = jnp.zeros((PAD, PAD), F32)
    square[:ROWS, :ROWS] = root_ref[...]
    root_high, root_low = two_parts(square[...])
    flat = forcing_ref.reshape(ROWS * COLS, LANES)
    start = inc_ref.reshape(ROWS * COLS, LANES)
    drive[ROWS - 3 :, :] = jnp.zeros((PAD - ROWS + 3, 2 * LANES), F32)
    for c in range(0, COLS, 2):
        drive[:ROWS, :LANES] = flat[pl.ds(c, ROWS, stride=COLS), :]
        drive[:ROWS, LANES:] = flat[pl.ds(c + 1, ROWS, stride=COLS), :]
        forced = product(root_high, root_low, drive[...])
        for k in range(2):
            column = forced[:, k * LANES : (k + 1) * LANES]
            base_ref[c + k, :ROWS, :] = start[pl.ds(c + k, ROWS, stride=COLS), :] - column[:ROWS]
            base_ref[c + k, ROWS:, :] = column[ROWS:]
    square[:ROWS, :ROWS] = 0.2 * physics_ref[...]
    once = square[...]
    twice = 2.0 * once + jnp.dot(once, once, precision=HIGHEST, preferred_element_type=F32)
    four = 2.0 * twice + jnp.dot(twice, twice, precision=HIGHEST, preferred_element_type=F32)
    six = twice + four + jnp.dot(twice, four, precision=HIGHEST, preferred_element_type=F32)
    high, low = two_parts(six)
    high_ref[...] = high
    low_ref[...] = low


def transport_kernel(inc_ref, rate_ref, west_ref, east_ref, order_ref, out_ref, table, own, odd, even):
    lane = lax.broadcasted_iota(jnp.int32, (1, LANES), 1)
    wide = COLS + 2 * STEPS
    for j in range(1, wide - 1):
        if j < STEPS:
            rates = [west_ref[j, ROWS + i : ROWS + i + 1, :] for i in range(4)]
        elif j < STEPS + COLS:
            rates = [rate_ref[i, j - STEPS : j - STEPS + 1, :] for i in range(4)]
        else:
            rates = [east_ref[j - STEPS - COLS, ROWS + i : ROWS + i + 1, :] for i in range(4)]
        center = 1.0 - (rates[0] + rates[1] + rates[2] + rates[3])
        north = jnp.where(lane == LANES - 1, 0.0, rates[2])
        south = jnp.where(lane == 0, 0.0, rates[3])
        for i, value in enumerate((center, rates[0], rates[1], north, south)):
            table[5 * j + i] = jnp.broadcast_to(value, (8, LANES))
    flat = inc_ref.reshape(ROWS * COLS, LANES)
    for c in range(COLS):
        own[c, :ROWS, :] = flat[pl.ds(c, ROWS, stride=COLS), :]
        own[c, ROWS:, :] = jnp.zeros((PAD - ROWS, LANES), F32)

    def block(index, carry):
        here = pl.ds(pl.multiple_of(index * PART, 8), PART)

        def load(step, j):
            if step > 0:
                value = (odd if step % 2 else even)[j]
            elif j < STEPS:
                value = west_ref[j, here, :]
            elif j < STEPS + COLS:
                value = own[j - STEPS, here, :]
            else:
                value = east_ref[j - STEPS - COLS, here, :]
            return value.reshape(PART // 8, 8, LANES)

        for step in range(1, STEPS + 1):
            for j in range(step, wide - step):
                v = load(step - 1, j)
                total = table[5 * j] * v
                total = total + table[5 * j + 1] * load(step - 1, j + 1)
                total = total + table[5 * j + 2] * load(step - 1, j - 1)
                total = total + table[5 * j + 3] * pltpu.roll(v, LANES - 1, 2)
                total = total + table[5 * j + 4] * pltpu.roll(v, 1, 2)
                total = total.reshape(PART, LANES)
                if step == STEPS:
                    out_ref[j - STEPS, here, :] = total
                else:
                    (odd if step % 2 else even)[j] = total
        return carry

    lax.fori_loop(0, PAD // PART, block, 0)


def mix_kernel(core_ref, state_ref, high_ref, low_ref, base_ref, order_ref, end_ref, keep_ref, send_ref):
    core = core_ref[0]
    for kind, out_ref in ((1, send_ref), (0, keep_ref)):
        start = 4 * (core ^ kind)
        for i in (0, 2):
            c = start + i
            state = jnp.concatenate([state_ref[c], state_ref[c + 1]], 1)
            end = state + product(high_ref[...], low_ref[...], state)
            for k in range(2):
                column = end[:, k * LANES : (k + 1) * LANES]
                end_ref[c + k] = column
                rest = base_ref[c + k] - column
                for q in range(4):
                    out_ref[4 * (i + k) + q] = rest[q * PART : (q + 1) * PART]


def scan_kernel(in_ref, order_ref, out_ref):
    def block(index, carry):
        here = pl.ds(pl.multiple_of(index * 8, 8), 8)
        total = jnp.zeros((8, LANES), F32)
        for k in range(PARTS):
            out_ref[k, here, :] = total
            total = total + in_ref[k, here, :]
        return carry

    lax.fori_loop(0, PART // 8, block, 0)


def share_kernel(core_ref, before_ref, keep_ref, order_ref, out_ref):
    first = (core_ref[0] == 0).astype(F32)
    out_ref[...] = before_ref[...] + first * keep_ref[...]


def finish_kernel(core_ref, base_ref, before_ref, partner_ref, other_ref, out_ref):
    core = core_ref[0]
    flat = out_ref.reshape(ROWS * COLS, LANES)
    second = (core == 1).astype(F32)
    for c in range(COLS):
        mine = core == c // 4
        i = c % 4
        for q in range(4):
            size = min(PART, ROWS - q * PART)
            own = before_ref[4 * i + q, :size] + second * partner_ref[4 * i + q, :size]
            earlier = jnp.where(mine, own, other_ref[4 * i + q, :size])
            flat[pl.ds(q * PART * COLS + c, size, stride=COLS), :] = (
                base_ref[c, q * PART : q * PART + size, :] + earlier
            )


def slot_places(column_x, me):
    tile = column_x >> 3
    relative = (tile - me + TILES) & (TILES - 1)
    bucket = lax.broadcasted_iota(jnp.int32, (TILES, SLOTS), 0)
    chosen = (bucket == relative).astype(F32)
    earlier = lax.broadcasted_iota(jnp.int32, (SLOTS, SLOTS), 0) < lax.broadcasted_iota(jnp.int32, (SLOTS, SLOTS), 1)
    rank = jnp.dot(chosen.astype(BF16), earlier.astype(F32).astype(BF16), preferred_element_type=F32)
    place = jnp.sum(chosen * rank, axis=0, keepdims=True)
    return chosen, place


def sort_kernel(me_ref, index_ref, frac_ref, sent_ref, out_ref, chosen_ref, spread_ref):
    column_x = index_ref[0:1, :]
    chosen, place = slot_places(column_x, me_ref[0])
    spread = lax.broadcasted_iota(jnp.int32, (CAP, SLOTS), 0) == place.astype(jnp.int32)
    spread = spread.astype(F32)
    chosen_ref[...] = chosen
    spread_ref[...] = spread
    values = jnp.concatenate(
        [
            (column_x & (COLS - 1)).astype(F32),
            index_ref[1:2, :].astype(F32),
            index_ref[2:3, :].astype(F32),
            frac_ref[0:1, :],
            frac_ref[1:2, :],
            jnp.zeros((FIELDS - 5, SLOTS), F32),
        ],
        0,
    )
    for j in range(TILES):
        masked = values * chosen[j : j + 1, :]
        out_ref[j] = lax.dot_general(
            masked, spread, (((1,), (1,)), ((), ())), precision=HIGHEST, preferred_element_type=F32
        )


def observe_kernel(obs_ref, end_ref, order_ref, out_ref, end_high, end_low):
    for c in range(COLS):
        high, low = two_parts(end_ref[c])
        end_high[:, c * LANES : (c + 1) * LANES] = high
        end_low[:, c * LANES : (c + 1) * LANES] = low
    lanes = 2 * CAP
    for j in range(0, TILES, 2):
        fields = [jnp.concatenate([obs_ref[j, i : i + 1], obs_ref[j + 1, i : i + 1]], 1) for i in range(5)]
        column, line, row = [(f + 0.5).astype(jnp.int32) for f in fields[:3]]
        across, upward = fields[3:]
        y = lax.broadcasted_iota(jnp.int32, (LANES, lanes), 0)
        here, after = y == line, y == line + 1
        highs, lows = [], []
        for c in range(COLS):
            mine = column == c
            near = jnp.where(mine, 1.0 - across, 0.0)
            far = jnp.where(mine, across, 0.0)
            weight = jnp.where(here, near, jnp.where(after, far, 0.0))
            high, low = two_parts(weight)
            highs.append(high)
            lows.append(low)
        high, low = jnp.concatenate(highs, 0), jnp.concatenate(lows, 0)
        taken = jnp.dot(end_high[...], high, preferred_element_type=F32)
        taken = taken + jnp.dot(end_high[...], low, preferred_element_type=F32)
        taken = taken + jnp.dot(end_low[...], high, preferred_element_type=F32)
        r = lax.broadcasted_iota(jnp.int32, (PAD, lanes), 0)
        weight = jnp.where(r == row, 1.0 - upward, jnp.where(r == row + 1, upward, 0.0))
        value = jnp.sum(weight * taken, axis=0, keepdims=True)
        out_ref[j : j + 1, :] = value[:, :CAP]
        out_ref[j + 1 : j + 2, :] = value[:, CAP:]


def depart_kernel(count_ref, back_ref, chosen_ref, spread_ref, value_ref, out_ref):
    spread = jnp.dot(back_ref[...], spread_ref[...], precision=HIGHEST, preferred_element_type=F32)
    evolved = jnp.sum(spread * chosen_ref[...], axis=0, keepdims=True)
    live = lax.broadcasted_iota(jnp.int32, (1, SLOTS), 1) < count_ref[0, 0]
    out_ref[...] = jnp.where(live, value_ref[...] - evolved, 0.0)


def hop(blocks, bit, sign):
    moving = [j for j in range(TILES) if j & bit]
    parcel = jnp.concatenate([blocks[j] for j in moving], 0)
    parcel = lax.ppermute(parcel, "tile", [(i, (i + sign * bit) % TILES) for i in range(TILES)])
    size = blocks[0].shape[0]
    result = list(blocks)
    for at, j in enumerate(moving):
        result[j] = parcel[at * size : (at + 1) * size]
    return result


def per_device(
    increment, forcing, error_root, physics, coefficients, obs_index, obs_frac, obs_value, obs_count
):
    state = increment.reshape(ROWS, COLS, LANES)
    drive = forcing.reshape(ROWS, COLS, LANES)
    rates = coefficients.reshape(4, COLS, LANES)
    core = jnp.reshape(lax.axis_index("core"), (1,)).astype(jnp.int32)
    me = jnp.reshape(lax.axis_index("tile"), (1,)).astype(jnp.int32)
    field = PAD * COLS * LANES * 4

    west, east, sent = pack(state, rates)
    from_east = lax.ppermute(west, "tile", [(i + 1, i) for i in range(TILES - 1)])
    from_west = lax.ppermute(east, "tile", [(i, i + 1) for i in range(TILES - 1)])

    places = obs_index.reshape(3, SLOTS)
    sorted_obs, chosen, spread = call(
        sort_kernel,
        [shape(TILES, FIELDS, CAP), shape(TILES, SLOTS), shape(CAP, SLOTS)],
        (me, places, obs_frac.reshape(2, SLOTS), sent),
        16,
        flops=10**8,
        moved=10**6,
        smem=(0,),
    )
    blocks = hop([sorted_obs[j] for j in range(TILES)], 4, 1)

    base, high, low = call(
        prepare_kernel,
        [shape(COLS, PAD, LANES), shape(PAD, PAD, dtype=BF16), shape(PAD, PAD, dtype=BF16)],
        (state, drive, error_root, physics.reshape(ROWS, ROWS)),
        16,
        scratch=[pltpu.VMEM((PAD, PAD), F32), pltpu.VMEM((PAD, 2 * LANES), F32)],
        flops=8 * 10**9,
        moved=5 * field,
    )

    wide = COLS + 2 * STEPS
    moved = call(
        transport_kernel,
        shape(COLS, PAD, LANES),
        (state, rates, from_west, from_east, blocks[7]),
        16,
        scratch=[
            pltpu.VMEM((5 * wide, 8, LANES), F32),
            pltpu.VMEM((COLS, PAD, LANES), F32),
            pltpu.VMEM((wide, PART, LANES), F32),
            pltpu.VMEM((wide, PART, LANES), F32),
        ],
        flops=4 * 10**9,
        moved=5 * field,
    )
    blocks = hop(blocks, 2, 1)
    parts = shape(PARTS, PART, LANES)
    end, keep, send = call(
        mix_kernel,
        [shape(COLS, PAD, LANES), parts, parts],
        (core, moved, high, low, base, blocks[7]),
        16,
        flops=2 * 10**9,
        moved=5 * field,
        smem=(0,),
    )
    swap = [(0, 1), (1, 0)]
    partner = lax.ppermute(send, "core", swap)
    blocks = hop(blocks, 1, 1)
    pair = keep + partner
    gathered = lax.all_to_all(pair, ("y", "x"), 0, 0, tiled=True)
    found = call(
        observe_kernel,
        shape(TILES, CAP),
        (jnp.stack(blocks, 0), end, pair),
        16,
        scratch=[pltpu.VMEM((PAD, COLS * LANES), BF16), pltpu.VMEM((PAD, COLS * LANES), BF16)],
        flops=3 * 10**9,
        moved=field,
        unread=(2,),
    )
    back = hop([found[j : j + 1] for j in range(TILES)], 4, -1)
    totals = call(scan_kernel, parts, (gathered, found), 8, flops=10**7, moved=field)
    before = lax.all_to_all(totals, ("y", "x"), 0, 0, tiled=True)
    back = hop(hop(back, 2, -1), 1, -1)
    departure = call(
        depart_kernel,
        shape(1, SLOTS),
        (obs_count, jnp.concatenate(back, 0), chosen, spread, obs_value),
        8,
        flops=10**7,
        moved=10**6,
        smem=(0,),
    )
    for_partner = call(
        share_kernel, parts, (core, before, keep, departure), 8, flops=10**7, moved=2 * field, smem=(0,)
    )
    other = lax.ppermute(for_partner, "core", swap)
    summed = call(
        finish_kernel,
        shape(ROWS, COLS, LANES),
        (core, base, before, partner, other),
        16,
        flops=10**7,
        moved=4 * field,
        smem=(0,),
    )
    return summed.reshape(increment.shape), departure


def solution(mesh):
    split = Mesh(mesh.devices.reshape(GRID_Y, GRID_X, CORES, TILES), ("y", "x", "core", "tile"))
    win = ("y", "x", "core")
    return jax.shard_map(
        per_device,
        mesh=split,
        in_specs=(
            P(win, None, None, "tile", None),
            P(win, None, None, "tile", None),
            P(),
            P(win, None, None),
            P(win, None, "tile", None),
            P(None, win, "tile"),
            P(None, win, "tile"),
            P(win, "tile"),
            P(win, "tile"),
        ),
        out_specs=(P(win, None, None, "tile", None), P(win, "tile")),
        check_vma=False,
    )
```

```python
import jax
import jax.numpy as jnp
from jax import lax
from jax.experimental import pallas as pl
from jax.experimental.pallas import tpu as pltpu
from jax.sharding import Mesh, PartitionSpec as P

STEPS = 6
ROWS = 411
PAD = 416
COLS = 8
LANES = 128
GRID_Y = 4
GRID_X = 4
CORES = 2
PARTS = 16
PART = 104
TILES = 8
CHUNKS = ((0, 208), (208, 104), (312, 104))
SLOTS = 512
CAP = 128
FIELDS = 8

F32 = jnp.float32
BF16 = jnp.bfloat16
HIGHEST = lax.Precision.HIGHEST
MIB = 1 << 20


def call(body, outs, ins, mib, scratch=(), flops=0, moved=0, smem=(), far=(), far_out=False):
    specs = [
        pl.BlockSpec(memory_space=pltpu.SMEM if at in smem else pl.ANY if at in far else pltpu.VMEM)
        for at in range(len(ins))
    ]
    out_spec = pl.BlockSpec(memory_space=pl.ANY if far_out else pltpu.VMEM)
    return pl.pallas_call(
        body,
        out_shape=outs,
        in_specs=specs,
        out_specs=[out_spec] * len(outs) if isinstance(outs, (list, tuple)) else out_spec,
        scratch_shapes=list(scratch),
        compiler_params=pltpu.CompilerParams(vmem_limit_bytes=mib * MIB),
        cost_estimate=pl.CostEstimate(flops=flops, bytes_accessed=moved, transcendentals=0),
    )(*ins)


def shape(*dims, dtype=F32):
    return jax.ShapeDtypeStruct(dims, dtype)


def two_parts(value):
    high = value.astype(BF16)
    low = (value - high.astype(F32)).astype(BF16)
    return high, low


def product(left_high, left_low, right):
    high, low = two_parts(right)
    total = jnp.dot(left_high, high, preferred_element_type=F32)
    total = total + jnp.dot(left_high, low, preferred_element_type=F32)
    return total + jnp.dot(left_low, high, preferred_element_type=F32)


def pack_kernel(inc_ref, rate_ref, *refs):
    count = len(CHUNKS)
    wests, easts = refs[:count], refs[count : 2 * count]
    held, rates = refs[2 * count : 2 * count + 2]
    west_bufs = refs[2 * count + 2 : 3 * count + 2]
    east_bufs = refs[3 * count + 2 : 4 * count + 2]
    in_sems, out_sems = refs[4 * count + 2 :]
    incoming = []
    for at, (start, size) in enumerate(CHUNKS):
        size = min(size, ROWS - start)
        rows = pl.ds(start, size)
        incoming.append(pltpu.make_async_copy(inc_ref.at[rows], held.at[rows], in_sems.at[at]))
    incoming.append(pltpu.make_async_copy(rate_ref, rates, in_sems.at[count]))
    for copy in incoming:
        copy.start()
    held[ROWS:] = jnp.zeros((PAD - ROWS, COLS, LANES), F32)
    flat = held.reshape(PAD * COLS, LANES)
    outgoing = []
    incoming[count].wait()
    for at, (start, size) in enumerate(CHUNKS):
        incoming[at].wait()
        for c in range(COLS):
            column = flat[pl.ds(start * COLS + c, size, stride=COLS), :]
            if at == 0:
                weights = [rates[i, c : c + 1, :] for i in range(4)]
                column = jnp.concatenate([column] + weights + [jnp.zeros((4, LANES), F32)], 0)
            if c < STEPS:
                west_bufs[at][c] = column
            if c >= COLS - STEPS:
                east_bufs[at][c - COLS + STEPS] = column
        outgoing.append(pltpu.make_async_copy(west_bufs[at], wests[at], out_sems.at[2 * at]))
        outgoing.append(pltpu.make_async_copy(east_bufs[at], easts[at], out_sems.at[2 * at + 1]))
        outgoing[-2].start()
        outgoing[-1].start()
    for copy in outgoing:
        copy.wait()


def pack(state, rates):
    dims = [(STEPS, size + (8 if at == 0 else 0), LANES) for at, (_, size) in enumerate(CHUNKS)]
    count = len(CHUNKS)
    outs = call(
        pack_kernel,
        [shape(*d) for d in dims] * 2,
        (state, rates),
        8,
        scratch=[pltpu.VMEM((PAD, COLS, LANES), F32), pltpu.VMEM((4, COLS, LANES), F32)]
        + [pltpu.VMEM(d, F32) for d in dims] * 2
        + [pltpu.SemaphoreType.DMA((count + 1,)), pltpu.SemaphoreType.DMA((2 * count,))],
        moved=3 * PAD * COLS * LANES * 4,
        far=(0, 1),
        far_out=True,
    )
    return outs[:count], outs[count:]


def prepare_kernel(inc_ref, forcing_ref, root_ref, physics_ref, base_ref, high_ref, low_ref, square, drive):
    square[...] = jnp.zeros((PAD, PAD), F32)
    square[:ROWS, :ROWS] = root_ref[...]
    root_high, root_low = two_parts(square[...])
    flat = forcing_ref.reshape(ROWS * COLS, LANES)
    start = inc_ref.reshape(ROWS * COLS, LANES)
    drive[ROWS - 3 :, :] = jnp.zeros((PAD - ROWS + 3, 2 * LANES), F32)
    for c in range(0, COLS, 2):
        drive[:ROWS, :LANES] = flat[pl.ds(c, ROWS, stride=COLS), :]
        drive[:ROWS, LANES:] = flat[pl.ds(c + 1, ROWS, stride=COLS), :]
        forced = product(root_high, root_low, drive[...])
        for k in range(2):
            column = forced[:, k * LANES : (k + 1) * LANES]
            base_ref[c + k, :ROWS, :] = start[pl.ds(c + k, ROWS, stride=COLS), :] - column[:ROWS]
            base_ref[c + k, ROWS:, :] = column[ROWS:]
    square[:ROWS, :ROWS] = 0.2 * physics_ref[...]
    once = square[...]
    twice = 2.0 * once + jnp.dot(once, once, precision=HIGHEST, preferred_element_type=F32)
    four = 2.0 * twice + jnp.dot(twice, twice, precision=HIGHEST, preferred_element_type=F32)
    six = twice + four + jnp.dot(twice, four, precision=HIGHEST, preferred_element_type=F32)
    high, low = two_parts(six)
    high_ref[...] = high
    low_ref[...] = low


def transport_kernel(
    start, size, inc_ref, rate_ref, west_ref, east_ref, west_rate_ref, east_rate_ref, order_ref, out_ref, passed_ref,
    table, own, odd, even, sem
):
    valid = min(size, ROWS - start)
    copy = pltpu.make_async_copy(inc_ref.at[pl.ds(start, valid)], own.at[pl.ds(0, valid)], sem)
    copy.start()
    passed_ref[...] = order_ref[...]
    lane = lax.broadcasted_iota(jnp.int32, (1, LANES), 1)
    wide = COLS + 2 * STEPS
    at = CHUNKS[0][1]
    for j in range(1, wide - 1):
        if j < STEPS:
            rates = [west_rate_ref[j, at + i : at + i + 1, :] for i in range(4)]
        elif j < STEPS + COLS:
            rates = [rate_ref[i, j - STEPS : j - STEPS + 1, :] for i in range(4)]
        else:
            rates = [east_rate_ref[j - STEPS - COLS, at + i : at + i + 1, :] for i in range(4)]
        center = 1.0 - (rates[0] + rates[1] + rates[2] + rates[3])
        north = jnp.where(lane == LANES - 1, 0.0, rates[2])
        south = jnp.where(lane == 0, 0.0, rates[3])
        for i, value in enumerate((center, rates[0], rates[1], north, south)):
            table[5 * j + i] = jnp.broadcast_to(value, (8, LANES))
    if valid < size:
        own[valid:] = jnp.zeros((size - valid, COLS, LANES), F32)
    flat = own.reshape(size * COLS, LANES)
    copy.wait()

    def block(index, carry):
        here = pl.ds(pl.multiple_of(index * PART, 8), PART)

        def load(step, j):
            if step > 0:
                value = (odd if step % 2 else even)[j]
            elif j < STEPS:
                value = west_ref[j, here, :]
            elif j < STEPS + COLS:
                value = flat[pl.ds(index * (PART * COLS) + j - STEPS, PART, stride=COLS), :]
            else:
                value = east_ref[j - STEPS - COLS, here, :]
            return value.reshape(PART // 8, 8, LANES)

        for step in range(1, STEPS + 1):
            for j in range(step, wide - step):
                v = load(step - 1, j)
                total = table[5 * j] * v
                total = total + table[5 * j + 1] * load(step - 1, j + 1)
                total = total + table[5 * j + 2] * load(step - 1, j - 1)
                total = total + table[5 * j + 3] * pltpu.roll(v, LANES - 1, 2)
                total = total + table[5 * j + 4] * pltpu.roll(v, 1, 2)
                total = total.reshape(PART, LANES)
                if step == STEPS:
                    out_ref[j - STEPS, here, :] = total
                else:
                    (odd if step % 2 else even)[j] = total
        return carry

    if size == PART:
        block(0, 0)
    else:
        lax.fori_loop(0, size // PART, block, 0)


def mix_kernel(core_ref, upper_ref, middle_ref, lower_ref, high_ref, low_ref, base_ref, order_ref, end_ref, keep_ref, send_ref):
    core = core_ref[0]
    for kind, out_ref in ((1, send_ref), (0, keep_ref)):
        start = 4 * (core ^ kind)
        for i in (0, 2):
            c = start + i
            state = jnp.concatenate(
                [
                    jnp.concatenate([ref[c + k] for ref in (upper_ref, middle_ref, lower_ref)], 0)
                    for k in range(2)
                ],
                1,
            )
            end = state + product(high_ref[...], low_ref[...], state)
            for k in range(2):
                column = end[:, k * LANES : (k + 1) * LANES]
                end_ref[c + k] = column
                rest = base_ref[c + k] - column
                for q in range(4):
                    out_ref[4 * (i + k) + q] = rest[q * PART : (q + 1) * PART]


def scan_kernel(in_ref, order_ref, out_ref):
    def block(index, carry):
        here = pl.ds(pl.multiple_of(index * 8, 8), 8)
        total = jnp.zeros((8, LANES), F32)
        for k in range(PARTS):
            out_ref[k, here, :] = total
            total = total + in_ref[k, here, :]
        return carry

    lax.fori_loop(0, PART // 8, block, 0)


def share_kernel(core_ref, before_ref, keep_ref, order_ref, out_ref):
    first = (core_ref[0] == 0).astype(F32)
    out_ref[...] = before_ref[...] + first * keep_ref[...]


def finish_kernel(core_ref, base_ref, before_ref, partner_ref, other_ref, out_ref):
    core = core_ref[0]
    flat = out_ref.reshape(ROWS * COLS, LANES)
    second = (core == 1).astype(F32)
    for c in range(COLS):
        mine = core == c // 4
        i = c % 4
        for q in range(4):
            size = min(PART, ROWS - q * PART)
            own = before_ref[4 * i + q, :size] + second * partner_ref[4 * i + q, :size]
            earlier = jnp.where(mine, own, other_ref[4 * i + q, :size])
            flat[pl.ds(q * PART * COLS + c, size, stride=COLS), :] = (
                base_ref[c, q * PART : q * PART + size, :] + earlier
            )


def sort_kernel(index_ref, frac_ref, order_ref, out_ref, chosen_ref, spread_ref):
    column_x = index_ref[0]
    bucket = lax.broadcasted_iota(jnp.int32, (TILES, SLOTS), 0)
    chosen = (bucket == (column_x >> 3)).astype(F32)
    before = lax.broadcasted_iota(jnp.int32, (SLOTS, SLOTS), 0) < lax.broadcasted_iota(jnp.int32, (SLOTS, SLOTS), 1)
    rank = jnp.dot(chosen.astype(BF16), before.astype(F32).astype(BF16), preferred_element_type=F32)
    place = jnp.sum(chosen * rank, axis=0, keepdims=True)
    spread = lax.broadcasted_iota(jnp.int32, (CAP, SLOTS), 0) == place.astype(jnp.int32)
    spread = spread.astype(F32)
    chosen_ref[...] = chosen
    spread_ref[...] = spread
    values = jnp.concatenate(
        [
            (column_x & (COLS - 1)).astype(F32),
            index_ref[1].astype(F32),
            index_ref[2].astype(F32),
            frac_ref[0],
            frac_ref[1],
            jnp.zeros((FIELDS - 5, SLOTS), F32),
        ],
        0,
    )
    for j in range(TILES):
        masked = values * chosen[j : j + 1, :]
        out_ref[j] = lax.dot_general(
            masked, spread, (((1,), (1,)), ((), ())), precision=HIGHEST, preferred_element_type=F32
        )


def observe_kernel(obs_ref, end_ref, order_ref, out_ref, end_high, end_low):
    for c in range(COLS):
        high, low = two_parts(end_ref[c])
        end_high[:, c * LANES : (c + 1) * LANES] = high
        end_low[:, c * LANES : (c + 1) * LANES] = low
    lanes = 2 * CAP
    for j in range(0, TILES, 2):
        fields = [jnp.concatenate([obs_ref[j, i : i + 1], obs_ref[j + 1, i : i + 1]], 1) for i in range(5)]
        column, line, row = [(f + 0.5).astype(jnp.int32) for f in fields[:3]]
        across, upward = fields[3:]
        y = lax.broadcasted_iota(jnp.int32, (LANES, lanes), 0)
        here, after = y == line, y == line + 1
        highs, lows = [], []
        for c in range(COLS):
            mine = column == c
            near = jnp.where(mine, 1.0 - across, 0.0)
            far = jnp.where(mine, across, 0.0)
            weight = jnp.where(here, near, jnp.where(after, far, 0.0))
            high, low = two_parts(weight)
            highs.append(high)
            lows.append(low)
        high, low = jnp.concatenate(highs, 0), jnp.concatenate(lows, 0)
        taken = jnp.dot(end_high[...], high, preferred_element_type=F32)
        taken = taken + jnp.dot(end_high[...], low, preferred_element_type=F32)
        taken = taken + jnp.dot(end_low[...], high, preferred_element_type=F32)
        r = lax.broadcasted_iota(jnp.int32, (PAD, lanes), 0)
        weight = jnp.where(r == row, 1.0 - upward, jnp.where(r == row + 1, upward, 0.0))
        value = jnp.sum(weight * taken, axis=0, keepdims=True)
        out_ref[j] = jnp.broadcast_to(value[:, :CAP], (8, CAP))
        out_ref[j + 1] = jnp.broadcast_to(value[:, CAP:], (8, CAP))


def depart_kernel(count_ref, back_ref, chosen_ref, spread_ref, value_ref, out_ref):
    back = jnp.concatenate([back_ref[j, 0:1, :] for j in range(TILES)], 0)
    spread = jnp.dot(back, spread_ref[...], precision=HIGHEST, preferred_element_type=F32)
    evolved = jnp.sum(spread * chosen_ref[...], axis=0, keepdims=True)
    live = lax.broadcasted_iota(jnp.int32, (1, SLOTS), 1) < count_ref[0, 0]
    out_ref[...] = jnp.where(live, value_ref[...] - evolved, 0.0)


def per_device(
    increment, forcing, error_root, physics, coefficients, obs_index, obs_frac, obs_value, obs_count
):
    state = increment.reshape(ROWS, COLS, LANES)
    drive = forcing.reshape(ROWS, COLS, LANES)
    rates = coefficients.reshape(4, COLS, LANES)
    core = jnp.reshape(lax.axis_index("core"), (1,)).astype(jnp.int32)
    field = PAD * COLS * LANES * 4

    wests, easts = pack(state, rates)
    to_west = [(i + 1, i) for i in range(TILES - 1)]
    to_east = [(i, i + 1) for i in range(TILES - 1)]
    halos = [
        (lax.ppermute(east, "tile", to_east), lax.ppermute(west, "tile", to_west))
        for west, east in zip(wests, easts)
    ]

    base, high, low = call(
        prepare_kernel,
        [shape(COLS, PAD, LANES), shape(PAD, PAD, dtype=BF16), shape(PAD, PAD, dtype=BF16)],
        (state, drive, error_root, physics.reshape(ROWS, ROWS)),
        16,
        scratch=[pltpu.VMEM((PAD, PAD), F32), pltpu.VMEM((PAD, 2 * LANES), F32)],
        flops=8 * 10**9,
        moved=5 * field,
    )
    queries, chosen, spread = call(
        sort_kernel,
        [shape(TILES, FIELDS, CAP), shape(TILES, SLOTS), shape(CAP, SLOTS)],
        (obs_index, obs_frac, halos[0][0]),
        8,
        flops=10**8,
        moved=10**6,
        far=(2,),
    )

    wide = COLS + 2 * STEPS
    moved = []
    for at, (start, size) in enumerate(CHUNKS):
        out, handed = call(
            lambda *refs, start=start, size=size: transport_kernel(start, size, *refs),
            [shape(COLS, size, LANES), shape(TILES, FIELDS, CAP)],
            (state, rates, *halos[at], *halos[0], queries),
            10,
            scratch=[
                pltpu.VMEM((5 * wide, 8, LANES), F32),
                pltpu.VMEM((size, COLS, LANES), F32),
                pltpu.VMEM((wide, PART, LANES), F32),
                pltpu.VMEM((wide, PART, LANES), F32),
                pltpu.SemaphoreType.DMA,
            ],
            flops=2 * 10**7 * size,
            moved=3 * field * size // PAD,
            far=(0,),
        )
        moved.append(out)
        if at == len(CHUNKS) - 2:
            arrived = lax.all_to_all(handed, "tile", 0, 0, tiled=True)
    parts = shape(PARTS, PART, LANES)
    end, keep, send = call(
        mix_kernel,
        [shape(COLS, PAD, LANES), parts, parts],
        (core, *moved, high, low, base, arrived),
        14,
        flops=2 * 10**9,
        moved=5 * field,
        smem=(0,),
    )
    swap = [(0, 1), (1, 0)]
    partner = lax.ppermute(send, "core", swap)
    pair = keep + partner
    gathered = lax.all_to_all(pair, ("y", "x"), 0, 0, tiled=True)
    found = call(
        observe_kernel,
        shape(TILES, 8, CAP),
        (arrived, end, pair),
        16,
        scratch=[pltpu.VMEM((PAD, COLS * LANES), BF16), pltpu.VMEM((PAD, COLS * LANES), BF16)],
        flops=3 * 10**9,
        moved=field,
        far=(2,),
    )
    back = lax.all_to_all(found, "tile", 0, 0, tiled=True)
    totals = call(scan_kernel, parts, (gathered, found), 8, flops=10**7, moved=field)
    before = lax.all_to_all(totals, ("y", "x"), 0, 0, tiled=True)
    departure = call(
        depart_kernel,
        shape(1, SLOTS),
        (obs_count, back, chosen, spread, obs_value),
        8,
        flops=10**7,
        moved=10**6,
        smem=(0,),
    )
    for_partner = call(
        share_kernel, parts, (core, before, keep, departure), 8, flops=10**7, moved=2 * field, smem=(0,)
    )
    other = lax.ppermute(for_partner, "core", swap)
    summed = call(
        finish_kernel,
        shape(ROWS, COLS, LANES),
        (core, base, before, partner, other),
        16,
        flops=10**7,
        moved=4 * field,
        smem=(0,),
    )
    return summed.reshape(increment.shape), departure


def solution(mesh):
    split = Mesh(mesh.devices.reshape(GRID_Y, GRID_X, CORES, TILES), ("y", "x", "core", "tile"))
    win = ("y", "x", "core")
    return jax.shard_map(
        per_device,
        mesh=split,
        in_specs=(
            P(win, None, None, "tile", None),
            P(win, None, None, "tile", None),
            P(),
            P(win, None, None),
            P(win, None, "tile", None),
            P(None, win, "tile"),
            P(None, win, "tile"),
            P(win, "tile"),
            P(win, "tile"),
        ),
        out_specs=(P(win, None, None, "tile", None), P(win, "tile")),
        check_vma=False,
    )
```

```python
import jax
import jax.numpy as jnp
from jax import lax
from jax.experimental import pallas as pl
from jax.experimental.pallas import tpu as pltpu
from jax.sharding import Mesh, PartitionSpec as P

STEPS = 6
ROWS = 411
PAD = 416
COLS = 8
LANES = 128
GRID_Y = 4
GRID_X = 4
CORES = 2
PARTS = 16
PART = 104
TILES = 8
CHUNKS = ((0, 208), (208, 208))
SLOTS = 512
CAP = 128
FIELDS = 8

F32 = jnp.float32
BF16 = jnp.bfloat16
HIGHEST = lax.Precision.HIGHEST
MIB = 1 << 20
WIDE = 56


def call(body, outs, ins, mib, scratch=(), flops=0, moved=0, smem=(), far=(), far_out=()):
    specs = [
        pl.BlockSpec(memory_space=pltpu.SMEM if at in smem else pltpu.HBM if at in far else pltpu.VMEM)
        for at in range(len(ins))
    ]
    many = isinstance(outs, (list, tuple))
    out_specs = [
        pl.BlockSpec(memory_space=pltpu.HBM if at in far_out else pltpu.VMEM)
        for at in range(len(outs) if many else 1)
    ]
    return pl.pallas_call(
        body,
        out_shape=outs,
        in_specs=specs,
        out_specs=out_specs if many else out_specs[0],
        scratch_shapes=list(scratch),
        compiler_params=pltpu.CompilerParams(vmem_limit_bytes=mib * MIB),
        cost_estimate=pl.CostEstimate(flops=flops, bytes_accessed=moved, transcendentals=0),
    )(*ins)


def shape(*dims, dtype=F32):
    return jax.ShapeDtypeStruct(dims, dtype)


def two_parts(value):
    high = value.astype(BF16)
    low = (value - high.astype(F32)).astype(BF16)
    return high, low


def product(left_high, left_low, right):
    high, low = two_parts(right)
    total = jnp.dot(left_high, high, preferred_element_type=F32)
    total = total + jnp.dot(left_high, low, preferred_element_type=F32)
    return total + jnp.dot(left_low, high, preferred_element_type=F32)


def pack_kernel(inc_ref, rate_ref, *refs):
    count = len(CHUNKS)
    wests, easts = refs[:count], refs[count : 2 * count]
    held, rates = refs[2 * count : 2 * count + 2]
    west_bufs = refs[2 * count + 2 : 3 * count + 2]
    east_bufs = refs[3 * count + 2 : 4 * count + 2]
    in_sems, out_sems = refs[4 * count + 2 :]
    incoming = [pltpu.make_async_copy(rate_ref, rates, in_sems.at[count])]
    for at, (start, size) in enumerate(CHUNKS):
        rows = pl.ds(start, min(size, ROWS - start))
        incoming.append(pltpu.make_async_copy(inc_ref.at[rows], held.at[rows], in_sems.at[at]))
    for copy in incoming:
        copy.start()
    held[ROWS:] = jnp.zeros((PAD - ROWS, COLS, LANES), F32)
    flat = held.reshape(PAD * COLS, LANES)
    outgoing = []
    incoming[0].wait()
    for at, (start, size) in enumerate(CHUNKS):
        incoming[at + 1].wait()
        for c in range(COLS):
            column = flat[pl.ds(start * COLS + c, size, stride=COLS), :]
            if at == 0:
                weights = [rates[i, c : c + 1, :] for i in range(4)]
                column = jnp.concatenate([column] + weights + [jnp.zeros((4, LANES), F32)], 0)
            if c < STEPS:
                west_bufs[at][c] = column
            if c >= COLS - STEPS:
                east_bufs[at][c - COLS + STEPS] = column
        outgoing.append(pltpu.make_async_copy(west_bufs[at], wests[at], out_sems.at[2 * at]))
        outgoing.append(pltpu.make_async_copy(east_bufs[at], easts[at], out_sems.at[2 * at + 1]))
        outgoing[-2].start()
        outgoing[-1].start()
    for copy in outgoing:
        copy.wait()


def pack(state, rates):
    dims = [(STEPS, size + (8 if at == 0 else 0), LANES) for at, (_, size) in enumerate(CHUNKS)]
    count = len(CHUNKS)
    outs = call(
        pack_kernel,
        [shape(*d) for d in dims] * 2,
        (state, rates),
        WIDE,
        scratch=[pltpu.VMEM((PAD, COLS, LANES), F32), pltpu.VMEM((4, COLS, LANES), F32)]
        + [pltpu.VMEM(d, F32) for d in dims] * 2
        + [pltpu.SemaphoreType.DMA((count + 1,)), pltpu.SemaphoreType.DMA((2 * count,))],
        moved=3 * PAD * COLS * LANES * 4,
        far=(0, 1),
        far_out=range(2 * count),
    )
    return outs[:count], outs[count:]


def prepare_kernel(
    inc_ref, forcing_ref, root_ref, physics_ref, base_ref, high_ref, low_ref,
    start, force, root, square, drive, base, high, low, sems
):
    incoming = [
        pltpu.make_async_copy(root_ref, root, sems.at[0]),
        pltpu.make_async_copy(forcing_ref, force, sems.at[1]),
        pltpu.make_async_copy(inc_ref, start, sems.at[2]),
    ]
    for copy in incoming:
        copy.start()
    square[...] = jnp.zeros((PAD, PAD), F32)
    square[:ROWS, :ROWS] = 0.2 * physics_ref[...]
    once = square[...]
    twice = 2.0 * once + product(*two_parts(once), once)
    twice_parts = two_parts(twice)
    four = 2.0 * twice + product(*twice_parts, twice)
    six = twice + four + product(*twice_parts, four)
    high[...], low[...] = two_parts(six)
    outgoing = [
        pltpu.make_async_copy(high, high_ref, sems.at[3]),
        pltpu.make_async_copy(low, low_ref, sems.at[4]),
    ]
    for copy in outgoing:
        copy.start()
    for copy in incoming:
        copy.wait()
    square[:ROWS, :ROWS] = root[...]
    root_high, root_low = two_parts(square[...])
    force_flat = force.reshape(ROWS * COLS, LANES)
    start_flat = start.reshape(ROWS * COLS, LANES)
    drive[ROWS - 3 :, :] = jnp.zeros((PAD - ROWS + 3, 2 * LANES), F32)
    for c in range(0, COLS, 2):
        drive[:ROWS, :LANES] = force_flat[pl.ds(c, ROWS, stride=COLS), :]
        drive[:ROWS, LANES:] = force_flat[pl.ds(c + 1, ROWS, stride=COLS), :]
        forced = product(root_high, root_low, drive[...])
        for k in range(2):
            column = forced[:, k * LANES : (k + 1) * LANES]
            base[c + k, :ROWS, :] = start_flat[pl.ds(c + k, ROWS, stride=COLS), :] - column[:ROWS]
            base[c + k, ROWS:, :] = column[ROWS:]
        pair = pl.ds(c, 2)
        outgoing.append(pltpu.make_async_copy(base.at[pair], base_ref.at[pair], sems.at[5 + c // 2]))
        outgoing[-1].start()
    for copy in outgoing:
        copy.wait()


def transport(at, refs, scratch, put, later=()):
    inc_ref, rate_ref, west_ref, east_ref, west_rate_ref, east_rate_ref = refs
    rate, west_rate, east_rate, table, own, west, east, odd, even, sems = scratch
    start, size = CHUNKS[at]
    blocks = size // PART
    first = CHUNKS[0][1]
    weights = [
        pltpu.make_async_copy(rate_ref, rate, sems.at[0]),
        pltpu.make_async_copy(west_rate_ref.at[:, pl.ds(first, 8)], west_rate, sems.at[1]),
        pltpu.make_async_copy(east_rate_ref.at[:, pl.ds(first, 8)], east_rate, sems.at[2]),
    ]
    fields = []
    for b in range(blocks):
        valid = min(PART, ROWS - start - b * PART)
        rows = pl.ds(b * PART, PART)
        fields.append(
            [
                pltpu.make_async_copy(
                    inc_ref.at[pl.ds(start + b * PART, valid)], own.at[b, pl.ds(0, valid)], sems.at[3 + 3 * b]
                ),
                pltpu.make_async_copy(west_ref.at[:, rows], west.at[b], sems.at[4 + 3 * b]),
                pltpu.make_async_copy(east_ref.at[:, rows], east.at[b], sems.at[5 + 3 * b]),
            ]
        )
    for copy in weights + [c for group in fields for c in group] + list(later):
        copy.start()
    for copy in weights:
        copy.wait()
    lane = lax.broadcasted_iota(jnp.int32, (1, LANES), 1)
    wide = COLS + 2 * STEPS
    for j in range(1, wide - 1):
        if j < STEPS:
            rates = [west_rate[j, i : i + 1, :] for i in range(4)]
        elif j < STEPS + COLS:
            rates = [rate[i, j - STEPS : j - STEPS + 1, :] for i in range(4)]
        else:
            rates = [east_rate[j - STEPS - COLS, i : i + 1, :] for i in range(4)]
        center = 1.0 - (rates[0] + rates[1] + rates[2] + rates[3])
        north = jnp.where(lane == LANES - 1, 0.0, rates[2])
        south = jnp.where(lane == 0, 0.0, rates[3])
        for i, value in enumerate((center, rates[0], rates[1], north, south)):
            table[5 * j + i] = jnp.broadcast_to(value, (8, LANES))
    flat = own.reshape(blocks * PART * COLS, LANES)
    for b in range(blocks):
        valid = min(PART, ROWS - start - b * PART)
        if valid < PART:
            own[b, valid:] = jnp.zeros((PART - valid, COLS, LANES), F32)
        for copy in fields[b]:
            copy.wait()

    def block(b, carry):
        def load(step, j):
            if step > 0:
                value = (odd if step % 2 else even)[j]
            elif j < STEPS:
                value = west[b, j]
            elif j < STEPS + COLS:
                value = flat[pl.ds(b * (PART * COLS) + j - STEPS, PART, stride=COLS), :]
            else:
                value = east[b, j - STEPS - COLS]
            return value.reshape(PART // 8, 8, LANES)

        for step in range(1, STEPS + 1):
            for j in range(step, wide - step):
                v = load(step - 1, j)
                total = table[5 * j] * v
                total = total + table[5 * j + 1] * load(step - 1, j + 1)
                total = total + table[5 * j + 2] * load(step - 1, j - 1)
                total = total + table[5 * j + 3] * pltpu.roll(v, LANES - 1, 2)
                total = total + table[5 * j + 4] * pltpu.roll(v, 1, 2)
                total = total.reshape(PART, LANES)
                if step == STEPS:
                    put(pl.ds(pl.multiple_of(b * PART, 8), PART), j - STEPS, total)
                else:
                    (odd if step % 2 else even)[j] = total
        return carry

    lax.fori_loop(0, blocks, block, 0)


def transport_scratch(at):
    blocks = CHUNKS[at][1] // PART
    wide = COLS + 2 * STEPS
    return [
        pltpu.VMEM((4, COLS, LANES), F32),
        pltpu.VMEM((STEPS, 8, LANES), F32),
        pltpu.VMEM((STEPS, 8, LANES), F32),
        pltpu.VMEM((5 * wide, 8, LANES), F32),
        pltpu.VMEM((blocks, PART, COLS, LANES), F32),
        pltpu.VMEM((blocks, STEPS, PART, LANES), F32),
        pltpu.VMEM((blocks, STEPS, PART, LANES), F32),
        pltpu.VMEM((wide, PART, LANES), F32),
        pltpu.VMEM((wide, PART, LANES), F32),
        pltpu.SemaphoreType.DMA((3 + 3 * blocks,)),
    ]


def upper_kernel(*refs):
    ins, out_ref, (out, sem), scratch = refs[:6], refs[6], refs[7:9], refs[9:]

    def put(rows, c, value):
        out[c, rows, :] = value

    transport(0, ins, scratch, put)
    copy = pltpu.make_async_copy(out, out_ref, sem)
    copy.start()
    copy.wait()


def lower_kernel(*refs):
    ins, (core_ref, upper_ref, high_ref, low_ref, base_ref) = refs[:6], refs[6:11]
    end_ref, keep_ref, send_ref, upper, lower, base, high, low, parts, sems = refs[12:22]
    incoming = [
        pltpu.make_async_copy(high_ref, high, sems.at[1]),
        pltpu.make_async_copy(low_ref, low, sems.at[2]),
        pltpu.make_async_copy(upper_ref, upper, sems.at[0]),
        pltpu.make_async_copy(base_ref, base, sems.at[3]),
    ]

    def put(rows, c, value):
        lower[c, rows, :] = value

    transport(1, ins, refs[22:], put, incoming)
    for copy in incoming:
        copy.wait()
    core = core_ref[0]
    outgoing = []
    for kind, out_ref in ((1, send_ref), (0, keep_ref)):
        start = 4 * (core ^ kind)
        for i in (0, 2):
            c = start + i
            column = jnp.concatenate(
                [jnp.concatenate([upper[c + k], lower[c + k]], 0) for k in range(2)], 1
            )
            end = column + product(high[...], low[...], column)
            for k in range(2):
                column = end[:, k * LANES : (k + 1) * LANES]
                rest = base[c + k] - column
                base[c + k] = column
                for q in range(4):
                    parts[kind, 4 * (i + k) + q] = rest[q * PART : (q + 1) * PART]
            pair, some = pl.ds(c, 2), pl.ds(4 * i, 8)
            outgoing.append(pltpu.make_async_copy(parts.at[kind, some], out_ref.at[some], sems.at[4 + kind * 2 + i // 2]))
            outgoing.append(pltpu.make_async_copy(base.at[pair], end_ref.at[pair], sems.at[8 + kind * 2 + i // 2]))
            outgoing[-2].start()
            outgoing[-1].start()
    for copy in outgoing:
        copy.wait()


def pair_kernel(keep_ref, partner_ref, order_ref, pair_ref):
    pair_ref[...] = keep_ref[...] + partner_ref[...]


def scan_kernel(in_ref, order_ref, out_ref):
    def block(index, carry):
        here = pl.ds(pl.multiple_of(index * 8, 8), 8)
        total = jnp.zeros((8, LANES), F32)
        for k in range(PARTS):
            out_ref[k, here, :] = total
            total = total + in_ref[k, here, :]
        return carry

    lax.fori_loop(0, PART // 8, block, 0)


def share_kernel(core_ref, before_ref, keep_ref, order_ref, out_ref):
    first = (core_ref[0] == 0).astype(F32)
    out_ref[...] = before_ref[...] + first * keep_ref[...]


def finish_kernel(core_ref, base_ref, before_ref, partner_ref, other_ref, out_ref):
    core = core_ref[0]
    flat = out_ref.reshape(ROWS * COLS, LANES)
    second = (core == 1).astype(F32)
    for c in range(COLS):
        mine = core == c // 4
        i = c % 4
        for q in range(4):
            size = min(PART, ROWS - q * PART)
            own = before_ref[4 * i + q, :size] + second * partner_ref[4 * i + q, :size]
            earlier = jnp.where(mine, own, other_ref[4 * i + q, :size])
            flat[pl.ds(q * PART * COLS + c, size, stride=COLS), :] = (
                base_ref[c, q * PART : q * PART + size, :] + earlier
            )


def sort_kernel(me_ref, index_ref, frac_ref, order_ref, out_ref, chosen_ref, spread_ref):
    column_x = index_ref[0]
    bucket = lax.broadcasted_iota(jnp.int32, (TILES, SLOTS), 0)
    further = ((column_x >> 3) - me_ref[0] + TILES) & (TILES - 1)
    chosen = (bucket == further).astype(F32)
    before = lax.broadcasted_iota(jnp.int32, (SLOTS, SLOTS), 0) < lax.broadcasted_iota(jnp.int32, (SLOTS, SLOTS), 1)
    rank = jnp.dot(chosen.astype(BF16), before.astype(F32).astype(BF16), preferred_element_type=F32)
    place = jnp.sum(chosen * rank, axis=0, keepdims=True)
    spread = lax.broadcasted_iota(jnp.int32, (CAP, SLOTS), 0) == place.astype(jnp.int32)
    spread = spread.astype(F32)
    chosen_ref[...] = chosen
    spread_ref[...] = spread
    values = jnp.concatenate(
        [
            (column_x & (COLS - 1)).astype(F32),
            index_ref[1].astype(F32),
            index_ref[2].astype(F32),
            frac_ref[0],
            frac_ref[1],
            jnp.zeros((FIELDS - 5, SLOTS), F32),
        ],
        0,
    )
    for j in range(TILES):
        masked = values * chosen[j : j + 1, :]
        out_ref[j] = lax.dot_general(
            masked, spread, (((1,), (1,)), ((), ())), precision=HIGHEST, preferred_element_type=F32
        )


def observe_kernel(obs_ref, end_ref, order_ref, out_ref, end_high, end_low):
    for c in range(COLS):
        high, low = two_parts(end_ref[c])
        end_high[:, c * LANES : (c + 1) * LANES] = high
        end_low[:, c * LANES : (c + 1) * LANES] = low
    lanes = 2 * CAP
    for j in range(0, TILES, 2):
        fields = [jnp.concatenate([obs_ref[j, i : i + 1], obs_ref[j + 1, i : i + 1]], 1) for i in range(5)]
        column, line, row = [(f + 0.5).astype(jnp.int32) for f in fields[:3]]
        across, upward = fields[3:]
        y = lax.broadcasted_iota(jnp.int32, (LANES, lanes), 0)
        here, after = y == line, y == line + 1
        highs, lows = [], []
        for c in range(COLS):
            mine = column == c
            near = jnp.where(mine, 1.0 - across, 0.0)
            far = jnp.where(mine, across, 0.0)
            weight = jnp.where(here, near, jnp.where(after, far, 0.0))
            high, low = two_parts(weight)
            highs.append(high)
            lows.append(low)
        high, low = jnp.concatenate(highs, 0), jnp.concatenate(lows, 0)
        taken = jnp.dot(end_high[...], high, preferred_element_type=F32)
        taken = taken + jnp.dot(end_high[...], low, preferred_element_type=F32)
        taken = taken + jnp.dot(end_low[...], high, preferred_element_type=F32)
        r = lax.broadcasted_iota(jnp.int32, (PAD, lanes), 0)
        weight = jnp.where(r == row, 1.0 - upward, jnp.where(r == row + 1, upward, 0.0))
        value = jnp.sum(weight * taken, axis=0, keepdims=True)
        out_ref[j : j + 1, :] = value[:, :CAP]
        out_ref[j + 1 : j + 2, :] = value[:, CAP:]


def depart_kernel(count_ref, back_ref, chosen_ref, spread_ref, value_ref, out_ref):
    spread = jnp.dot(back_ref[...], spread_ref[...], precision=HIGHEST, preferred_element_type=F32)
    evolved = jnp.sum(spread * chosen_ref[...], axis=0, keepdims=True)
    live = lax.broadcasted_iota(jnp.int32, (1, SLOTS), 1) < count_ref[0, 0]
    out_ref[...] = jnp.where(live, value_ref[...] - evolved, 0.0)


def hop(blocks, bit, sign):
    moving = [j for j in range(TILES) if j & bit]
    parcel = jnp.concatenate([blocks[j] for j in moving], 0)
    parcel = lax.ppermute(parcel, "tile", [(i, (i + sign * bit) % TILES) for i in range(TILES)])
    size = blocks[0].shape[0]
    result = list(blocks)
    for at, j in enumerate(moving):
        result[j] = parcel[at * size : (at + 1) * size]
    return result


def per_device(
    increment, forcing, error_root, physics, coefficients, obs_index, obs_frac, obs_value, obs_count
):
    state = increment.reshape(ROWS, COLS, LANES)
    drive = forcing.reshape(ROWS, COLS, LANES)
    rates = coefficients.reshape(4, COLS, LANES)
    core = jnp.reshape(lax.axis_index("core"), (1,)).astype(jnp.int32)
    me = jnp.reshape(lax.axis_index("tile"), (1,)).astype(jnp.int32)
    field = PAD * COLS * LANES * 4

    to_west = [(i + 1, i) for i in range(TILES - 1)]
    to_east = [(i, i + 1) for i in range(TILES - 1)]

    wests, easts = pack(state, rates)
    halo0, halo1 = [
        (lax.ppermute(east, "tile", to_east), lax.ppermute(west, "tile", to_west))
        for west, east in zip(wests, easts)
    ]
    base, high, low = call(
        prepare_kernel,
        [shape(COLS, PAD, LANES), shape(PAD, PAD, dtype=BF16), shape(PAD, PAD, dtype=BF16)],
        (state, drive, error_root, physics.reshape(ROWS, ROWS)),
        WIDE,
        scratch=[
            pltpu.VMEM((ROWS, COLS, LANES), F32),
            pltpu.VMEM((ROWS, COLS, LANES), F32),
            pltpu.VMEM((ROWS, ROWS), F32),
            pltpu.VMEM((PAD, PAD), F32),
            pltpu.VMEM((PAD, 2 * LANES), F32),
            pltpu.VMEM((COLS, PAD, LANES), F32),
            pltpu.VMEM((PAD, PAD), BF16),
            pltpu.VMEM((PAD, PAD), BF16),
            pltpu.SemaphoreType.DMA((9,)),
        ],
        flops=8 * 10**9,
        moved=5 * field,
        far=(0, 1, 2),
        far_out=(0, 1, 2),
    )
    upper = call(
        upper_kernel,
        shape(COLS, CHUNKS[0][1], LANES),
        (state, rates, *halo0, *halo0),
        WIDE,
        scratch=[pltpu.VMEM((COLS, CHUNKS[0][1], LANES), F32), pltpu.SemaphoreType.DMA] + transport_scratch(0),
        flops=4 * 10**9,
        moved=field,
        far=range(6),
        far_out=(0,),
    )
    queries, chosen, spread = call(
        sort_kernel,
        [shape(TILES, FIELDS, CAP), shape(TILES, SLOTS), shape(CAP, SLOTS)],
        (me, obs_index, obs_frac, upper),
        8,
        flops=10**8,
        moved=10**6,
        smem=(0,),
        far=(3,),
    )
    blocks = hop([queries[j] for j in range(TILES)], 4, 1)
    parts = shape(PARTS, PART, LANES)
    end, keep, send = call(
        lower_kernel,
        [shape(COLS, PAD, LANES), parts, parts],
        (state, rates, *halo1, *halo0, core, upper, high, low, base, blocks[7]),
        WIDE,
        scratch=[
            pltpu.VMEM((COLS, CHUNKS[0][1], LANES), F32),
            pltpu.VMEM((COLS, CHUNKS[1][1], LANES), F32),
            pltpu.VMEM((COLS, PAD, LANES), F32),
            pltpu.VMEM((PAD, PAD), BF16),
            pltpu.VMEM((PAD, PAD), BF16),
            pltpu.VMEM((2, PARTS, PART, LANES), F32),
            pltpu.SemaphoreType.DMA((12,)),
        ]
        + transport_scratch(1),
        flops=6 * 10**9,
        moved=5 * field,
        smem=(6,),
        far=(0, 1, 2, 3, 4, 5, 7, 8, 9, 10, 11),
        far_out=range(3),
    )
    swap = [(0, 1), (1, 0)]
    partner = lax.ppermute(send, "core", swap)
    blocks = hop(blocks, 2, 1)
    pair = call(pair_kernel, parts, (keep, partner, blocks[7]), 6, flops=10**6, moved=2 * field)
    gathered = lax.all_to_all(pair, ("y", "x"), 0, 0, tiled=True)
    blocks = hop(blocks, 1, 1)
    arrived = jnp.concatenate(blocks, 0).reshape(TILES, FIELDS, CAP)
    found = call(
        observe_kernel,
        shape(TILES, CAP),
        (arrived, end, pair),
        10,
        scratch=[pltpu.VMEM((PAD, COLS * LANES), BF16), pltpu.VMEM((PAD, COLS * LANES), BF16)],
        flops=3 * 10**9,
        moved=field,
        far=(2,),
    )
    totals = call(scan_kernel, parts, (gathered, found), 6, flops=10**7, moved=field)
    before = lax.all_to_all(totals, ("y", "x"), 0, 0, tiled=True)
    back = [found[j : j + 1] for j in range(TILES)]
    for bit in (4, 2, 1):
        back = hop(back, bit, -1)
    departure = call(
        depart_kernel,
        shape(1, SLOTS),
        (obs_count, jnp.concatenate(back, 0), chosen, spread, obs_value),
        4,
        flops=10**7,
        moved=10**6,
        smem=(0,),
    )
    for_partner = call(
        share_kernel, parts, (core, before, keep, departure), 6, flops=10**7, moved=2 * field, smem=(0,), far=(3,)
    )
    other = lax.ppermute(for_partner, "core", swap)
    summed = call(
        finish_kernel,
        shape(ROWS, COLS, LANES),
        (core, base, before, partner, other),
        10,
        flops=10**7,
        moved=4 * field,
        smem=(0,),
    )
    return summed.reshape(increment.shape), departure


def solution(mesh):
    split = Mesh(mesh.devices.reshape(GRID_Y, GRID_X, CORES, TILES), ("y", "x", "core", "tile"))
    win = ("y", "x", "core")
    return jax.shard_map(
        per_device,
        mesh=split,
        in_specs=(
            P(win, None, None, "tile", None),
            P(win, None, None, "tile", None),
            P(),
            P(win, None, None),
            P(win, None, "tile", None),
            P(None, win, "tile"),
            P(None, win, "tile"),
            P(win, "tile"),
            P(win, "tile"),
        ),
        out_specs=(P(win, None, None, "tile", None), P(win, "tile")),
        check_vma=False,
    )
```

```python
import jax
import jax.numpy as jnp
from jax import lax
from jax.experimental import pallas as pl
from jax.experimental.pallas import tpu as pltpu
from jax.sharding import Mesh, PartitionSpec as P

STEPS = 6
ROWS = 411
PAD = 416
COLS = 8
LANES = 128
GRID_Y = 4
GRID_X = 4
CORES = 2
PARTS = 16
PART = 104
TILES = 8
HALF = 208
SLOTS = 512
CAP = 128
FIELDS = 8

F32 = jnp.float32
BF16 = jnp.bfloat16
HIGHEST = lax.Precision.HIGHEST
MIB = 1 << 20
WIDE = 56


def call(body, outs, ins, mib, scratch=(), flops=0, moved=0, smem=(), far=(), far_out=(), unread=()):
    specs = [
        pl.BlockSpec(
            memory_space=pltpu.SMEM if at in smem else pltpu.HBM if at in far else pl.ANY if at in unread else pltpu.VMEM
        )
        for at in range(len(ins))
    ]
    many = isinstance(outs, (list, tuple))
    out_specs = [
        pl.BlockSpec(memory_space=pltpu.HBM if at in far_out else pltpu.VMEM)
        for at in range(len(outs) if many else 1)
    ]
    return pl.pallas_call(
        body,
        out_shape=outs,
        in_specs=specs,
        out_specs=out_specs if many else out_specs[0],
        scratch_shapes=list(scratch),
        compiler_params=pltpu.CompilerParams(vmem_limit_bytes=mib * MIB),
        cost_estimate=pl.CostEstimate(flops=flops, bytes_accessed=moved, transcendentals=0),
    )(*ins)


def shape(*dims, dtype=F32):
    return jax.ShapeDtypeStruct(dims, dtype)


def two_parts(value):
    high = value.astype(BF16)
    low = (value - high.astype(F32)).astype(BF16)
    return high, low


def product(left_high, left_low, right):
    high, low = two_parts(right)
    total = jnp.dot(left_high, high, preferred_element_type=F32)
    total = total + jnp.dot(left_high, low, preferred_element_type=F32)
    return total + jnp.dot(left_low, high, preferred_element_type=F32)


def pack_kernel(inc_ref, rate_ref, west_ref, east_ref, held, rates, west, east, in_sems, out_sems):
    count = PAD // PART
    incoming = [pltpu.make_async_copy(rate_ref, rates, in_sems.at[count])]
    for b in range(count):
        rows = pl.ds(b * PART, min(PART, ROWS - b * PART))
        incoming.append(pltpu.make_async_copy(inc_ref.at[rows], held.at[rows], in_sems.at[b]))
    for copy in incoming:
        copy.start()
    flat = held.reshape(PAD * COLS, LANES)
    outgoing = []
    incoming[0].wait()
    for b in range(count):
        incoming[b + 1].wait()
        size = min(PART, ROWS - b * PART)
        for c in range(COLS):
            column = flat[pl.ds(b * PART * COLS + c, size, stride=COLS), :]
            if size < PART:
                weights = [rates[i, c : c + 1, :] for i in range(4)]
                column = jnp.concatenate([column] + weights + [jnp.zeros((1, LANES), F32)], 0)
            if c < STEPS:
                west[c, b * PART : (b + 1) * PART, :] = column
            if c >= COLS - STEPS:
                east[c - COLS + STEPS, b * PART : (b + 1) * PART, :] = column
        rows = pl.ds(b * PART, PART)
        outgoing.append(pltpu.make_async_copy(west.at[:, rows], west_ref.at[:, rows], out_sems.at[2 * b]))
        outgoing.append(pltpu.make_async_copy(east.at[:, rows], east_ref.at[:, rows], out_sems.at[2 * b + 1]))
        outgoing[-2].start()
        outgoing[-1].start()
    for copy in outgoing:
        copy.wait()


def pack(state, rates):
    halo = shape(STEPS, PAD, LANES)
    return call(
        pack_kernel,
        [halo, halo],
        (state, rates),
        WIDE,
        scratch=[
            pltpu.VMEM((PAD, COLS, LANES), F32),
            pltpu.VMEM((4, COLS, LANES), F32),
            pltpu.VMEM((STEPS, PAD, LANES), F32),
            pltpu.VMEM((STEPS, PAD, LANES), F32),
            pltpu.SemaphoreType.DMA((PAD // PART + 1,)),
            pltpu.SemaphoreType.DMA((2 * PAD // PART,)),
        ],
        moved=3 * PAD * COLS * LANES * 4,
        far=(0, 1),
        far_out=(0, 1),
    )


def prepare_kernel(
    inc_ref, forcing_ref, root_ref, physics_ref, order_ref, base_ref, high_ref, low_ref,
    start, force, root, square, drive, base, high, low, sems
):
    incoming = [
        pltpu.make_async_copy(root_ref, root, sems.at[0]),
        pltpu.make_async_copy(forcing_ref, force, sems.at[1]),
        pltpu.make_async_copy(inc_ref, start, sems.at[2]),
    ]
    for copy in incoming:
        copy.start()
    square[...] = jnp.zeros((PAD, PAD), F32)
    square[:ROWS, :ROWS] = 0.2 * physics_ref[...]
    once = square[...]
    twice = 2.0 * once + product(*two_parts(once), once)
    twice_parts = two_parts(twice)
    four = 2.0 * twice + product(*twice_parts, twice)
    six = twice + four + product(*twice_parts, four)
    high[...], low[...] = two_parts(six)
    outgoing = [
        pltpu.make_async_copy(high, high_ref, sems.at[3]),
        pltpu.make_async_copy(low, low_ref, sems.at[4]),
    ]
    for copy in outgoing:
        copy.start()
    for copy in incoming:
        copy.wait()
    square[:ROWS, :ROWS] = root[...]
    root_high, root_low = two_parts(square[...])
    force_flat = force.reshape(ROWS * COLS, LANES)
    start_flat = start.reshape(ROWS * COLS, LANES)
    drive[ROWS - 3 :, :] = jnp.zeros((PAD - ROWS + 3, 2 * LANES), F32)
    for c in range(0, COLS, 2):
        drive[:ROWS, :LANES] = force_flat[pl.ds(c, ROWS, stride=COLS), :]
        drive[:ROWS, LANES:] = force_flat[pl.ds(c + 1, ROWS, stride=COLS), :]
        forced = product(root_high, root_low, drive[...])
        for k in range(2):
            column = forced[:, k * LANES : (k + 1) * LANES]
            base[c + k, :ROWS, :] = start_flat[pl.ds(c + k, ROWS, stride=COLS), :] - column[:ROWS]
            base[c + k, ROWS:, :] = column[ROWS:]
        pair = pl.ds(c, 2)
        outgoing.append(pltpu.make_async_copy(base.at[pair], base_ref.at[pair], sems.at[5 + c // 2]))
        outgoing[-1].start()
    for copy in outgoing:
        copy.wait()


def advance_kernel(
    inc_ref, rate_ref, west_ref, east_ref, core_ref, high_ref, low_ref, base_ref,
    end_ref, keep_ref, send_ref,
    rate, west_rate, east_rate, table, band, own, west, east, odd, even, state, base, high, low, sems
):
    at = PAD - 8
    weights = [
        pltpu.make_async_copy(rate_ref, rate, sems.at[0]),
        pltpu.make_async_copy(west_ref.at[:, pl.ds(at, 8)], west_rate, sems.at[1]),
        pltpu.make_async_copy(east_ref.at[:, pl.ds(at, 8)], east_rate, sems.at[2]),
    ]
    fields = []
    for b in range(2):
        valid = min(HALF, ROWS - b * HALF)
        rows = pl.ds(b * HALF, HALF)
        mine = pl.ds(b * HALF, valid)
        fields.append(pltpu.make_async_copy(inc_ref.at[mine], own.at[mine], sems.at[3 + 3 * b]))
        fields.append(pltpu.make_async_copy(west_ref.at[:, rows], west.at[:, rows], sems.at[4 + 3 * b]))
        fields.append(pltpu.make_async_copy(east_ref.at[:, rows], east.at[:, rows], sems.at[5 + 3 * b]))
    later = [
        pltpu.make_async_copy(high_ref, high, sems.at[9]),
        pltpu.make_async_copy(low_ref, low, sems.at[10]),
        pltpu.make_async_copy(base_ref, base, sems.at[11]),
    ]
    for copy in weights + fields + later:
        copy.start()
    own[ROWS:] = jnp.zeros((PAD - ROWS, COLS, LANES), F32)
    for copy in weights:
        copy.wait()
    row = lax.broadcasted_iota(jnp.int32, (LANES, LANES), 0)
    lane = lax.broadcasted_iota(jnp.int32, (LANES, LANES), 1)
    wide = COLS + 2 * STEPS
    first = ROWS - at
    for j in range(1, wide - 1):
        if j < STEPS:
            rates = [west_rate[j, first + i : first + i + 1, :] for i in range(4)]
        elif j < STEPS + COLS:
            rates = [rate[i, j - STEPS : j - STEPS + 1, :] for i in range(4)]
        else:
            rates = [east_rate[j - STEPS - COLS, first + i : first + i + 1, :] for i in range(4)]
        center = 1.0 - (rates[0] + rates[1] + rates[2] + rates[3])
        table[2 * j] = jnp.broadcast_to(rates[0], (8, LANES))
        table[2 * j + 1] = jnp.broadcast_to(rates[1], (8, LANES))
        along = jnp.where(row == lane, center, 0.0)
        along = jnp.where(row == lane + 1, rates[2], along)
        along = jnp.where(row == lane - 1, rates[3], along)
        along_high, along_low = two_parts(along)
        band[j, :LANES, :LANES] = along_high
        band[j, LANES:, :LANES] = along_high
        band[j, :LANES, LANES:] = along_low
        band[j, LANES:, LANES:] = jnp.zeros((LANES, LANES), BF16)
    flat = own.reshape(PAD * COLS, LANES)

    for copy in fields:
        copy.wait()

    def block(b, carry):
        rows = pl.ds(pl.multiple_of(b * HALF, 16), HALF)

        def load(step, j):
            if step > 0:
                return (odd if step % 2 else even)[j]
            if j < STEPS:
                return west[j, rows, :]
            if j < STEPS + COLS:
                return flat[pl.ds(b * (HALF * COLS) + j - STEPS, HALF, stride=COLS), :]
            return east[j - STEPS - COLS, rows, :]

        def tiles(value):
            return value.reshape(HALF // 8, 8, LANES)

        for step in range(1, STEPS + 1):
            for j in range(step, wide - step):
                parts = jnp.concatenate(two_parts(load(step - 1, j)), 1)
                along = jnp.dot(parts, band[j], preferred_element_type=F32)
                total = tiles(along[:, :LANES] + along[:, LANES:])
                total = total + table[2 * j] * tiles(load(step - 1, j + 1))
                total = total + table[2 * j + 1] * tiles(load(step - 1, j - 1))
                total = total.reshape(HALF, LANES)
                if step == STEPS:
                    state[j - STEPS, rows, :] = total
                else:
                    (odd if step % 2 else even)[j] = total
        return carry

    lax.fori_loop(0, 2, block, 0)

    for copy in later:
        copy.wait()
    core = core_ref[0]
    outgoing = []
    for kind, out_ref in ((1, send_ref), (0, keep_ref)):
        start = 4 * (core ^ kind)
        for i in (0, 2):
            c = start + i
            column = jnp.concatenate([state[c], state[c + 1]], 1)
            end = column + product(high[...], low[...], column)
            for k in range(2):
                column = end[:, k * LANES : (k + 1) * LANES]
                state[c + k] = column
                rest = base[c + k] - column
                for q in range(4):
                    out_ref[4 * (i + k) + q] = rest[q * PART : (q + 1) * PART]
            pair = pl.ds(c, 2)
            outgoing.append(pltpu.make_async_copy(state.at[pair], end_ref.at[pair], sems.at[12 + kind * 2 + i // 2]))
            outgoing[-1].start()
    for copy in outgoing:
        copy.wait()


def pair_kernel(keep_ref, partner_ref, order_ref, pair_ref):
    pair_ref[...] = keep_ref[...] + partner_ref[...]


def scan_kernel(in_ref, order_ref, out_ref):
    def block(index, carry):
        here = pl.ds(pl.multiple_of(index * 8, 8), 8)
        total = jnp.zeros((8, LANES), F32)
        for k in range(PARTS):
            out_ref[k, here, :] = total
            total = total + in_ref[k, here, :]
        return carry

    lax.fori_loop(0, PART // 8, block, 0)


def share_kernel(core_ref, before_ref, keep_ref, order_ref, out_ref):
    first = (core_ref[0] == 0).astype(F32)
    out_ref[...] = before_ref[...] + first * keep_ref[...]


def finish_kernel(core_ref, base_ref, before_ref, partner_ref, other_ref, out_ref):
    core = core_ref[0]
    flat = out_ref.reshape(ROWS * COLS, LANES)
    second = (core == 1).astype(F32)
    for c in range(COLS):
        mine = core == c // 4
        i = c % 4
        for q in range(4):
            size = min(PART, ROWS - q * PART)
            own = before_ref[4 * i + q, :size] + second * partner_ref[4 * i + q, :size]
            earlier = jnp.where(mine, own, other_ref[4 * i + q, :size])
            flat[pl.ds(q * PART * COLS + c, size, stride=COLS), :] = (
                base_ref[c, q * PART : q * PART + size, :] + earlier
            )


def sort_kernel(me_ref, index_ref, frac_ref, order_ref, out_ref, chosen_ref, spread_ref):
    column_x = index_ref[0]
    bucket = lax.broadcasted_iota(jnp.int32, (TILES, SLOTS), 0)
    further = ((column_x >> 3) - me_ref[0] + TILES) & (TILES - 1)
    chosen = (bucket == further).astype(F32)
    before = lax.broadcasted_iota(jnp.int32, (SLOTS, SLOTS), 0) < lax.broadcasted_iota(jnp.int32, (SLOTS, SLOTS), 1)
    rank = jnp.dot(chosen.astype(BF16), before.astype(F32).astype(BF16), preferred_element_type=F32)
    place = jnp.sum(chosen * rank, axis=0, keepdims=True)
    spread = lax.broadcasted_iota(jnp.int32, (CAP, SLOTS), 0) == place.astype(jnp.int32)
    spread = spread.astype(F32)
    chosen_ref[...] = chosen
    spread_ref[...] = spread
    values = jnp.concatenate(
        [
            (column_x & (COLS - 1)).astype(F32),
            index_ref[1].astype(F32),
            index_ref[2].astype(F32),
            frac_ref[0],
            frac_ref[1],
            jnp.zeros((FIELDS - 5, SLOTS), F32),
        ],
        0,
    )
    for j in range(TILES):
        masked = values * chosen[j : j + 1, :]
        out_ref[j] = lax.dot_general(
            masked, spread, (((1,), (1,)), ((), ())), precision=HIGHEST, preferred_element_type=F32
        )


def hand_on_kernel(in_ref, west_ref, east_ref, out_ref):
    out_ref[...] = in_ref[...]


def observe_kernel(obs_ref, end_ref, order_ref, out_ref, end_high, end_low):
    for c in range(COLS):
        high, low = two_parts(end_ref[c])
        end_high[:, c * LANES : (c + 1) * LANES] = high
        end_low[:, c * LANES : (c + 1) * LANES] = low
    lanes = 2 * CAP
    for j in range(0, TILES, 2):
        fields = [jnp.concatenate([obs_ref[j, i : i + 1], obs_ref[j + 1, i : i + 1]], 1) for i in range(5)]
        column, line, row = [(f + 0.5).astype(jnp.int32) for f in fields[:3]]
        across, upward = fields[3:]
        y = lax.broadcasted_iota(jnp.int32, (LANES, lanes), 0)
        here, after = y == line, y == line + 1
        highs, lows = [], []
        for c in range(COLS):
            mine = column == c
            near = jnp.where(mine, 1.0 - across, 0.0)
            far = jnp.where(mine, across, 0.0)
            weight = jnp.where(here, near, jnp.where(after, far, 0.0))
            high, low = two_parts(weight)
            highs.append(high)
            lows.append(low)
        high, low = jnp.concatenate(highs, 0), jnp.concatenate(lows, 0)
        taken = jnp.dot(end_high[...], high, preferred_element_type=F32)
        taken = taken + jnp.dot(end_high[...], low, preferred_element_type=F32)
        taken = taken + jnp.dot(end_low[...], high, preferred_element_type=F32)
        r = lax.broadcasted_iota(jnp.int32, (PAD, lanes), 0)
        weight = jnp.where(r == row, 1.0 - upward, jnp.where(r == row + 1, upward, 0.0))
        value = jnp.sum(weight * taken, axis=0, keepdims=True)
        out_ref[j : j + 1, :] = value[:, :CAP]
        out_ref[j + 1 : j + 2, :] = value[:, CAP:]


def depart_kernel(count_ref, back_ref, chosen_ref, spread_ref, value_ref, out_ref):
    spread = jnp.dot(back_ref[...], spread_ref[...], precision=HIGHEST, preferred_element_type=F32)
    evolved = jnp.sum(spread * chosen_ref[...], axis=0, keepdims=True)
    live = lax.broadcasted_iota(jnp.int32, (1, SLOTS), 1) < count_ref[0, 0]
    out_ref[...] = jnp.where(live, value_ref[...] - evolved, 0.0)


def hop(blocks, bit, sign):
    moving = [j for j in range(TILES) if j & bit]
    parcel = jnp.concatenate([blocks[j] for j in moving], 0)
    parcel = lax.ppermute(parcel, "tile", [(i, (i + sign * bit) % TILES) for i in range(TILES)])
    size = blocks[0].shape[0]
    result = list(blocks)
    for at, j in enumerate(moving):
        result[j] = parcel[at * size : (at + 1) * size]
    return result


def per_device(
    increment, forcing, error_root, physics, coefficients, obs_index, obs_frac, obs_value, obs_count
):
    state = increment.reshape(ROWS, COLS, LANES)
    drive = forcing.reshape(ROWS, COLS, LANES)
    rates = coefficients.reshape(4, COLS, LANES)
    core = jnp.reshape(lax.axis_index("core"), (1,)).astype(jnp.int32)
    me = jnp.reshape(lax.axis_index("tile"), (1,)).astype(jnp.int32)
    field = PAD * COLS * LANES * 4

    to_west = [(i + 1, i) for i in range(TILES - 1)]
    to_east = [(i, i + 1) for i in range(TILES - 1)]

    west, east = pack(state, rates)
    from_west = lax.ppermute(east, "tile", to_east)
    from_east = lax.ppermute(west, "tile", to_west)
    base, high, low = call(
        prepare_kernel,
        [shape(COLS, PAD, LANES), shape(PAD, PAD, dtype=BF16), shape(PAD, PAD, dtype=BF16)],
        (state, drive, error_root, physics.reshape(ROWS, ROWS), west),
        WIDE,
        scratch=[
            pltpu.VMEM((ROWS, COLS, LANES), F32),
            pltpu.VMEM((ROWS, COLS, LANES), F32),
            pltpu.VMEM((ROWS, ROWS), F32),
            pltpu.VMEM((PAD, PAD), F32),
            pltpu.VMEM((PAD, 2 * LANES), F32),
            pltpu.VMEM((COLS, PAD, LANES), F32),
            pltpu.VMEM((PAD, PAD), BF16),
            pltpu.VMEM((PAD, PAD), BF16),
            pltpu.SemaphoreType.DMA((9,)),
        ],
        flops=10**8,
        moved=10**6,
        far=(0, 1, 2),
        far_out=(0, 1, 2),
        unread=(4,),
    )
    queries, chosen, spread = call(
        sort_kernel,
        [shape(TILES, FIELDS, CAP), shape(TILES, SLOTS), shape(CAP, SLOTS)],
        (me, obs_index, obs_frac, base),
        8,
        flops=10**7,
        moved=10**5,
        smem=(0,),
        unread=(3,),
    )
    queries = call(
        hand_on_kernel,
        shape(TILES, FIELDS, CAP),
        (queries, from_west, from_east),
        4,
        moved=10**5,
        unread=(1, 2),
    )
    blocks = hop([queries[j] for j in range(TILES)], 4, 1)
    parts = shape(PARTS, PART, LANES)
    wide = COLS + 2 * STEPS
    end, keep, send = call(
        advance_kernel,
        [shape(COLS, PAD, LANES), parts, parts],
        (state, rates, from_west, from_east, core, high, low, base),
        30,
        scratch=[
            pltpu.VMEM((4, COLS, LANES), F32),
            pltpu.VMEM((STEPS, 8, LANES), F32),
            pltpu.VMEM((STEPS, 8, LANES), F32),
            pltpu.VMEM((2 * wide, 8, LANES), F32),
            pltpu.VMEM((wide, 2 * LANES, 2 * LANES), BF16),
            pltpu.VMEM((PAD, COLS, LANES), F32),
            pltpu.VMEM((STEPS, PAD, LANES), F32),
            pltpu.VMEM((STEPS, PAD, LANES), F32),
            pltpu.VMEM((wide, HALF, LANES), F32),
            pltpu.VMEM((wide, HALF, LANES), F32),
            pltpu.VMEM((COLS, PAD, LANES), F32),
            pltpu.VMEM((COLS, PAD, LANES), F32),
            pltpu.VMEM((PAD, PAD), BF16),
            pltpu.VMEM((PAD, PAD), BF16),
            pltpu.SemaphoreType.DMA((16,)),
        ],
        flops=15 * 10**9,
        moved=6 * field,
        smem=(4,),
        far=(0, 1, 2, 3, 5, 6, 7),
        far_out=(0,),
    )
    swap = [(0, 1), (1, 0)]
    partner = lax.ppermute(send, "core", swap)
    blocks = hop(blocks, 2, 1)
    pair = call(pair_kernel, parts, (keep, partner, blocks[7]), 6, flops=10**6, moved=2 * field, unread=(2,))
    gathered = lax.all_to_all(pair, ("y", "x"), 0, 0, tiled=True)
    blocks = hop(blocks, 1, 1)
    arrived = jnp.concatenate(blocks, 0).reshape(TILES, FIELDS, CAP)
    found = call(
        observe_kernel,
        shape(TILES, CAP),
        (arrived, end, pair),
        10,
        scratch=[pltpu.VMEM((PAD, COLS * LANES), BF16), pltpu.VMEM((PAD, COLS * LANES), BF16)],
        flops=3 * 10**9,
        moved=field,
        unread=(2,),
    )
    totals = call(scan_kernel, parts, (gathered, found), 6, flops=10**7, moved=field, unread=(1,))
    before = lax.all_to_all(totals, ("y", "x"), 0, 0, tiled=True)
    back = [found[j : j + 1] for j in range(TILES)]
    for bit in (4, 2, 1):
        back = hop(back, bit, -1)
    departure = call(
        depart_kernel,
        shape(1, SLOTS),
        (obs_count, jnp.concatenate(back, 0), chosen, spread, obs_value),
        4,
        flops=10**7,
        moved=10**6,
        smem=(0,),
    )
    for_partner = call(
        share_kernel, parts, (core, before, keep, departure), 6, flops=10**7, moved=2 * field, smem=(0,), unread=(3,)
    )
    other = lax.ppermute(for_partner, "core", swap)
    summed = call(
        finish_kernel,
        shape(ROWS, COLS, LANES),
        (core, base, before, partner, other),
        10,
        flops=10**7,
        moved=4 * field,
        smem=(0,),
    )
    return summed.reshape(increment.shape), departure


def solution(mesh):
    split = Mesh(mesh.devices.reshape(GRID_Y, GRID_X, CORES, TILES), ("y", "x", "core", "tile"))
    win = ("y", "x", "core")
    return jax.shard_map(
        per_device,
        mesh=split,
        in_specs=(
            P(win, None, None, "tile", None),
            P(win, None, None, "tile", None),
            P(),
            P(win, None, None),
            P(win, None, "tile", None),
            P(None, win, "tile"),
            P(None, win, "tile"),
            P(win, "tile"),
            P(win, "tile"),
        ),
        out_specs=(P(win, None, None, "tile", None), P(win, "tile")),
        check_vma=False,
    )
```

```python
import jax
import jax.numpy as jnp
from jax import lax
from jax.experimental import pallas as pl
from jax.experimental.pallas import tpu as pltpu
from jax.sharding import Mesh, PartitionSpec as P

STEPS = 6
ROWS = 411
PAD = 416
COLS = 8
LANES = 128
GRID_Y = 4
GRID_X = 4
CORES = 2
PARTS = 16
PART = 104
TILES = 8
HALF = 208
SLOTS = 512
CAP = 128
FIELDS = 8

F32 = jnp.float32
BF16 = jnp.bfloat16
HIGHEST = lax.Precision.HIGHEST
MIB = 1 << 20
WIDE = 56


def call(body, outs, ins, scratch=(), flops=0, moved=0, smem=(), far=(), far_out=()):
    specs = [
        pl.BlockSpec(memory_space=pltpu.SMEM if at in smem else pl.ANY if at in far else pltpu.VMEM)
        for at in range(len(ins))
    ]
    many = isinstance(outs, (list, tuple))
    out_specs = [
        pl.BlockSpec(memory_space=pl.ANY if at in far_out else pltpu.VMEM)
        for at in range(len(outs) if many else 1)
    ]
    return pl.pallas_call(
        body,
        out_shape=outs,
        in_specs=specs,
        out_specs=out_specs if many else out_specs[0],
        scratch_shapes=list(scratch),
        compiler_params=pltpu.CompilerParams(vmem_limit_bytes=WIDE * MIB),
        cost_estimate=pl.CostEstimate(flops=flops, bytes_accessed=moved, transcendentals=0),
    )(*ins)


def shape(*dims, dtype=F32):
    return jax.ShapeDtypeStruct(dims, dtype)


def two_parts(value):
    high = value.astype(BF16)
    low = (value - high.astype(F32)).astype(BF16)
    return high, low


def product(left_high, left_low, right):
    high, low = two_parts(right)
    total = jnp.dot(left_high, high, preferred_element_type=F32)
    total = total + jnp.dot(left_high, low, preferred_element_type=F32)
    return total + jnp.dot(left_low, high, preferred_element_type=F32)


def pack_kernel(inc_ref, rate_ref, west_ref, east_ref, sent_ref, held, rates, west, east, in_sems, out_sems):
    count = PAD // PART
    incoming = [pltpu.make_async_copy(rate_ref, rates, in_sems.at[count])]
    for b in range(count):
        rows = pl.ds(b * PART, min(PART, ROWS - b * PART))
        incoming.append(pltpu.make_async_copy(inc_ref.at[rows], held.at[rows], in_sems.at[b]))
    for copy in incoming:
        copy.start()
    sent_ref[...] = jnp.zeros((8, LANES), F32)
    flat = held.reshape(PAD * COLS, LANES)
    outgoing = []
    incoming[0].wait()
    for b in range(count):
        incoming[b + 1].wait()
        size = min(PART, ROWS - b * PART)
        for c in range(COLS):
            column = flat[pl.ds(b * PART * COLS + c, size, stride=COLS), :]
            if size < PART:
                weights = [rates[i, c : c + 1, :] for i in range(4)]
                column = jnp.concatenate([column] + weights + [jnp.zeros((1, LANES), F32)], 0)
            if c < STEPS:
                west[c, b * PART : (b + 1) * PART, :] = column
            if c >= COLS - STEPS:
                east[c - COLS + STEPS, b * PART : (b + 1) * PART, :] = column
        rows = pl.ds(b * PART, PART)
        outgoing.append(pltpu.make_async_copy(west.at[:, rows], west_ref.at[:, rows], out_sems.at[2 * b]))
        outgoing.append(pltpu.make_async_copy(east.at[:, rows], east_ref.at[:, rows], out_sems.at[2 * b + 1]))
        outgoing[-2].start()
        outgoing[-1].start()
    for copy in outgoing:
        copy.wait()


def pack(state, rates):
    halo = shape(STEPS, PAD, LANES)
    return call(
        pack_kernel,
        [halo, halo, shape(8, LANES)],
        (state, rates),
        scratch=[
            pltpu.VMEM((PAD, COLS, LANES), F32),
            pltpu.VMEM((4, COLS, LANES), F32),
            pltpu.VMEM((STEPS, PAD, LANES), F32),
            pltpu.VMEM((STEPS, PAD, LANES), F32),
            pltpu.SemaphoreType.DMA((PAD // PART + 1,)),
            pltpu.SemaphoreType.DMA((2 * PAD // PART,)),
        ],
        moved=3 * PAD * COLS * LANES * 4,
        far=(0, 1),
        far_out=(0, 1),
    )


def prepare_kernel(
    inc_ref, forcing_ref, root_ref, physics_ref, order_ref, base_ref, high_ref, low_ref, ready_ref,
    start, force, root, square, drive, base, high, low, sems
):
    incoming = [
        pltpu.make_async_copy(root_ref, root, sems.at[0]),
        pltpu.make_async_copy(forcing_ref, force, sems.at[1]),
        pltpu.make_async_copy(inc_ref, start, sems.at[2]),
    ]
    for copy in incoming:
        copy.start()
    ready_ref[...] = jnp.zeros((8, LANES), F32)
    square[...] = jnp.zeros((PAD, PAD), F32)
    square[:ROWS, :ROWS] = 0.2 * physics_ref[...]
    once = square[...]
    twice = 2.0 * once + product(*two_parts(once), once)
    twice_parts = two_parts(twice)
    four = 2.0 * twice + product(*twice_parts, twice)
    six = twice + four + product(*twice_parts, four)
    high[...], low[...] = two_parts(six)
    outgoing = [
        pltpu.make_async_copy(high, high_ref, sems.at[3]),
        pltpu.make_async_copy(low, low_ref, sems.at[4]),
    ]
    for copy in outgoing:
        copy.start()
    for copy in incoming:
        copy.wait()
    square[:ROWS, :ROWS] = root[...]
    root_high, root_low = two_parts(square[...])
    force_flat = force.reshape(ROWS * COLS, LANES)
    start_flat = start.reshape(ROWS * COLS, LANES)
    drive[ROWS - 3 :, :] = jnp.zeros((PAD - ROWS + 3, 2 * LANES), F32)
    for c in range(0, COLS, 2):
        drive[:ROWS, :LANES] = force_flat[pl.ds(c, ROWS, stride=COLS), :]
        drive[:ROWS, LANES:] = force_flat[pl.ds(c + 1, ROWS, stride=COLS), :]
        forced = product(root_high, root_low, drive[...])
        for k in range(2):
            column = forced[:, k * LANES : (k + 1) * LANES]
            base[c + k, :ROWS, :] = start_flat[pl.ds(c + k, ROWS, stride=COLS), :] - column[:ROWS]
            base[c + k, ROWS:, :] = column[ROWS:]
        pair = pl.ds(c, 2)
        outgoing.append(pltpu.make_async_copy(base.at[pair], base_ref.at[pair], sems.at[5 + c // 2]))
        outgoing[-1].start()
    for copy in outgoing:
        copy.wait()


def advance_kernel(
    inc_ref, rate_ref, west_ref, east_ref, core_ref, high_ref, low_ref, base_ref, order_ref,
    end_ref, keep_ref, send_ref,
    rate, west_rate, east_rate, table, band, own, west, east, odd, even, state, base, high, low, sems
):
    at = PAD - 8
    weights = [
        pltpu.make_async_copy(rate_ref, rate, sems.at[0]),
        pltpu.make_async_copy(west_ref.at[:, pl.ds(at, 8)], west_rate, sems.at[1]),
        pltpu.make_async_copy(east_ref.at[:, pl.ds(at, 8)], east_rate, sems.at[2]),
    ]
    fields = []
    for b in range(2):
        valid = min(HALF, ROWS - b * HALF)
        rows = pl.ds(b * HALF, HALF)
        mine = pl.ds(b * HALF, valid)
        fields.append(pltpu.make_async_copy(inc_ref.at[mine], own.at[mine], sems.at[3 + 3 * b]))
        fields.append(pltpu.make_async_copy(west_ref.at[:, rows], west.at[:, rows], sems.at[4 + 3 * b]))
        fields.append(pltpu.make_async_copy(east_ref.at[:, rows], east.at[:, rows], sems.at[5 + 3 * b]))
    later = [
        pltpu.make_async_copy(high_ref, high, sems.at[9]),
        pltpu.make_async_copy(low_ref, low, sems.at[10]),
        pltpu.make_async_copy(base_ref, base, sems.at[11]),
    ]
    for copy in weights + fields + later:
        copy.start()
    own[ROWS:] = jnp.zeros((PAD - ROWS, COLS, LANES), F32)
    for copy in weights:
        copy.wait()
    row = lax.broadcasted_iota(jnp.int32, (LANES, LANES), 0)
    lane = lax.broadcasted_iota(jnp.int32, (LANES, LANES), 1)
    wide = COLS + 2 * STEPS
    first = ROWS - at
    for j in range(1, wide - 1):
        if j < STEPS:
            rates = [west_rate[j, first + i : first + i + 1, :] for i in range(4)]
        elif j < STEPS + COLS:
            rates = [rate[i, j - STEPS : j - STEPS + 1, :] for i in range(4)]
        else:
            rates = [east_rate[j - STEPS - COLS, first + i : first + i + 1, :] for i in range(4)]
        center = 1.0 - (rates[0] + rates[1] + rates[2] + rates[3])
        table[2 * j] = jnp.broadcast_to(rates[0], (8, LANES))
        table[2 * j + 1] = jnp.broadcast_to(rates[1], (8, LANES))
        along = jnp.where(row == lane, center, 0.0)
        along = jnp.where(row == lane + 1, rates[2], along)
        along = jnp.where(row == lane - 1, rates[3], along)
        along_high, along_low = two_parts(along)
        band[j, :LANES, :LANES] = along_high
        band[j, LANES:, :LANES] = along_high
        band[j, :LANES, LANES:] = along_low
        band[j, LANES:, LANES:] = jnp.zeros((LANES, LANES), BF16)
    flat = own.reshape(PAD * COLS, LANES)

    for copy in fields:
        copy.wait()

    def block(b, carry):
        rows = pl.ds(pl.multiple_of(b * HALF, 16), HALF)

        def load(step, j):
            if step > 0:
                return (odd if step % 2 else even)[j]
            if j < STEPS:
                return west[j, rows, :]
            if j < STEPS + COLS:
                return flat[pl.ds(b * (HALF * COLS) + j - STEPS, HALF, stride=COLS), :]
            return east[j - STEPS - COLS, rows, :]

        def tiles(value):
            return value.reshape(HALF // 8, 8, LANES)

        for step in range(1, STEPS + 1):
            for j in range(step, wide - step):
                parts = jnp.concatenate(two_parts(load(step - 1, j)), 1)
                along = jnp.dot(parts, band[j], preferred_element_type=F32)
                total = tiles(along[:, :LANES] + along[:, LANES:])
                total = total + table[2 * j] * tiles(load(step - 1, j + 1))
                total = total + table[2 * j + 1] * tiles(load(step - 1, j - 1))
                total = total.reshape(HALF, LANES)
                if step == STEPS:
                    state[j - STEPS, rows, :] = total
                else:
                    (odd if step % 2 else even)[j] = total
        return carry

    lax.fori_loop(0, 2, block, 0)

    for copy in later:
        copy.wait()
    core = core_ref[0]
    outgoing = []
    for kind, out_ref in ((1, send_ref), (0, keep_ref)):
        start = 4 * (core ^ kind)
        for i in (0, 2):
            c = start + i
            column = jnp.concatenate([state[c], state[c + 1]], 1)
            end = column + product(high[...], low[...], column)
            for k in range(2):
                column = end[:, k * LANES : (k + 1) * LANES]
                state[c + k] = column
                rest = base[c + k] - column
                for q in range(4):
                    out_ref[4 * (i + k) + q] = rest[q * PART : (q + 1) * PART]
            pair = pl.ds(c, 2)
            outgoing.append(pltpu.make_async_copy(state.at[pair], end_ref.at[pair], sems.at[12 + kind * 2 + i // 2]))
            outgoing[-1].start()
    for copy in outgoing:
        copy.wait()


def pair_kernel(keep_ref, partner_ref, pair_ref, ready_ref):
    pair_ref[...] = keep_ref[...] + partner_ref[...]
    ready_ref[...] = jnp.zeros((8, LANES), F32)


def scan_kernel(in_ref, order_ref, out_ref):
    def block(index, carry):
        here = pl.ds(pl.multiple_of(index * 8, 8), 8)
        total = jnp.zeros((8, LANES), F32)
        for k in range(PARTS):
            out_ref[k, here, :] = total
            total = total + in_ref[k, here, :]
        return carry

    lax.fori_loop(0, PART // 8, block, 0)


def share_kernel(core_ref, before_ref, keep_ref, order_ref, out_ref):
    first = (core_ref[0] == 0).astype(F32)
    out_ref[...] = before_ref[...] + first * keep_ref[...]


def finish_kernel(core_ref, base_ref, before_ref, partner_ref, other_ref, out_ref, base, before, partner, other, out, sems, out_sems):
    core = core_ref[0]
    incoming = []
    for q in range(4):
        rows = pl.ds(q * PART, PART)
        incoming.append(
            [
                pltpu.make_async_copy(base_ref.at[:, rows], base.at[:, rows], sems.at[0, q]),
                pltpu.make_async_copy(before_ref.at[:, q], before.at[:, q], sems.at[1, q]),
                pltpu.make_async_copy(partner_ref.at[:, q], partner.at[:, q], sems.at[2, q]),
                pltpu.make_async_copy(other_ref.at[:, q], other.at[:, q], sems.at[3, q]),
            ]
        )
        for copy in incoming[q]:
            copy.start()
    flat = out.reshape(PAD * COLS, LANES)
    second = (core == 1).astype(F32)
    outgoing = []
    for q in range(4):
        for copy in incoming[q]:
            copy.wait()
        for c in range(COLS):
            i = c % 4
            own = before[i, q] + second * partner[i, q]
            earlier = jnp.where(core == c // 4, own, other[i, q])
            flat[pl.ds(q * PART * COLS + c, PART, stride=COLS), :] = (
                base[c, q * PART : (q + 1) * PART, :] + earlier
            )
        rows = pl.ds(q * PART, min(PART, ROWS - q * PART))
        outgoing.append(pltpu.make_async_copy(out.at[rows], out_ref.at[rows], out_sems.at[q]))
        outgoing[-1].start()
    for copy in outgoing:
        copy.wait()


def spread_of(place):
    return (lax.broadcasted_iota(jnp.int32, (CAP, SLOTS), 0) == place.astype(jnp.int32)).astype(F32)


def sort_kernel(index_ref, frac_ref, order_ref, out_ref, place_ref):
    column_x = index_ref[0]
    bucket = lax.broadcasted_iota(jnp.int32, (TILES, SLOTS), 0)
    chosen = (bucket == (column_x >> 3)).astype(F32)
    before = lax.broadcasted_iota(jnp.int32, (SLOTS, SLOTS), 0) < lax.broadcasted_iota(jnp.int32, (SLOTS, SLOTS), 1)
    rank = jnp.dot(chosen.astype(BF16), before.astype(F32).astype(BF16), preferred_element_type=F32)
    place = jnp.sum(chosen * rank, axis=0, keepdims=True)
    spread = spread_of(place)
    place_ref[:TILES] = chosen
    place_ref[TILES:] = jnp.broadcast_to(place, (TILES, SLOTS))
    values = jnp.concatenate(
        [
            (column_x & (COLS - 1)).astype(F32),
            index_ref[1].astype(F32),
            index_ref[2].astype(F32),
            frac_ref[0],
            frac_ref[1],
            jnp.zeros((FIELDS - 5, SLOTS), F32),
        ],
        0,
    )
    for j in range(TILES):
        masked = values * chosen[j : j + 1, :]
        out_ref[j] = lax.dot_general(
            masked, spread, (((1,), (1,)), ((), ())), precision=HIGHEST, preferred_element_type=F32
        )


def observe_kernel(me_ref, obs_ref, end_ref, order_ref, out_ref, end_high, end_low, end, sems):
    copies = [pltpu.make_async_copy(end_ref.at[c], end.at[c], sems.at[c]) for c in range(COLS)]
    for copy in copies:
        copy.start()
    for c in range(COLS):
        copies[c].wait()
        high, low = two_parts(end[c])
        end_high[:, c * LANES : (c + 1) * LANES] = high
        end_low[:, c * LANES : (c + 1) * LANES] = low
    lanes = 2 * CAP
    for j in range(0, TILES, 2):
        tiles = [(me_ref[0] - j - k + TILES) & (TILES - 1) for k in range(2)]
        fields = [jnp.concatenate([obs_ref[t, i : i + 1] for t in tiles], 1) for i in range(5)]
        column, line, row = [(f + 0.5).astype(jnp.int32) for f in fields[:3]]
        across, upward = fields[3:]
        y = lax.broadcasted_iota(jnp.int32, (LANES, lanes), 0)
        here, after = y == line, y == line + 1
        highs, lows = [], []
        for c in range(COLS):
            mine = column == c
            near = jnp.where(mine, 1.0 - across, 0.0)
            far = jnp.where(mine, across, 0.0)
            weight = jnp.where(here, near, jnp.where(after, far, 0.0))
            high, low = two_parts(weight)
            highs.append(high)
            lows.append(low)
        high, low = jnp.concatenate(highs, 0), jnp.concatenate(lows, 0)
        taken = jnp.dot(end_high[...], high, preferred_element_type=F32)
        taken = taken + jnp.dot(end_high[...], low, preferred_element_type=F32)
        taken = taken + jnp.dot(end_low[...], high, preferred_element_type=F32)
        r = lax.broadcasted_iota(jnp.int32, (PAD, lanes), 0)
        weight = jnp.where(r == row, 1.0 - upward, jnp.where(r == row + 1, upward, 0.0))
        value = jnp.sum(weight * taken, axis=0, keepdims=True)
        out_ref[j : j + 1, :] = value[:, :CAP]
        out_ref[j + 1 : j + 2, :] = value[:, CAP:]


def depart_kernel(count_ref, me_ref, back_ref, place_ref, value_ref, out_ref):
    spread = jnp.dot(
        back_ref[...], spread_of(place_ref[TILES : TILES + 1]), precision=HIGHEST, preferred_element_type=F32
    )
    evolved = jnp.zeros((1, SLOTS), F32)
    for j in range(TILES):
        tile = (me_ref[0] + j) & (TILES - 1)
        evolved = evolved + spread[j : j + 1] * place_ref[pl.ds(tile, 1)]
    live = lax.broadcasted_iota(jnp.int32, (1, SLOTS), 1) < count_ref[0, 0]
    out_ref[...] = jnp.where(live, value_ref[...] - evolved, 0.0)


def ring_step(blocks, by, offsets):
    size = blocks[0].shape[0]
    parcel = jnp.concatenate([blocks[o] for o in offsets], 0)
    parcel = lax.ppermute(parcel, "tile", [(i, (i + by) % TILES) for i in range(TILES)])
    return {o: parcel[at * size : (at + 1) * size] for at, o in enumerate(offsets)}


def give_back(found):
    blocks = {o: found[-o % TILES : -o % TILES + 1] for o in range(-4, 4)}
    for width, forward, backward in ((3, (2, 3), (-4, -3, -2)), (1, (-2, 1), (-4, -1, 2))):
        arrived = {**ring_step(blocks, width, forward), **ring_step(blocks, -width, backward)}
        blocks = {**blocks, **arrived}
    return jnp.concatenate([blocks[-j if j <= 4 else TILES - j] for j in range(TILES)], 0)


def per_device(
    increment, forcing, error_root, physics, coefficients, obs_index, obs_frac, obs_value, obs_count
):
    state = increment.reshape(ROWS, COLS, LANES)
    drive = forcing.reshape(ROWS, COLS, LANES)
    rates = coefficients.reshape(4, COLS, LANES)
    core = jnp.reshape(lax.axis_index("core"), (1,)).astype(jnp.int32)
    me = jnp.reshape(lax.axis_index("tile"), (1,)).astype(jnp.int32)
    field = PAD * COLS * LANES * 4

    to_west = [(i + 1, i) for i in range(TILES - 1)]
    to_east = [(i, i + 1) for i in range(TILES - 1)]

    west, east, sent = pack(state, rates)
    from_west = lax.ppermute(east, "tile", to_east)
    from_east = lax.ppermute(west, "tile", to_west)
    base, high, low, ready = call(
        prepare_kernel,
        [shape(COLS, PAD, LANES), shape(PAD, PAD, dtype=BF16), shape(PAD, PAD, dtype=BF16), shape(8, LANES)],
        (state, drive, error_root, physics.reshape(ROWS, ROWS), sent),
        scratch=[
            pltpu.VMEM((ROWS, COLS, LANES), F32),
            pltpu.VMEM((ROWS, COLS, LANES), F32),
            pltpu.VMEM((ROWS, ROWS), F32),
            pltpu.VMEM((PAD, PAD), F32),
            pltpu.VMEM((PAD, 2 * LANES), F32),
            pltpu.VMEM((COLS, PAD, LANES), F32),
            pltpu.VMEM((PAD, PAD), BF16),
            pltpu.VMEM((PAD, PAD), BF16),
            pltpu.SemaphoreType.DMA((9,)),
        ],
        flops=10**8,
        moved=10**6,
        far=(0, 1, 2),
        far_out=(0, 1, 2),
    )
    queries, places = call(
        sort_kernel,
        [shape(TILES, FIELDS, CAP), shape(2 * TILES, SLOTS)],
        (obs_index, obs_frac, ready),
        flops=10**7,
        moved=10**5,
    )
    arrived = lax.all_to_all(queries, "tile", 0, 0, tiled=True)
    parts = shape(PARTS, PART, LANES)
    wide = COLS + 2 * STEPS
    end, keep, send = call(
        advance_kernel,
        [shape(COLS, PAD, LANES), parts, parts],
        (state, rates, from_west, from_east, core, high, low, base, arrived),
        scratch=[
            pltpu.VMEM((4, COLS, LANES), F32),
            pltpu.VMEM((STEPS, 8, LANES), F32),
            pltpu.VMEM((STEPS, 8, LANES), F32),
            pltpu.VMEM((2 * wide, 8, LANES), F32),
            pltpu.VMEM((wide, 2 * LANES, 2 * LANES), BF16),
            pltpu.VMEM((PAD, COLS, LANES), F32),
            pltpu.VMEM((STEPS, PAD, LANES), F32),
            pltpu.VMEM((STEPS, PAD, LANES), F32),
            pltpu.VMEM((wide, HALF, LANES), F32),
            pltpu.VMEM((wide, HALF, LANES), F32),
            pltpu.VMEM((COLS, PAD, LANES), F32),
            pltpu.VMEM((COLS, PAD, LANES), F32),
            pltpu.VMEM((PAD, PAD), BF16),
            pltpu.VMEM((PAD, PAD), BF16),
            pltpu.SemaphoreType.DMA((16,)),
        ],
        flops=15 * 10**9,
        moved=6 * field,
        smem=(4,),
        far=(0, 1, 2, 3, 5, 6, 7, 8),
        far_out=(0,),
    )
    swap = [(0, 1), (1, 0)]
    partner = lax.ppermute(send, "core", swap)
    pair, paired = call(pair_kernel, [parts, shape(8, LANES)], (keep, partner), flops=10**6, moved=2 * field)
    gathered = lax.all_to_all(pair, ("y", "x"), 0, 0, tiled=True)
    found = call(
        observe_kernel,
        shape(TILES, CAP),
        (me, arrived, end, paired),
        scratch=[
            pltpu.VMEM((PAD, COLS * LANES), BF16),
            pltpu.VMEM((PAD, COLS * LANES), BF16),
            pltpu.VMEM((COLS, PAD, LANES), F32),
            pltpu.SemaphoreType.DMA((COLS,)),
        ],
        flops=3 * 10**9,
        moved=field,
        smem=(0,),
        far=(2,),
    )
    totals = call(scan_kernel, parts, (gathered, found), flops=10**7, moved=field)
    before = lax.all_to_all(totals, ("y", "x"), 0, 0, tiled=True)
    departure = call(
        depart_kernel,
        shape(1, SLOTS),
        (obs_count, me, give_back(found), places, obs_value),
        flops=10**7,
        moved=10**6,
        smem=(0, 1),
    )
    for_partner = call(
        share_kernel, parts, (core, before, keep, departure), flops=10**7, moved=2 * field, smem=(0,), far=(3,)
    )
    other = lax.ppermute(for_partner, "core", swap)
    fours = (4, 4, PART, LANES)
    summed = call(
        finish_kernel,
        shape(ROWS, COLS, LANES),
        (core, base, before.reshape(fours), partner.reshape(fours), other.reshape(fours)),
        scratch=[pltpu.VMEM((COLS, PAD, LANES), F32)]
        + [pltpu.VMEM(fours, F32)] * 3
        + [pltpu.VMEM((PAD, COLS, LANES), F32), pltpu.SemaphoreType.DMA((4, 4)), pltpu.SemaphoreType.DMA((4,))],
        flops=10**7,
        moved=4 * field,
        smem=(0,),
        far=(1, 2, 3, 4),
        far_out=(0,),
    )
    return summed.reshape(increment.shape), departure


def solution(mesh):
    split = Mesh(mesh.devices.reshape(GRID_Y, GRID_X, CORES, TILES), ("y", "x", "core", "tile"))
    win = ("y", "x", "core")
    return jax.shard_map(
        per_device,
        mesh=split,
        in_specs=(
            P(win, None, None, "tile", None),
            P(win, None, None, "tile", None),
            P(),
            P(win, None, None),
            P(win, None, "tile", None),
            P(None, win, "tile"),
            P(None, win, "tile"),
            P(win, "tile"),
            P(win, "tile"),
        ),
        out_specs=(P(win, None, None, "tile", None), P(win, "tile")),
        check_vma=False,
    )
```

```python
import jax
import jax.numpy as jnp
from jax import lax
from jax.experimental import pallas as pl
from jax.experimental.pallas import tpu as pltpu
from jax.sharding import Mesh, PartitionSpec as P

STEPS = 6
ROWS = 411
PAD = 416
COLS = 8
LANES = 128
GRID_Y = 4
GRID_X = 4
CORES = 2
PARTS = 16
PART = 104
TILES = 8
HALF = 208
SLOTS = 512
CAP = 128
FIELDS = 8

F32 = jnp.float32
BF16 = jnp.bfloat16
HIGHEST = lax.Precision.HIGHEST
MIB = 1 << 20
WIDE = 56


def call(body, outs, ins, scratch=(), flops=0, moved=0, smem=(), far=(), far_out=(), mib=WIDE):
    specs = [
        pl.BlockSpec(memory_space=pltpu.SMEM if at in smem else pl.ANY if at in far else pltpu.VMEM)
        for at in range(len(ins))
    ]
    many = isinstance(outs, (list, tuple))
    out_specs = [
        pl.BlockSpec(memory_space=pl.ANY if at in far_out else pltpu.VMEM)
        for at in range(len(outs) if many else 1)
    ]
    return pl.pallas_call(
        body,
        out_shape=outs,
        in_specs=specs,
        out_specs=out_specs if many else out_specs[0],
        scratch_shapes=list(scratch),
        compiler_params=pltpu.CompilerParams(vmem_limit_bytes=mib * MIB),
        cost_estimate=pl.CostEstimate(flops=flops, bytes_accessed=moved, transcendentals=0),
    )(*ins)


def shape(*dims, dtype=F32):
    return jax.ShapeDtypeStruct(dims, dtype)


def two_parts(value):
    high = value.astype(BF16)
    low = (value - high.astype(F32)).astype(BF16)
    return high, low


def product(left_high, left_low, right):
    high, low = two_parts(right)
    total = jnp.dot(left_high, high, preferred_element_type=F32)
    total = total + jnp.dot(left_high, low, preferred_element_type=F32)
    return total + jnp.dot(left_low, high, preferred_element_type=F32)


def pack_kernel(inc_ref, rate_ref, west_ref, east_ref, sent_ref, held, rates, west, east, in_sems, out_sems):
    count = PAD // PART
    incoming = [pltpu.make_async_copy(rate_ref, rates, in_sems.at[count])]
    for b in range(count):
        rows = pl.ds(b * PART, min(PART, ROWS - b * PART))
        incoming.append(pltpu.make_async_copy(inc_ref.at[rows], held.at[rows], in_sems.at[b]))
    for copy in incoming:
        copy.start()
    sent_ref[...] = jnp.zeros((8, LANES), F32)
    flat = held.reshape(PAD * COLS, LANES)
    outgoing = []
    incoming[0].wait()
    for b in range(count):
        incoming[b + 1].wait()
        size = min(PART, ROWS - b * PART)
        for c in range(COLS):
            column = flat[pl.ds(b * PART * COLS + c, size, stride=COLS), :]
            if size < PART:
                weights = [rates[i, c : c + 1, :] for i in range(4)]
                column = jnp.concatenate([column] + weights + [jnp.zeros((1, LANES), F32)], 0)
            if c < STEPS:
                west[c, b * PART : (b + 1) * PART, :] = column
            if c >= COLS - STEPS:
                east[c - COLS + STEPS, b * PART : (b + 1) * PART, :] = column
        rows = pl.ds(b * PART, PART)
        outgoing.append(pltpu.make_async_copy(west.at[:, rows], west_ref.at[:, rows], out_sems.at[2 * b]))
        outgoing.append(pltpu.make_async_copy(east.at[:, rows], east_ref.at[:, rows], out_sems.at[2 * b + 1]))
        outgoing[-2].start()
        outgoing[-1].start()
    for copy in outgoing:
        copy.wait()


def pack(state, rates):
    halo = shape(STEPS, PAD, LANES)
    return call(
        pack_kernel,
        [halo, halo, shape(8, LANES)],
        (state, rates),
        scratch=[
            pltpu.VMEM((PAD, COLS, LANES), F32),
            pltpu.VMEM((4, COLS, LANES), F32),
            pltpu.VMEM((STEPS, PAD, LANES), F32),
            pltpu.VMEM((STEPS, PAD, LANES), F32),
            pltpu.SemaphoreType.DMA((PAD // PART + 1,)),
            pltpu.SemaphoreType.DMA((2 * PAD // PART,)),
        ],
        moved=3 * PAD * COLS * LANES * 4,
        far=(0, 1),
        far_out=(0, 1),
    )


def prepare_kernel(
    inc_ref, forcing_ref, root_ref, physics_ref, order_ref, base_ref, high_ref, low_ref, ready_ref,
    start, force, root, square, drive, base, high, low, sems
):
    incoming = [
        pltpu.make_async_copy(root_ref, root, sems.at[0]),
        pltpu.make_async_copy(forcing_ref, force, sems.at[1]),
        pltpu.make_async_copy(inc_ref, start, sems.at[2]),
    ]
    for copy in incoming:
        copy.start()
    ready_ref[...] = jnp.zeros((8, LANES), F32)
    square[...] = jnp.zeros((PAD, PAD), F32)
    square[:ROWS, :ROWS] = 0.2 * physics_ref[...]
    once = square[...]
    twice = 2.0 * once + product(*two_parts(once), once)
    twice_parts = two_parts(twice)
    four = 2.0 * twice + product(*twice_parts, twice)
    six = twice + four + product(*twice_parts, four)
    high[...], low[...] = two_parts(six)
    outgoing = [
        pltpu.make_async_copy(high, high_ref, sems.at[3]),
        pltpu.make_async_copy(low, low_ref, sems.at[4]),
    ]
    for copy in outgoing:
        copy.start()
    for copy in incoming:
        copy.wait()
    square[:ROWS, :ROWS] = root[...]
    root_high, root_low = two_parts(square[...])
    force_flat = force.reshape(ROWS * COLS, LANES)
    start_flat = start.reshape(ROWS * COLS, LANES)
    drive[ROWS - 3 :, :] = jnp.zeros((PAD - ROWS + 3, 2 * LANES), F32)
    for c in range(0, COLS, 2):
        drive[:ROWS, :LANES] = force_flat[pl.ds(c, ROWS, stride=COLS), :]
        drive[:ROWS, LANES:] = force_flat[pl.ds(c + 1, ROWS, stride=COLS), :]
        forced = product(root_high, root_low, drive[...])
        for k in range(2):
            column = forced[:, k * LANES : (k + 1) * LANES]
            base[c + k, :ROWS, :] = start_flat[pl.ds(c + k, ROWS, stride=COLS), :] - column[:ROWS]
            base[c + k, ROWS:, :] = column[ROWS:]
        pair = pl.ds(c, 2)
        outgoing.append(pltpu.make_async_copy(base.at[pair], base_ref.at[pair], sems.at[5 + c // 2]))
        outgoing[-1].start()
    for copy in outgoing:
        copy.wait()


def rotated(j):
    return j % 5 in (0, 2)


def advance_kernel(
    inc_ref, rate_ref, west_ref, east_ref, core_ref, high_ref, low_ref, base_ref, order_ref,
    end_ref, keep_ref, send_ref,
    rate, west_rate, east_rate, table, band, own, west, east, odd, even, state, base, high, low, split, sems
):
    at = PAD - 8
    weights = [
        pltpu.make_async_copy(rate_ref, rate, sems.at[0]),
        pltpu.make_async_copy(west_ref.at[:, pl.ds(at, 8)], west_rate, sems.at[1]),
        pltpu.make_async_copy(east_ref.at[:, pl.ds(at, 8)], east_rate, sems.at[2]),
    ]
    fields = []
    for b in range(2):
        valid = min(HALF, ROWS - b * HALF)
        rows = pl.ds(b * HALF, HALF)
        mine = pl.ds(b * HALF, valid)
        fields.append(pltpu.make_async_copy(inc_ref.at[mine], own.at[mine], sems.at[3 + 3 * b]))
        fields.append(pltpu.make_async_copy(west_ref.at[:, rows], west.at[:, rows], sems.at[4 + 3 * b]))
        fields.append(pltpu.make_async_copy(east_ref.at[:, rows], east.at[:, rows], sems.at[5 + 3 * b]))
    later = [
        pltpu.make_async_copy(high_ref, high, sems.at[9]),
        pltpu.make_async_copy(low_ref, low, sems.at[10]),
        pltpu.make_async_copy(base_ref, base, sems.at[11]),
    ]
    for copy in weights + fields + later:
        copy.start()
    own[ROWS:] = jnp.zeros((PAD - ROWS, COLS, LANES), F32)
    for copy in weights:
        copy.wait()
    row = lax.broadcasted_iota(jnp.int32, (LANES, LANES), 0)
    lane = lax.broadcasted_iota(jnp.int32, (LANES, LANES), 1)
    wide = COLS + 2 * STEPS
    first = ROWS - at
    for j in range(1, wide - 1):
        if j < STEPS:
            rates = [west_rate[j, first + i : first + i + 1, :] for i in range(4)]
        elif j < STEPS + COLS:
            rates = [rate[i, j - STEPS : j - STEPS + 1, :] for i in range(4)]
        else:
            rates = [east_rate[j - STEPS - COLS, first + i : first + i + 1, :] for i in range(4)]
        center = 1.0 - (rates[0] + rates[1] + rates[2] + rates[3])
        table[5 * j] = jnp.broadcast_to(rates[0], (8, LANES))
        table[5 * j + 1] = jnp.broadcast_to(rates[1], (8, LANES))
        if rotated(j):
            table[5 * j + 2] = jnp.broadcast_to(center, (8, LANES))
            table[5 * j + 3] = jnp.broadcast_to(jnp.where(lane[:1] == LANES - 1, 0.0, rates[2]), (8, LANES))
            table[5 * j + 4] = jnp.broadcast_to(jnp.where(lane[:1] == 0, 0.0, rates[3]), (8, LANES))
            continue
        along = jnp.where(row == lane, center, 0.0)
        along = jnp.where(row == lane + 1, rates[2], along)
        along = jnp.where(row == lane - 1, rates[3], along)
        along_high, along_low = two_parts(along)
        band[j, :LANES, :LANES] = along_high
        band[j, LANES:, :LANES] = along_high
        band[j, :LANES, LANES:] = along_low
        band[j, LANES:, LANES:] = jnp.zeros((LANES, LANES), BF16)
    flat = own.reshape(PAD * COLS, LANES)

    for copy in fields[:3]:
        copy.wait()

    def block(b, carry):
        rows = pl.ds(pl.multiple_of(b * HALF, 16), HALF)

        @pl.when(b == 1)
        def _():
            for copy in fields[3:]:
                copy.wait()

        def load(step, j):
            if step > 0:
                return (odd if step % 2 else even)[j]
            if j < STEPS:
                return west[j, rows, :]
            if j < STEPS + COLS:
                return flat[pl.ds(b * (HALF * COLS) + j - STEPS, HALF, stride=COLS), :]
            return east[j - STEPS - COLS, rows, :]

        def tiles(value):
            return value.reshape(HALF // 8, 8, LANES)

        for step in range(1, STEPS + 1):
            for j in range(step, wide - step):
                value = load(step - 1, j)
                if rotated(j):
                    value = tiles(value)
                    total = table[5 * j + 2] * value
                    total = total + table[5 * j + 3] * pltpu.roll(value, LANES - 1, 2)
                    total = total + table[5 * j + 4] * pltpu.roll(value, 1, 2)
                else:
                    parts = jnp.concatenate(two_parts(value), 1)
                    along = jnp.dot(parts, band[j], preferred_element_type=F32)
                    total = tiles(along[:, :LANES] + along[:, LANES:])
                total = total + table[5 * j] * tiles(load(step - 1, j + 1))
                total = total + table[5 * j + 1] * tiles(load(step - 1, j - 1))
                total = total.reshape(HALF, LANES)
                if step == STEPS:
                    state[j - STEPS, rows, :] = total
                else:
                    (odd if step % 2 else even)[j] = total
        return carry

    lax.fori_loop(0, 2, block, 0)

    for copy in later:
        copy.wait()
    core = core_ref[0]
    outgoing = []
    for kind, out_ref in ((1, send_ref), (0, keep_ref)):
        start = 4 * (core ^ kind)
        for i in (0, 2):
            c = start + i
            column = jnp.concatenate([state[c], state[c + 1]], 1)
            end = column + product(high[...], low[...], column)
            for k in range(2):
                column = end[:, k * LANES : (k + 1) * LANES]
                state[c + k] = column
                rest = base[c + k] - column
                for q in range(4):
                    split[kind, 4 * (i + k) + q] = rest[q * PART : (q + 1) * PART]
            pair, some = pl.ds(c, 2), pl.ds(4 * i, 8)
            outgoing.append(pltpu.make_async_copy(split.at[kind, some], out_ref.at[some], sems.at[16 + kind * 2 + i // 2]))
            outgoing[-1].start()
            outgoing.append(pltpu.make_async_copy(state.at[pair], end_ref.at[pair], sems.at[12 + kind * 2 + i // 2]))
            outgoing[-1].start()
    for copy in outgoing:
        copy.wait()


def pair_kernel(keep_ref, partner_ref, pair_ref, ready_ref):
    pair_ref[...] = keep_ref[...] + partner_ref[...]
    ready_ref[...] = jnp.zeros((8, LANES), F32)


def scan_kernel(in_ref, order_ref, out_ref):
    def block(index, carry):
        here = pl.ds(pl.multiple_of(index * 8, 8), 8)
        total = jnp.zeros((8, LANES), F32)
        for k in range(PARTS):
            out_ref[k, here, :] = total
            total = total + in_ref[k, here, :]
        return carry

    lax.fori_loop(0, PART // 8, block, 0)


def share_kernel(core_ref, before_ref, keep_ref, order_ref, out_ref):
    first = (core_ref[0] == 0).astype(F32)
    out_ref[...] = before_ref[...] + first * keep_ref[...]


def finish_kernel(core_ref, base_ref, before_ref, partner_ref, other_ref, out_ref, out, sems):
    core = core_ref[0]
    flat = out.reshape(PAD * COLS, LANES)
    second = (core == 1).astype(F32)
    outgoing = []
    for q in range(4):
        for c in range(COLS):
            at = 4 * (c % 4) + q
            own = before_ref[at] + second * partner_ref[at]
            earlier = jnp.where(core == c // 4, own, other_ref[at])
            flat[pl.ds(q * PART * COLS + c, PART, stride=COLS), :] = (
                base_ref[c, q * PART : (q + 1) * PART, :] + earlier
            )
        rows = pl.ds(q * PART, min(PART, ROWS - q * PART))
        outgoing.append(pltpu.make_async_copy(out.at[rows], out_ref.at[rows], sems.at[q]))
        outgoing[-1].start()
    for copy in outgoing:
        copy.wait()


def spread_of(place):
    return (lax.broadcasted_iota(jnp.int32, (CAP, SLOTS), 0) == place.astype(jnp.int32)).astype(F32)


def sort_kernel(index_ref, frac_ref, order_ref, out_ref, place_ref):
    column_x = index_ref[0]
    bucket = lax.broadcasted_iota(jnp.int32, (TILES, SLOTS), 0)
    chosen = (bucket == (column_x >> 3)).astype(F32)
    before = lax.broadcasted_iota(jnp.int32, (SLOTS, SLOTS), 0) < lax.broadcasted_iota(jnp.int32, (SLOTS, SLOTS), 1)
    rank = jnp.dot(chosen.astype(BF16), before.astype(F32).astype(BF16), preferred_element_type=F32)
    place = jnp.sum(chosen * rank, axis=0, keepdims=True)
    spread = spread_of(place)
    place_ref[:TILES] = chosen
    place_ref[TILES:] = jnp.broadcast_to(place, (TILES, SLOTS))
    values = jnp.concatenate(
        [
            (column_x & (COLS - 1)).astype(F32),
            index_ref[1].astype(F32),
            index_ref[2].astype(F32),
            frac_ref[0],
            frac_ref[1],
            jnp.zeros((FIELDS - 5, SLOTS), F32),
        ],
        0,
    )
    for j in range(TILES):
        masked = values * chosen[j : j + 1, :]
        out_ref[j] = lax.dot_general(
            masked, spread, (((1,), (1,)), ((), ())), precision=HIGHEST, preferred_element_type=F32
        )


def observe_kernel(me_ref, obs_ref, end_ref, order_ref, out_ref, end_high, end_low):
    for c in range(COLS):
        high, low = two_parts(end_ref[c])
        end_high[:, c * LANES : (c + 1) * LANES] = high
        end_low[:, c * LANES : (c + 1) * LANES] = low
    lanes = 2 * CAP
    for j in range(0, TILES, 2):
        tiles = [(me_ref[0] - j - k + TILES) & (TILES - 1) for k in range(2)]
        fields = [jnp.concatenate([obs_ref[t, i : i + 1] for t in tiles], 1) for i in range(5)]
        column, line, row = [(f + 0.5).astype(jnp.int32) for f in fields[:3]]
        across, upward = fields[3:]
        y = lax.broadcasted_iota(jnp.int32, (LANES, lanes), 0)
        here, after = y == line, y == line + 1
        highs, lows = [], []
        for c in range(COLS):
            mine = column == c
            near = jnp.where(mine, 1.0 - across, 0.0)
            far = jnp.where(mine, across, 0.0)
            weight = jnp.where(here, near, jnp.where(after, far, 0.0))
            high, low = two_parts(weight)
            highs.append(high)
            lows.append(low)
        high, low = jnp.concatenate(highs, 0), jnp.concatenate(lows, 0)
        taken = jnp.dot(end_high[...], high, preferred_element_type=F32)
        taken = taken + jnp.dot(end_high[...], low, preferred_element_type=F32)
        taken = taken + jnp.dot(end_low[...], high, preferred_element_type=F32)
        r = lax.broadcasted_iota(jnp.int32, (PAD, lanes), 0)
        weight = jnp.where(r == row, 1.0 - upward, jnp.where(r == row + 1, upward, 0.0))
        value = jnp.sum(weight * taken, axis=0, keepdims=True)
        out_ref[j : j + 1, :] = value[:, :CAP]
        out_ref[j + 1 : j + 2, :] = value[:, CAP:]


def depart_kernel(count_ref, me_ref, back_ref, place_ref, value_ref, out_ref, ready_ref):
    ready_ref[...] = jnp.zeros((8, LANES), F32)
    spread = jnp.dot(
        back_ref[...], spread_of(place_ref[TILES : TILES + 1]), precision=HIGHEST, preferred_element_type=F32
    )
    evolved = jnp.zeros((1, SLOTS), F32)
    for j in range(TILES):
        tile = (me_ref[0] + j) & (TILES - 1)
        evolved = evolved + spread[j : j + 1] * place_ref[pl.ds(tile, 1)]
    live = lax.broadcasted_iota(jnp.int32, (1, SLOTS), 1) < count_ref[0, 0]
    out_ref[...] = jnp.where(live, value_ref[...] - evolved, 0.0)


def ring_step(blocks, by, offsets):
    size = blocks[0].shape[0]
    parcel = jnp.concatenate([blocks[o] for o in offsets], 0)
    parcel = lax.ppermute(parcel, "tile", [(i, (i + by) % TILES) for i in range(TILES)])
    return {o: parcel[at * size : (at + 1) * size] for at, o in enumerate(offsets)}


def give_back(found):
    blocks = {o: found[-o % TILES : -o % TILES + 1] for o in range(-4, 4)}
    for width, forward, backward in ((3, (2, 3), (-4, -3, -2)), (1, (-2, 1), (-4, -1, 2))):
        arrived = {**ring_step(blocks, width, forward), **ring_step(blocks, -width, backward)}
        blocks = {**blocks, **arrived}
    return jnp.concatenate([blocks[-j if j <= 4 else TILES - j] for j in range(TILES)], 0)


def per_device(
    increment, forcing, error_root, physics, coefficients, obs_index, obs_frac, obs_value, obs_count
):
    state = increment.reshape(ROWS, COLS, LANES)
    drive = forcing.reshape(ROWS, COLS, LANES)
    rates = coefficients.reshape(4, COLS, LANES)
    core = jnp.reshape(lax.axis_index("core"), (1,)).astype(jnp.int32)
    me = jnp.reshape(lax.axis_index("tile"), (1,)).astype(jnp.int32)
    field = PAD * COLS * LANES * 4

    to_west = [(i + 1, i) for i in range(TILES - 1)]
    to_east = [(i, i + 1) for i in range(TILES - 1)]

    west, east, sent = pack(state, rates)
    from_west = lax.ppermute(east, "tile", to_east)
    from_east = lax.ppermute(west, "tile", to_west)
    base, high, low, ready = call(
        prepare_kernel,
        [shape(COLS, PAD, LANES), shape(PAD, PAD, dtype=BF16), shape(PAD, PAD, dtype=BF16), shape(8, LANES)],
        (state, drive, error_root, physics.reshape(ROWS, ROWS), sent),
        scratch=[
            pltpu.VMEM((ROWS, COLS, LANES), F32),
            pltpu.VMEM((ROWS, COLS, LANES), F32),
            pltpu.VMEM((ROWS, ROWS), F32),
            pltpu.VMEM((PAD, PAD), F32),
            pltpu.VMEM((PAD, 2 * LANES), F32),
            pltpu.VMEM((COLS, PAD, LANES), F32),
            pltpu.VMEM((PAD, PAD), BF16),
            pltpu.VMEM((PAD, PAD), BF16),
            pltpu.SemaphoreType.DMA((9,)),
        ],
        flops=10**8,
        moved=10**6,
        far=(0, 1, 2),
        far_out=(0, 1, 2),
    )
    queries, places = call(
        sort_kernel,
        [shape(TILES, FIELDS, CAP), shape(2 * TILES, SLOTS)],
        (obs_index, obs_frac, ready),
        flops=10**7,
        moved=10**5,
        mib=8,
    )
    arrived = lax.all_to_all(queries, "tile", 0, 0, tiled=True)
    parts = shape(PARTS, PART, LANES)
    wide = COLS + 2 * STEPS
    end, keep, send = call(
        advance_kernel,
        [shape(COLS, PAD, LANES), parts, parts],
        (state, rates, from_west, from_east, core, high, low, base, arrived),
        scratch=[
            pltpu.VMEM((4, COLS, LANES), F32),
            pltpu.VMEM((STEPS, 8, LANES), F32),
            pltpu.VMEM((STEPS, 8, LANES), F32),
            pltpu.VMEM((5 * wide, 8, LANES), F32),
            pltpu.VMEM((wide, 2 * LANES, 2 * LANES), BF16),
            pltpu.VMEM((PAD, COLS, LANES), F32),
            pltpu.VMEM((STEPS, PAD, LANES), F32),
            pltpu.VMEM((STEPS, PAD, LANES), F32),
            pltpu.VMEM((wide, HALF, LANES), F32),
            pltpu.VMEM((wide, HALF, LANES), F32),
            pltpu.VMEM((COLS, PAD, LANES), F32),
            pltpu.VMEM((COLS, PAD, LANES), F32),
            pltpu.VMEM((PAD, PAD), BF16),
            pltpu.VMEM((PAD, PAD), BF16),
            pltpu.VMEM((2, PARTS, PART, LANES), F32),
            pltpu.SemaphoreType.DMA((20,)),
        ],
        flops=15 * 10**9,
        moved=6 * field,
        smem=(4,),
        far=(0, 1, 2, 3, 5, 6, 7, 8),
        far_out=range(3),
    )
    swap = [(0, 1), (1, 0)]
    partner = lax.ppermute(send, "core", swap)
    pair, paired = call(pair_kernel, [parts, shape(8, LANES)], (keep, partner), flops=10**6, moved=2 * field, mib=6)
    gathered = lax.all_to_all(pair, ("y", "x"), 0, 0, tiled=True)
    found = call(
        observe_kernel,
        shape(TILES, CAP),
        (me, arrived, end, paired),
        scratch=[
            pltpu.VMEM((PAD, COLS * LANES), BF16),
            pltpu.VMEM((PAD, COLS * LANES), BF16),
        ],
        flops=3 * 10**9,
        moved=field,
        smem=(0,),
        mib=10,
    )
    totals = call(scan_kernel, parts, (gathered, found), flops=10**7, moved=field, mib=6)
    before = lax.all_to_all(totals, ("y", "x"), 0, 0, tiled=True)
    departure, departed = call(
        depart_kernel,
        [shape(1, SLOTS), shape(8, LANES)],
        (obs_count, me, give_back(found), places, obs_value),
        flops=10**7,
        moved=10**6,
        smem=(0, 1),
        mib=4,
    )
    for_partner = call(
        share_kernel, parts, (core, before, keep, departed), flops=10**7, moved=2 * field, smem=(0,), mib=6
    )
    other = lax.ppermute(for_partner, "core", swap)
    summed = call(
        finish_kernel,
        shape(ROWS, COLS, LANES),
        (core, base, before, partner, other),
        scratch=[pltpu.VMEM((PAD, COLS, LANES), F32), pltpu.SemaphoreType.DMA((4,))],
        flops=10**7,
        moved=4 * field,
        smem=(0,),
        far_out=(0,),
        mib=10,
    )
    return summed.reshape(increment.shape), departure


def solution(mesh):
    split = Mesh(mesh.devices.reshape(GRID_Y, GRID_X, CORES, TILES), ("y", "x", "core", "tile"))
    win = ("y", "x", "core")
    return jax.shard_map(
        per_device,
        mesh=split,
        in_specs=(
            P(win, None, None, "tile", None),
            P(win, None, None, "tile", None),
            P(),
            P(win, None, None),
            P(win, None, "tile", None),
            P(None, win, "tile"),
            P(None, win, "tile"),
            P(win, "tile"),
            P(win, "tile"),
        ),
        out_specs=(P(win, None, None, "tile", None), P(win, "tile")),
        check_vma=False,
    )
```

```python
import jax
import jax.numpy as jnp
from jax import lax
from jax.experimental import pallas as pl
from jax.experimental.pallas import tpu as pltpu
from jax.sharding import Mesh, PartitionSpec as P

STEPS = 6
ROWS = 411
PAD = 416
COLS = 8
LANES = 128
GRID_Y = 4
GRID_X = 4
CORES = 2
PARTS = 16
PART = 104
TILES = 8
HALF = 208
SLOTS = 512
CAP = 128
FIELDS = 8

F32 = jnp.float32
BF16 = jnp.bfloat16
HIGHEST = lax.Precision.HIGHEST
MIB = 1 << 20
WIDE = 56


def call(body, outs, ins, scratch=(), flops=0, moved=0, smem=(), far=(), far_out=(), mib=WIDE):
    specs = [
        pl.BlockSpec(memory_space=pltpu.SMEM if at in smem else pl.ANY if at in far else pltpu.VMEM)
        for at in range(len(ins))
    ]
    many = isinstance(outs, (list, tuple))
    out_specs = [
        pl.BlockSpec(memory_space=pl.ANY if at in far_out else pltpu.VMEM)
        for at in range(len(outs) if many else 1)
    ]
    return pl.pallas_call(
        body,
        out_shape=outs,
        in_specs=specs,
        out_specs=out_specs if many else out_specs[0],
        scratch_shapes=list(scratch),
        compiler_params=pltpu.CompilerParams(vmem_limit_bytes=mib * MIB),
        cost_estimate=pl.CostEstimate(flops=flops, bytes_accessed=moved, transcendentals=0),
    )(*ins)


def shape(*dims, dtype=F32):
    return jax.ShapeDtypeStruct(dims, dtype)


def two_parts(value):
    high = value.astype(BF16)
    low = (value - high.astype(F32)).astype(BF16)
    return high, low


def product(left_high, left_low, right):
    high, low = two_parts(right)
    total = jnp.dot(left_high, high, preferred_element_type=F32)
    total = total + jnp.dot(left_high, low, preferred_element_type=F32)
    return total + jnp.dot(left_low, high, preferred_element_type=F32)


def pack_kernel(inc_ref, rate_ref, west0_ref, east0_ref, west1_ref, east1_ref, sent_ref, held, rates, west, east, in_sems, out_sems):
    count = PAD // PART
    incoming = [pltpu.make_async_copy(rate_ref, rates, in_sems.at[count])]
    for b in range(count):
        rows = pl.ds(b * PART, min(PART, ROWS - b * PART))
        incoming.append(pltpu.make_async_copy(inc_ref.at[rows], held.at[rows], in_sems.at[b]))
    for copy in incoming:
        copy.start()
    sent_ref[...] = jnp.zeros((8, LANES), F32)
    flat = held.reshape(PAD * COLS, LANES)
    held[ROWS:] = jnp.zeros((PAD - ROWS, COLS, LANES), F32)
    outgoing = []
    incoming[0].wait()
    for half, (west_ref, east_ref) in enumerate(((west0_ref, east0_ref), (west1_ref, east1_ref))):
        for b in (2 * half, 2 * half + 1):
            incoming[b + 1].wait()
            rows = slice(b * PART, (b + 1) * PART)
            for c in range(COLS):
                column = flat[pl.ds(b * PART * COLS + c, PART, stride=COLS), :]
                if c < STEPS:
                    west[c, rows, :] = column
                if c >= COLS - STEPS:
                    east[c - COLS + STEPS, rows, :] = column
        if half == 0:
            for c in range(COLS):
                weights = [rates[i, c : c + 1, :] for i in range(4)]
                weights = jnp.concatenate(weights + [jnp.zeros((4, LANES), F32)], 0)
                if c < STEPS:
                    west[c, PAD:, :] = weights
                if c >= COLS - STEPS:
                    east[c - COLS + STEPS, PAD:, :] = weights
        for at, (held_side, side_ref) in enumerate(((west, west_ref), (east, east_ref))):
            mine = pl.ds(half * HALF, HALF)
            outgoing.append(
                pltpu.make_async_copy(held_side.at[:, mine], side_ref.at[:, pl.ds(0, HALF)], out_sems.at[4 * half + at])
            )
            outgoing[-1].start()
            if half == 0:
                outgoing.append(
                    pltpu.make_async_copy(
                        held_side.at[:, pl.ds(PAD, 8)], side_ref.at[:, pl.ds(HALF, 8)], out_sems.at[2 + at]
                    )
                )
                outgoing[-1].start()
    for copy in outgoing:
        copy.wait()


def pack(state, rates):
    first, second = shape(STEPS, HALF + 8, LANES), shape(STEPS, HALF, LANES)
    return call(
        pack_kernel,
        [first, first, second, second, shape(8, LANES)],
        (state, rates),
        scratch=[
            pltpu.VMEM((PAD, COLS, LANES), F32),
            pltpu.VMEM((4, COLS, LANES), F32),
            pltpu.VMEM((STEPS, PAD + 8, LANES), F32),
            pltpu.VMEM((STEPS, PAD + 8, LANES), F32),
            pltpu.SemaphoreType.DMA((PAD // PART + 1,)),
            pltpu.SemaphoreType.DMA((6,)),
        ],
        moved=3 * PAD * COLS * LANES * 4,
        far=(0, 1),
        far_out=range(4),
    )


def prepare_kernel(
    inc_ref, forcing_ref, root_ref, physics_ref, order_ref, base_ref, high_ref, low_ref, ready_ref,
    start, force, root, square, drive, base, high, low, sems
):
    incoming = [
        pltpu.make_async_copy(root_ref, root, sems.at[0]),
        pltpu.make_async_copy(forcing_ref, force, sems.at[1]),
        pltpu.make_async_copy(inc_ref, start, sems.at[2]),
    ]
    for copy in incoming:
        copy.start()
    ready_ref[...] = jnp.zeros((8, LANES), F32)
    square[...] = jnp.zeros((PAD, PAD), F32)
    square[:ROWS, :ROWS] = 0.2 * physics_ref[...]
    once = square[...]
    twice = 2.0 * once + product(*two_parts(once), once)
    twice_parts = two_parts(twice)
    four = 2.0 * twice + product(*twice_parts, twice)
    six = twice + four + product(*twice_parts, four)
    high[...], low[...] = two_parts(six)
    outgoing = [
        pltpu.make_async_copy(high, high_ref, sems.at[3]),
        pltpu.make_async_copy(low, low_ref, sems.at[4]),
    ]
    for copy in outgoing:
        copy.start()
    for copy in incoming:
        copy.wait()
    square[:ROWS, :ROWS] = root[...]
    root_high, root_low = two_parts(square[...])
    force_flat = force.reshape(ROWS * COLS, LANES)
    start_flat = start.reshape(ROWS * COLS, LANES)
    drive[ROWS - 3 :, :] = jnp.zeros((PAD - ROWS + 3, 2 * LANES), F32)
    for c in range(0, COLS, 2):
        drive[:ROWS, :LANES] = force_flat[pl.ds(c, ROWS, stride=COLS), :]
        drive[:ROWS, LANES:] = force_flat[pl.ds(c + 1, ROWS, stride=COLS), :]
        forced = product(root_high, root_low, drive[...])
        for k in range(2):
            column = forced[:, k * LANES : (k + 1) * LANES]
            base[c + k, :ROWS, :] = start_flat[pl.ds(c + k, ROWS, stride=COLS), :] - column[:ROWS]
            base[c + k, ROWS:, :] = column[ROWS:]
        pair = pl.ds(c, 2)
        outgoing.append(pltpu.make_async_copy(base.at[pair], base_ref.at[pair], sems.at[5 + c // 2]))
        outgoing[-1].start()
    for copy in outgoing:
        copy.wait()


def rotated(j):
    return j % 5 in (0, 2)


def transport(half, refs, scratch, out, later=()):
    inc_ref, rate_ref, west_ref, east_ref, west_rate_ref, east_rate_ref = refs
    rate, west_rate, east_rate, table, band, own, west, east, odd, even, sems = scratch
    valid = min(HALF, ROWS - half * HALF)
    weights = [
        pltpu.make_async_copy(rate_ref, rate, sems.at[0]),
        pltpu.make_async_copy(west_rate_ref.at[:, pl.ds(HALF, 8)], west_rate, sems.at[1]),
        pltpu.make_async_copy(east_rate_ref.at[:, pl.ds(HALF, 8)], east_rate, sems.at[2]),
    ]
    rows = pl.ds(0, HALF)
    fields = [
        pltpu.make_async_copy(inc_ref.at[pl.ds(half * HALF, valid)], own.at[pl.ds(0, valid)], sems.at[3]),
        pltpu.make_async_copy(west_ref.at[:, rows], west, sems.at[4]),
        pltpu.make_async_copy(east_ref.at[:, rows], east, sems.at[5]),
    ]
    for copy in weights + fields + list(later):
        copy.start()
    if valid < HALF:
        own[valid:] = jnp.zeros((HALF - valid, COLS, LANES), F32)
    for copy in weights:
        copy.wait()
    row = lax.broadcasted_iota(jnp.int32, (LANES, LANES), 0)
    lane = lax.broadcasted_iota(jnp.int32, (LANES, LANES), 1)
    wide = COLS + 2 * STEPS
    for j in range(1, wide - 1):
        if j < STEPS:
            rates = [west_rate[j, i : i + 1, :] for i in range(4)]
        elif j < STEPS + COLS:
            rates = [rate[i, j - STEPS : j - STEPS + 1, :] for i in range(4)]
        else:
            rates = [east_rate[j - STEPS - COLS, i : i + 1, :] for i in range(4)]
        center = 1.0 - (rates[0] + rates[1] + rates[2] + rates[3])
        table[5 * j] = jnp.broadcast_to(rates[0], (8, LANES))
        table[5 * j + 1] = jnp.broadcast_to(rates[1], (8, LANES))
        if rotated(j):
            table[5 * j + 2] = jnp.broadcast_to(center, (8, LANES))
            table[5 * j + 3] = jnp.broadcast_to(jnp.where(lane[:1] == LANES - 1, 0.0, rates[2]), (8, LANES))
            table[5 * j + 4] = jnp.broadcast_to(jnp.where(lane[:1] == 0, 0.0, rates[3]), (8, LANES))
            continue
        along = jnp.where(row == lane, center, 0.0)
        along = jnp.where(row == lane + 1, rates[2], along)
        along = jnp.where(row == lane - 1, rates[3], along)
        along_high, along_low = two_parts(along)
        band[j, :LANES, :LANES] = along_high
        band[j, LANES:, :LANES] = along_high
        band[j, :LANES, LANES:] = along_low
        band[j, LANES:, LANES:] = jnp.zeros((LANES, LANES), BF16)
    flat = own.reshape(HALF * COLS, LANES)
    for copy in fields:
        copy.wait()

    def load(step, j):
        if step > 0:
            return (odd if step % 2 else even)[j]
        if j < STEPS:
            return west[j]
        if j < STEPS + COLS:
            return flat[pl.ds(j - STEPS, HALF, stride=COLS), :]
        return east[j - STEPS - COLS]

    def tiles(value):
        return value.reshape(HALF // 8, 8, LANES)

    for step in range(1, STEPS + 1):
        for j in range(step, wide - step):
            value = load(step - 1, j)
            if rotated(j):
                value = tiles(value)
                total = table[5 * j + 2] * value
                total = total + table[5 * j + 3] * pltpu.roll(value, LANES - 1, 2)
                total = total + table[5 * j + 4] * pltpu.roll(value, 1, 2)
            else:
                parts = jnp.concatenate(two_parts(value), 1)
                along = jnp.dot(parts, band[j], preferred_element_type=F32)
                total = tiles(along[:, :LANES] + along[:, LANES:])
            total = total + table[5 * j] * tiles(load(step - 1, j + 1))
            total = total + table[5 * j + 1] * tiles(load(step - 1, j - 1))
            total = total.reshape(HALF, LANES)
            if step == STEPS:
                out[j - STEPS] = total
            else:
                (odd if step % 2 else even)[j] = total


def transport_scratch():
    wide = COLS + 2 * STEPS
    return [
        pltpu.VMEM((4, COLS, LANES), F32),
        pltpu.VMEM((STEPS, 8, LANES), F32),
        pltpu.VMEM((STEPS, 8, LANES), F32),
        pltpu.VMEM((5 * wide, 8, LANES), F32),
        pltpu.VMEM((wide, 2 * LANES, 2 * LANES), BF16),
        pltpu.VMEM((HALF, COLS, LANES), F32),
        pltpu.VMEM((STEPS, HALF, LANES), F32),
        pltpu.VMEM((STEPS, HALF, LANES), F32),
        pltpu.VMEM((wide, HALF, LANES), F32),
        pltpu.VMEM((wide, HALF, LANES), F32),
        pltpu.SemaphoreType.DMA((6,)),
    ]


def upper_kernel(*refs):
    ins, (order_ref, out_ref, ready_ref, out, sem), scratch = refs[:6], refs[6:11], refs[11:]
    ready_ref[...] = jnp.zeros((8, LANES), F32)
    transport(0, ins, scratch, out)
    copy = pltpu.make_async_copy(out, out_ref, sem)
    copy.start()
    copy.wait()


def advance_kernel(*refs):
    ins, (core_ref, upper_ref, high_ref, low_ref, base_ref, order_ref) = refs[:6], refs[6:12]
    end_ref, keep_ref, send_ref, upper, lower, base, high, low, split, sems = refs[12:22]
    later = [
        pltpu.make_async_copy(high_ref, high, sems.at[0]),
        pltpu.make_async_copy(low_ref, low, sems.at[1]),
        pltpu.make_async_copy(upper_ref, upper, sems.at[2]),
        pltpu.make_async_copy(base_ref, base, sems.at[3]),
    ]
    transport(1, ins, refs[22:], lower, later)
    for copy in later:
        copy.wait()
    core = core_ref[0]
    outgoing = []
    for kind, out_ref in ((1, send_ref), (0, keep_ref)):
        start = 4 * (core ^ kind)
        for i in (0, 2):
            c = start + i
            column = jnp.concatenate([jnp.concatenate([upper[c + k], lower[c + k]], 0) for k in range(2)], 1)
            end = column + product(high[...], low[...], column)
            for k in range(2):
                column = end[:, k * LANES : (k + 1) * LANES]
                rest = base[c + k] - column
                base[c + k] = column
                for q in range(4):
                    split[kind, 4 * (i + k) + q] = rest[q * PART : (q + 1) * PART]
            pair, some = pl.ds(c, 2), pl.ds(4 * i, 8)
            outgoing.append(pltpu.make_async_copy(split.at[kind, some], out_ref.at[some], sems.at[4 + kind * 2 + i // 2]))
            outgoing.append(pltpu.make_async_copy(base.at[pair], end_ref.at[pair], sems.at[8 + kind * 2 + i // 2]))
            outgoing[-2].start()
            outgoing[-1].start()
    for copy in outgoing:
        copy.wait()


def scan_kernel(in_ref, order_ref, out_ref):
    def block(index, carry):
        here = pl.ds(pl.multiple_of(index * 8, 8), 8)
        total = jnp.zeros((8, LANES), F32)
        for k in range(PARTS):
            out_ref[k, here, :] = total
            total = total + in_ref[k, here, :]
        return carry

    lax.fori_loop(0, PART // 8, block, 0)


def share_kernel(core_ref, before_ref, keep_ref, order_ref, out_ref):
    first = (core_ref[0] == 0).astype(F32)
    out_ref[...] = before_ref[...] + first * keep_ref[...]


def finish_kernel(core_ref, base_ref, before_ref, partner_ref, other_ref, out_ref, out, sems):
    core = core_ref[0]
    flat = out.reshape(PAD * COLS, LANES)
    second = (core == 1).astype(F32)
    outgoing = []
    for q in range(4):
        for c in range(COLS):
            at = 4 * (c % 4) + q
            own = before_ref[at] + second * partner_ref[at]
            earlier = jnp.where(core == c // 4, own, other_ref[at])
            flat[pl.ds(q * PART * COLS + c, PART, stride=COLS), :] = (
                base_ref[c, q * PART : (q + 1) * PART, :] + earlier
            )
        rows = pl.ds(q * PART, min(PART, ROWS - q * PART))
        outgoing.append(pltpu.make_async_copy(out.at[rows], out_ref.at[rows], sems.at[q]))
        outgoing[-1].start()
    for copy in outgoing:
        copy.wait()


def spread_of(place):
    return (lax.broadcasted_iota(jnp.int32, (CAP, SLOTS), 0) == place.astype(jnp.int32)).astype(F32)


def sort_kernel(index_ref, frac_ref, order_ref, out_ref, place_ref):
    column_x = index_ref[0]
    bucket = lax.broadcasted_iota(jnp.int32, (TILES, SLOTS), 0)
    chosen = (bucket == (column_x >> 3)).astype(F32)
    before = lax.broadcasted_iota(jnp.int32, (SLOTS, SLOTS), 0) < lax.broadcasted_iota(jnp.int32, (SLOTS, SLOTS), 1)
    rank = jnp.dot(chosen.astype(BF16), before.astype(F32).astype(BF16), preferred_element_type=F32)
    place = jnp.sum(chosen * rank, axis=0, keepdims=True)
    spread = spread_of(place)
    place_ref[:TILES] = chosen
    place_ref[TILES:] = jnp.broadcast_to(place, (TILES, SLOTS))
    values = jnp.concatenate(
        [
            (column_x & (COLS - 1)).astype(F32),
            index_ref[1].astype(F32),
            index_ref[2].astype(F32),
            frac_ref[0],
            frac_ref[1],
            jnp.zeros((FIELDS - 5, SLOTS), F32),
        ],
        0,
    )
    for j in range(TILES):
        masked = values * chosen[j : j + 1, :]
        out_ref[j] = lax.dot_general(
            masked, spread, (((1,), (1,)), ((), ())), precision=HIGHEST, preferred_element_type=F32
        )


def observe_kernel(me_ref, obs_ref, end_ref, order_ref, out_ref, end_high, end_low):
    for c in range(COLS):
        high, low = two_parts(end_ref[c])
        end_high[:, c * LANES : (c + 1) * LANES] = high
        end_low[:, c * LANES : (c + 1) * LANES] = low
    lanes = 2 * CAP
    for j in range(0, TILES, 2):
        tiles = [(me_ref[0] - j - k + TILES) & (TILES - 1) for k in range(2)]
        fields = [jnp.concatenate([obs_ref[t, i : i + 1] for t in tiles], 1) for i in range(5)]
        column, line, row = [(f + 0.5).astype(jnp.int32) for f in fields[:3]]
        across, upward = fields[3:]
        y = lax.broadcasted_iota(jnp.int32, (LANES, lanes), 0)
        here, after = y == line, y == line + 1
        highs, lows = [], []
        for c in range(COLS):
            mine = column == c
            near = jnp.where(mine, 1.0 - across, 0.0)
            far = jnp.where(mine, across, 0.0)
            weight = jnp.where(here, near, jnp.where(after, far, 0.0))
            high, low = two_parts(weight)
            highs.append(high)
            lows.append(low)
        high, low = jnp.concatenate(highs, 0), jnp.concatenate(lows, 0)
        taken = jnp.dot(end_high[...], high, preferred_element_type=F32)
        taken = taken + jnp.dot(end_high[...], low, preferred_element_type=F32)
        taken = taken + jnp.dot(end_low[...], high, preferred_element_type=F32)
        r = lax.broadcasted_iota(jnp.int32, (PAD, lanes), 0)
        weight = jnp.where(r == row, 1.0 - upward, jnp.where(r == row + 1, upward, 0.0))
        value = jnp.sum(weight * taken, axis=0, keepdims=True)
        out_ref[j : j + 1, :] = value[:, :CAP]
        out_ref[j + 1 : j + 2, :] = value[:, CAP:]


def depart_kernel(count_ref, me_ref, back_ref, place_ref, value_ref, out_ref, ready_ref):
    ready_ref[...] = jnp.zeros((8, LANES), F32)
    spread = jnp.dot(
        back_ref[...], spread_of(place_ref[TILES : TILES + 1]), precision=HIGHEST, preferred_element_type=F32
    )
    evolved = jnp.zeros((1, SLOTS), F32)
    for j in range(TILES):
        tile = (me_ref[0] + j) & (TILES - 1)
        evolved = evolved + spread[j : j + 1] * place_ref[pl.ds(tile, 1)]
    live = lax.broadcasted_iota(jnp.int32, (1, SLOTS), 1) < count_ref[0, 0]
    out_ref[...] = jnp.where(live, value_ref[...] - evolved, 0.0)


def ring_step(blocks, by, offsets):
    size = blocks[0].shape[0]
    parcel = jnp.concatenate([blocks[o] for o in offsets], 0)
    parcel = lax.ppermute(parcel, "tile", [(i, (i + by) % TILES) for i in range(TILES)])
    return {o: parcel[at * size : (at + 1) * size] for at, o in enumerate(offsets)}


def give_back(found):
    blocks = {o: found[-o % TILES : -o % TILES + 1] for o in range(-4, 4)}
    for width, forward, backward in ((3, (2, 3), (-4, -3, -2)), (1, (-2, 1), (-4, -1, 2))):
        arrived = {**ring_step(blocks, width, forward), **ring_step(blocks, -width, backward)}
        blocks = {**blocks, **arrived}
    return jnp.concatenate([blocks[-j if j <= 4 else TILES - j] for j in range(TILES)], 0)


def per_device(
    increment, forcing, error_root, physics, coefficients, obs_index, obs_frac, obs_value, obs_count
):
    state = increment.reshape(ROWS, COLS, LANES)
    drive = forcing.reshape(ROWS, COLS, LANES)
    rates = coefficients.reshape(4, COLS, LANES)
    core = jnp.reshape(lax.axis_index("core"), (1,)).astype(jnp.int32)
    me = jnp.reshape(lax.axis_index("tile"), (1,)).astype(jnp.int32)
    field = PAD * COLS * LANES * 4

    to_west = [(i + 1, i) for i in range(TILES - 1)]
    to_east = [(i, i + 1) for i in range(TILES - 1)]

    west0, east0, west1, east1, sent = pack(state, rates)
    halo0 = lax.ppermute(east0, "tile", to_east), lax.ppermute(west0, "tile", to_west)
    halo1 = lax.ppermute(east1, "tile", to_east), lax.ppermute(west1, "tile", to_west)
    base, high, low, ready = call(
        prepare_kernel,
        [shape(COLS, PAD, LANES), shape(PAD, PAD, dtype=BF16), shape(PAD, PAD, dtype=BF16), shape(8, LANES)],
        (state, drive, error_root, physics.reshape(ROWS, ROWS), sent),
        scratch=[
            pltpu.VMEM((ROWS, COLS, LANES), F32),
            pltpu.VMEM((ROWS, COLS, LANES), F32),
            pltpu.VMEM((ROWS, ROWS), F32),
            pltpu.VMEM((PAD, PAD), F32),
            pltpu.VMEM((PAD, 2 * LANES), F32),
            pltpu.VMEM((COLS, PAD, LANES), F32),
            pltpu.VMEM((PAD, PAD), BF16),
            pltpu.VMEM((PAD, PAD), BF16),
            pltpu.SemaphoreType.DMA((9,)),
        ],
        flops=10**8,
        moved=10**6,
        far=(0, 1, 2),
        far_out=(0, 1, 2),
    )
    upper, uppered = call(
        upper_kernel,
        [shape(COLS, HALF, LANES), shape(8, LANES)],
        (state, rates, *halo0, *halo0, ready),
        scratch=[pltpu.VMEM((COLS, HALF, LANES), F32), pltpu.SemaphoreType.DMA] + transport_scratch(),
        flops=10**8,
        moved=10**6,
        far=range(6),
        far_out=(0,),
    )
    queries, places = call(
        sort_kernel,
        [shape(TILES, FIELDS, CAP), shape(2 * TILES, SLOTS)],
        (obs_index, obs_frac, uppered),
        flops=10**7,
        moved=10**5,
        mib=8,
    )
    arrived = lax.all_to_all(queries, "tile", 0, 0, tiled=True)
    parts = shape(PARTS, PART, LANES)
    end, keep, send = call(
        advance_kernel,
        [shape(COLS, PAD, LANES), parts, parts],
        (state, rates, *halo1, *halo0, core, upper, high, low, base, arrived),
        scratch=[
            pltpu.VMEM((COLS, HALF, LANES), F32),
            pltpu.VMEM((COLS, HALF, LANES), F32),
            pltpu.VMEM((COLS, PAD, LANES), F32),
            pltpu.VMEM((PAD, PAD), BF16),
            pltpu.VMEM((PAD, PAD), BF16),
            pltpu.VMEM((2, PARTS, PART, LANES), F32),
            pltpu.SemaphoreType.DMA((12,)),
        ]
        + transport_scratch(),
        flops=15 * 10**9,
        moved=6 * field,
        smem=(6,),
        far=(0, 1, 2, 3, 4, 5, 7, 8, 9, 10, 11),
        far_out=range(3),
    )
    swap = [(0, 1), (1, 0)]
    partner = lax.ppermute(send, "core", swap)
    pair = keep + partner
    paired = pair[0, :8]
    gathered = lax.all_to_all(pair, ("y", "x"), 0, 0, tiled=True)
    found = call(
        observe_kernel,
        shape(TILES, CAP),
        (me, arrived, end, paired),
        scratch=[
            pltpu.VMEM((PAD, COLS * LANES), BF16),
            pltpu.VMEM((PAD, COLS * LANES), BF16),
        ],
        flops=3 * 10**9,
        moved=field,
        smem=(0,),
        mib=10,
    )
    totals = call(scan_kernel, parts, (gathered, found), flops=10**7, moved=field, mib=6)
    before = lax.all_to_all(totals, ("y", "x"), 0, 0, tiled=True)
    departure, departed = call(
        depart_kernel,
        [shape(1, SLOTS), shape(8, LANES)],
        (obs_count, me, give_back(found), places, obs_value),
        flops=10**7,
        moved=10**6,
        smem=(0, 1),
        mib=4,
    )
    for_partner = call(
        share_kernel, parts, (core, before, keep, departed), flops=10**7, moved=2 * field, smem=(0,), mib=6
    )
    other = lax.ppermute(for_partner, "core", swap)
    summed = call(
        finish_kernel,
        shape(ROWS, COLS, LANES),
        (core, base, before, partner, other),
        scratch=[pltpu.VMEM((PAD, COLS, LANES), F32), pltpu.SemaphoreType.DMA((4,))],
        flops=10**7,
        moved=4 * field,
        smem=(0,),
        far_out=(0,),
        mib=10,
    )
    return summed.reshape(increment.shape), departure


def solution(mesh):
    split = Mesh(mesh.devices.reshape(GRID_Y, GRID_X, CORES, TILES), ("y", "x", "core", "tile"))
    win = ("y", "x", "core")
    return jax.shard_map(
        per_device,
        mesh=split,
        in_specs=(
            P(win, None, None, "tile", None),
            P(win, None, None, "tile", None),
            P(),
            P(win, None, None),
            P(win, None, "tile", None),
            P(None, win, "tile"),
            P(None, win, "tile"),
            P(win, "tile"),
            P(win, "tile"),
        ),
        out_specs=(P(win, None, None, "tile", None), P(win, "tile")),
        check_vma=False,
    )
```

```python
import jax
import jax.numpy as jnp
from jax import lax
from jax.experimental import pallas as pl
from jax.experimental.pallas import tpu as pltpu
from jax.sharding import Mesh, PartitionSpec as P

STEPS = 6
ROWS = 411
PAD = 416
COLS = 8
LANES = 128
GRID_Y = 4
GRID_X = 4
CORES = 2
PARTS = 16
PART = 104
TILES = 8
HALF = 208
SLOTS = 512
CAP = 128
FIELDS = 8

F32 = jnp.float32
BF16 = jnp.bfloat16
HIGHEST = lax.Precision.HIGHEST
MIB = 1 << 20
WIDE = 56


def call(body, outs, ins, scratch=(), flops=0, moved=0, smem=(), far=(), far_out=(), mib=WIDE):
    specs = [
        pl.BlockSpec(memory_space=pltpu.SMEM if at in smem else pl.ANY if at in far else pltpu.VMEM)
        for at in range(len(ins))
    ]
    many = isinstance(outs, (list, tuple))
    out_specs = [
        pl.BlockSpec(memory_space=pl.ANY if at in far_out else pltpu.VMEM)
        for at in range(len(outs) if many else 1)
    ]
    return pl.pallas_call(
        body,
        out_shape=outs,
        in_specs=specs,
        out_specs=out_specs if many else out_specs[0],
        scratch_shapes=list(scratch),
        compiler_params=pltpu.CompilerParams(vmem_limit_bytes=mib * MIB),
        cost_estimate=pl.CostEstimate(flops=flops, bytes_accessed=moved, transcendentals=0),
    )(*ins)


def shape(*dims, dtype=F32):
    return jax.ShapeDtypeStruct(dims, dtype)


def two_parts(value):
    high = value.astype(BF16)
    low = (value - high.astype(F32)).astype(BF16)
    return high, low


def product(left_high, left_low, right):
    high, low = two_parts(right)
    total = jnp.dot(left_high, high, preferred_element_type=F32)
    total = total + jnp.dot(left_high, low, preferred_element_type=F32)
    return total + jnp.dot(left_low, high, preferred_element_type=F32)


def pack_kernel(inc_ref, rate_ref, west_ref, east_ref, sent_ref, held, rates, west, east, in_sems, out_sems):
    count = PAD // PART
    incoming = [pltpu.make_async_copy(rate_ref, rates, in_sems.at[count])]
    for b in range(count):
        rows = pl.ds(b * PART, min(PART, ROWS - b * PART))
        incoming.append(pltpu.make_async_copy(inc_ref.at[rows], held.at[rows], in_sems.at[b]))
    for copy in incoming:
        copy.start()
    sent_ref[...] = jnp.zeros((8, LANES), F32)
    flat = held.reshape(PAD * COLS, LANES)
    outgoing = []
    incoming[0].wait()
    for b in range(count):
        incoming[b + 1].wait()
        size = min(PART, ROWS - b * PART)
        for c in range(COLS):
            column = flat[pl.ds(b * PART * COLS + c, size, stride=COLS), :]
            if size < PART:
                weights = [rates[i, c : c + 1, :] for i in range(4)]
                column = jnp.concatenate([column] + weights + [jnp.zeros((1, LANES), F32)], 0)
            if c < STEPS:
                west[c, b * PART : (b + 1) * PART, :] = column
            if c >= COLS - STEPS:
                east[c - COLS + STEPS, b * PART : (b + 1) * PART, :] = column
        rows = pl.ds(b * PART, PART)
        outgoing.append(pltpu.make_async_copy(west.at[:, rows], west_ref.at[:, rows], out_sems.at[2 * b]))
        outgoing.append(pltpu.make_async_copy(east.at[:, rows], east_ref.at[:, rows], out_sems.at[2 * b + 1]))
        outgoing[-2].start()
        outgoing[-1].start()
    for copy in outgoing:
        copy.wait()


def pack(state, rates):
    halo = shape(STEPS, PAD, LANES)
    return call(
        pack_kernel,
        [halo, halo, shape(8, LANES)],
        (state, rates),
        scratch=[
            pltpu.VMEM((PAD, COLS, LANES), F32),
            pltpu.VMEM((4, COLS, LANES), F32),
            pltpu.VMEM((STEPS, PAD, LANES), F32),
            pltpu.VMEM((STEPS, PAD, LANES), F32),
            pltpu.SemaphoreType.DMA((PAD // PART + 1,)),
            pltpu.SemaphoreType.DMA((2 * PAD // PART,)),
        ],
        moved=3 * PAD * COLS * LANES * 4,
        far=(0, 1),
        far_out=(0, 1),
    )


def prepare_kernel(
    inc_ref, forcing_ref, root_ref, physics_ref, order_ref, base_ref, high_ref, low_ref, ready_ref,
    start, force, root, square, drive, base, high, low, sems
):
    incoming = [
        pltpu.make_async_copy(root_ref, root, sems.at[0]),
        pltpu.make_async_copy(forcing_ref, force, sems.at[1]),
        pltpu.make_async_copy(inc_ref, start, sems.at[2]),
    ]
    for copy in incoming:
        copy.start()
    ready_ref[...] = jnp.zeros((8, LANES), F32)
    square[...] = jnp.zeros((PAD, PAD), F32)
    square[:ROWS, :ROWS] = 0.2 * physics_ref[...]
    once = square[...]
    twice = 2.0 * once + product(*two_parts(once), once)
    twice_parts = two_parts(twice)
    four = 2.0 * twice + product(*twice_parts, twice)
    six = twice + four + product(*twice_parts, four)
    high[...], low[...] = two_parts(six)
    outgoing = [
        pltpu.make_async_copy(high, high_ref, sems.at[3]),
        pltpu.make_async_copy(low, low_ref, sems.at[4]),
    ]
    for copy in outgoing:
        copy.start()
    for copy in incoming:
        copy.wait()
    square[:ROWS, :ROWS] = root[...]
    root_high, root_low = two_parts(square[...])
    force_flat = force.reshape(ROWS * COLS, LANES)
    start_flat = start.reshape(ROWS * COLS, LANES)
    drive[ROWS - 3 :, :] = jnp.zeros((PAD - ROWS + 3, 2 * LANES), F32)
    for c in range(0, COLS, 2):
        drive[:ROWS, :LANES] = force_flat[pl.ds(c, ROWS, stride=COLS), :]
        drive[:ROWS, LANES:] = force_flat[pl.ds(c + 1, ROWS, stride=COLS), :]
        forced = product(root_high, root_low, drive[...])
        for k in range(2):
            column = forced[:, k * LANES : (k + 1) * LANES]
            base[c + k, :ROWS, :] = start_flat[pl.ds(c + k, ROWS, stride=COLS), :] - column[:ROWS]
            base[c + k, ROWS:, :] = column[ROWS:]
        pair = pl.ds(c, 2)
        outgoing.append(pltpu.make_async_copy(base.at[pair], base_ref.at[pair], sems.at[5 + c // 2]))
        outgoing[-1].start()
    for copy in outgoing:
        copy.wait()


def rotated(j):
    return j % 5 in (0, 2)


def advance_kernel(
    inc_ref, rate_ref, west_ref, east_ref, core_ref, high_ref, low_ref, base_ref, order_ref,
    end_ref, keep_ref, send_ref, table, band, odd, even
):
    row = lax.broadcasted_iota(jnp.int32, (LANES, LANES), 0)
    lane = lax.broadcasted_iota(jnp.int32, (LANES, LANES), 1)
    wide = COLS + 2 * STEPS
    for j in range(1, wide - 1):
        if j < STEPS:
            rates = [west_ref[j, ROWS + i : ROWS + i + 1, :] for i in range(4)]
        elif j < STEPS + COLS:
            rates = [rate_ref[i, j - STEPS : j - STEPS + 1, :] for i in range(4)]
        else:
            rates = [east_ref[j - STEPS - COLS, ROWS + i : ROWS + i + 1, :] for i in range(4)]
        center = 1.0 - (rates[0] + rates[1] + rates[2] + rates[3])
        table[5 * j] = jnp.broadcast_to(rates[0], (8, LANES))
        table[5 * j + 1] = jnp.broadcast_to(rates[1], (8, LANES))
        if rotated(j):
            table[5 * j + 2] = jnp.broadcast_to(center, (8, LANES))
            table[5 * j + 3] = jnp.broadcast_to(jnp.where(lane[:1] == LANES - 1, 0.0, rates[2]), (8, LANES))
            table[5 * j + 4] = jnp.broadcast_to(jnp.where(lane[:1] == 0, 0.0, rates[3]), (8, LANES))
            continue
        along = jnp.where(row == lane, center, 0.0)
        along = jnp.where(row == lane + 1, rates[2], along)
        along = jnp.where(row == lane - 1, rates[3], along)
        along_high, along_low = two_parts(along)
        band[j, :LANES, :LANES] = along_high
        band[j, LANES:, :LANES] = along_high
        band[j, :LANES, LANES:] = along_low
        band[j, LANES:, LANES:] = jnp.zeros((LANES, LANES), BF16)
    flat = inc_ref.reshape(ROWS * COLS, LANES)
    for c in range(COLS):
        even[STEPS + c, :ROWS, :] = flat[pl.ds(c, ROWS, stride=COLS), :]
        even[STEPS + c, ROWS:, :] = jnp.zeros((PAD - ROWS, LANES), F32)

    def load(step, j, rows):
        if step == 0 and j < STEPS:
            return west_ref[j, rows, :]
        if step == 0 and j >= STEPS + COLS:
            return east_ref[j - STEPS - COLS, rows, :]
        return (odd if step % 2 else even)[j, rows, :]

    def tiles(value):
        return value.reshape(value.shape[0] // 8, 8, LANES)

    def finish(step, j, rows, total):
        total = total + table[5 * j] * tiles(load(step - 1, j + 1, rows))
        total = total + table[5 * j + 1] * tiles(load(step - 1, j - 1, rows))
        total = total.reshape(total.shape[0] * 8, LANES)
        if step == STEPS:
            end_ref[j - STEPS, rows, :] = total
        else:
            (odd if step % 2 else even)[j, rows, :] = total

    quarters = [slice(q * PART, (q + 1) * PART) for q in range(4)]
    for step in range(1, STEPS + 1):
        for j in range(step, wide - step):
            if rotated(j):
                for rows in quarters:
                    value = tiles(load(step - 1, j, rows))
                    total = table[5 * j + 2] * value
                    total = total + table[5 * j + 3] * pltpu.roll(value, LANES - 1, 2)
                    total = total + table[5 * j + 4] * pltpu.roll(value, 1, 2)
                    finish(step, j, rows, total)
            else:
                parts = jnp.concatenate(two_parts(load(step - 1, j, slice(None))), 1)
                along = jnp.dot(parts, band[j], preferred_element_type=F32)
                for rows in quarters:
                    finish(step, j, rows, tiles(along[rows, :LANES] + along[rows, LANES:]))

    core = core_ref[0]
    for kind, out_ref in ((1, send_ref), (0, keep_ref)):
        start = 4 * (core ^ kind)
        for i in (0, 2):
            c = start + i
            column = jnp.concatenate([end_ref[c], end_ref[c + 1]], 1)
            end = column + product(high_ref[...], low_ref[...], column)
            for k in range(2):
                column = end[:, k * LANES : (k + 1) * LANES]
                end_ref[c + k] = column
                rest = base_ref[c + k] - column
                for q in range(4):
                    out_ref[4 * (i + k) + q] = rest[q * PART : (q + 1) * PART]


def pair_kernel(keep_ref, partner_ref, pair_ref, ready_ref):
    pair_ref[...] = keep_ref[...] + partner_ref[...]
    ready_ref[...] = jnp.zeros((8, LANES), F32)


def scan_kernel(in_ref, order_ref, out_ref):
    def block(index, carry):
        here = pl.ds(pl.multiple_of(index * 8, 8), 8)
        total = jnp.zeros((8, LANES), F32)
        for k in range(PARTS):
            out_ref[k, here, :] = total
            total = total + in_ref[k, here, :]
        return carry

    lax.fori_loop(0, PART // 8, block, 0)


def share_kernel(core_ref, before_ref, keep_ref, order_ref, out_ref):
    first = (core_ref[0] == 0).astype(F32)
    out_ref[...] = before_ref[...] + first * keep_ref[...]


def finish_kernel(core_ref, base_ref, before_ref, partner_ref, other_ref, out_ref, out, sems):
    core = core_ref[0]
    flat = out.reshape(PAD * COLS, LANES)
    second = (core == 1).astype(F32)
    outgoing = []
    for q in range(4):
        for c in range(COLS):
            at = 4 * (c % 4) + q
            own = before_ref[at] + second * partner_ref[at]
            earlier = jnp.where(core == c // 4, own, other_ref[at])
            flat[pl.ds(q * PART * COLS + c, PART, stride=COLS), :] = (
                base_ref[c, q * PART : (q + 1) * PART, :] + earlier
            )
        rows = pl.ds(q * PART, min(PART, ROWS - q * PART))
        outgoing.append(pltpu.make_async_copy(out.at[rows], out_ref.at[rows], sems.at[q]))
        outgoing[-1].start()
    for copy in outgoing:
        copy.wait()


def spread_of(place):
    return (lax.broadcasted_iota(jnp.int32, (CAP, SLOTS), 0) == place.astype(jnp.int32)).astype(F32)


def sort_kernel(index_ref, frac_ref, order_ref, out_ref, place_ref):
    column_x = index_ref[0]
    bucket = lax.broadcasted_iota(jnp.int32, (TILES, SLOTS), 0)
    chosen = (bucket == (column_x >> 3)).astype(F32)
    before = lax.broadcasted_iota(jnp.int32, (SLOTS, SLOTS), 0) < lax.broadcasted_iota(jnp.int32, (SLOTS, SLOTS), 1)
    rank = jnp.dot(chosen.astype(BF16), before.astype(F32).astype(BF16), preferred_element_type=F32)
    place = jnp.sum(chosen * rank, axis=0, keepdims=True)
    spread = spread_of(place)
    place_ref[:TILES] = chosen
    place_ref[TILES:] = jnp.broadcast_to(place, (TILES, SLOTS))
    values = jnp.concatenate(
        [
            (column_x & (COLS - 1)).astype(F32),
            index_ref[1].astype(F32),
            index_ref[2].astype(F32),
            frac_ref[0],
            frac_ref[1],
            jnp.zeros((FIELDS - 5, SLOTS), F32),
        ],
        0,
    )
    for j in range(TILES):
        masked = values * chosen[j : j + 1, :]
        out_ref[j] = lax.dot_general(
            masked, spread, (((1,), (1,)), ((), ())), precision=HIGHEST, preferred_element_type=F32
        )


def observe_kernel(me_ref, obs_ref, end_ref, order_ref, out_ref, end_high, end_low):
    for c in range(COLS):
        high, low = two_parts(end_ref[c])
        end_high[:, c * LANES : (c + 1) * LANES] = high
        end_low[:, c * LANES : (c + 1) * LANES] = low
    lanes = 2 * CAP
    for j in range(0, TILES, 2):
        tiles = [(me_ref[0] - j - k + TILES) & (TILES - 1) for k in range(2)]
        fields = [jnp.concatenate([obs_ref[t, i : i + 1] for t in tiles], 1) for i in range(5)]
        column, line, row = [(f + 0.5).astype(jnp.int32) for f in fields[:3]]
        across, upward = fields[3:]
        y = lax.broadcasted_iota(jnp.int32, (LANES, lanes), 0)
        here, after = y == line, y == line + 1
        highs, lows = [], []
        for c in range(COLS):
            mine = column == c
            near = jnp.where(mine, 1.0 - across, 0.0)
            far = jnp.where(mine, across, 0.0)
            weight = jnp.where(here, near, jnp.where(after, far, 0.0))
            high, low = two_parts(weight)
            highs.append(high)
            lows.append(low)
        high, low = jnp.concatenate(highs, 0), jnp.concatenate(lows, 0)
        taken = jnp.dot(end_high[...], high, preferred_element_type=F32)
        taken = taken + jnp.dot(end_high[...], low, preferred_element_type=F32)
        taken = taken + jnp.dot(end_low[...], high, preferred_element_type=F32)
        r = lax.broadcasted_iota(jnp.int32, (PAD, lanes), 0)
        weight = jnp.where(r == row, 1.0 - upward, jnp.where(r == row + 1, upward, 0.0))
        value = jnp.sum(weight * taken, axis=0, keepdims=True)
        out_ref[j : j + 1, :] = value[:, :CAP]
        out_ref[j + 1 : j + 2, :] = value[:, CAP:]


def depart_kernel(count_ref, me_ref, back_ref, place_ref, value_ref, out_ref, ready_ref):
    ready_ref[...] = jnp.zeros((8, LANES), F32)
    spread = jnp.dot(
        back_ref[...], spread_of(place_ref[TILES : TILES + 1]), precision=HIGHEST, preferred_element_type=F32
    )
    evolved = jnp.zeros((1, SLOTS), F32)
    for j in range(TILES):
        tile = (me_ref[0] + j) & (TILES - 1)
        evolved = evolved + spread[j : j + 1] * place_ref[pl.ds(tile, 1)]
    live = lax.broadcasted_iota(jnp.int32, (1, SLOTS), 1) < count_ref[0, 0]
    out_ref[...] = jnp.where(live, value_ref[...] - evolved, 0.0)


def ring_step(blocks, by, offsets):
    size = blocks[0].shape[0]
    parcel = jnp.concatenate([blocks[o] for o in offsets], 0)
    parcel = lax.ppermute(parcel, "tile", [(i, (i + by) % TILES) for i in range(TILES)])
    return {o: parcel[at * size : (at + 1) * size] for at, o in enumerate(offsets)}


def give_back(found):
    blocks = {o: found[-o % TILES : -o % TILES + 1] for o in range(-4, 4)}
    for width, forward, backward in ((3, (2, 3), (-4, -3, -2)), (1, (-2, 1), (-4, -1, 2))):
        arrived = {**ring_step(blocks, width, forward), **ring_step(blocks, -width, backward)}
        blocks = {**blocks, **arrived}
    return jnp.concatenate([blocks[-j if j <= 4 else TILES - j] for j in range(TILES)], 0)


def per_device(
    increment, forcing, error_root, physics, coefficients, obs_index, obs_frac, obs_value, obs_count
):
    state = increment.reshape(ROWS, COLS, LANES)
    drive = forcing.reshape(ROWS, COLS, LANES)
    rates = coefficients.reshape(4, COLS, LANES)
    core = jnp.reshape(lax.axis_index("core"), (1,)).astype(jnp.int32)
    me = jnp.reshape(lax.axis_index("tile"), (1,)).astype(jnp.int32)
    field = PAD * COLS * LANES * 4

    to_west = [(i + 1, i) for i in range(TILES - 1)]
    to_east = [(i, i + 1) for i in range(TILES - 1)]

    west, east, sent = pack(state, rates)
    from_west = lax.ppermute(east, "tile", to_east)
    from_east = lax.ppermute(west, "tile", to_west)
    base, high, low, ready = call(
        prepare_kernel,
        [shape(COLS, PAD, LANES), shape(PAD, PAD, dtype=BF16), shape(PAD, PAD, dtype=BF16), shape(8, LANES)],
        (state, drive, error_root, physics.reshape(ROWS, ROWS), sent),
        scratch=[
            pltpu.VMEM((ROWS, COLS, LANES), F32),
            pltpu.VMEM((ROWS, COLS, LANES), F32),
            pltpu.VMEM((ROWS, ROWS), F32),
            pltpu.VMEM((PAD, PAD), F32),
            pltpu.VMEM((PAD, 2 * LANES), F32),
            pltpu.VMEM((COLS, PAD, LANES), F32),
            pltpu.VMEM((PAD, PAD), BF16),
            pltpu.VMEM((PAD, PAD), BF16),
            pltpu.SemaphoreType.DMA((9,)),
        ],
        flops=10**8,
        moved=10**6,
        far=(0, 1, 2),
        far_out=(0, 1, 2),
        mib=24,
    )
    queries, places = call(
        sort_kernel,
        [shape(TILES, FIELDS, CAP), shape(2 * TILES, SLOTS)],
        (obs_index, obs_frac, ready),
        flops=10**7,
        moved=10**5,
        mib=8,
    )
    arrived = lax.all_to_all(queries, "tile", 0, 0, tiled=True)
    parts = shape(PARTS, PART, LANES)
    wide = COLS + 2 * STEPS
    end, keep, send = call(
        advance_kernel,
        [shape(COLS, PAD, LANES), parts, parts],
        (state, rates, from_west, from_east, core, high, low, base, arrived),
        scratch=[
            pltpu.VMEM((5 * wide, 8, LANES), F32),
            pltpu.VMEM((wide, 2 * LANES, 2 * LANES), BF16),
            pltpu.VMEM((wide, PAD, LANES), F32),
            pltpu.VMEM((wide, PAD, LANES), F32),
        ],
        flops=15 * 10**9,
        moved=6 * field,
        smem=(4,),
        far=(8,),
        mib=36,
    )
    swap = [(0, 1), (1, 0)]
    partner = lax.ppermute(send, "core", swap)
    pair, paired = call(pair_kernel, [parts, shape(8, LANES)], (keep, partner), flops=10**6, moved=2 * field, mib=6)
    gathered = lax.all_to_all(pair, ("y", "x"), 0, 0, tiled=True)
    found = call(
        observe_kernel,
        shape(TILES, CAP),
        (me, arrived, end, paired),
        scratch=[
            pltpu.VMEM((PAD, COLS * LANES), BF16),
            pltpu.VMEM((PAD, COLS * LANES), BF16),
        ],
        flops=3 * 10**9,
        moved=field,
        smem=(0,),
        mib=10,
    )
    totals = call(scan_kernel, parts, (gathered, found), flops=10**7, moved=field, mib=6)
    before = lax.all_to_all(totals, ("y", "x"), 0, 0, tiled=True)
    departure, departed = call(
        depart_kernel,
        [shape(1, SLOTS), shape(8, LANES)],
        (obs_count, me, give_back(found), places, obs_value),
        flops=10**7,
        moved=10**6,
        smem=(0, 1),
        mib=4,
    )
    for_partner = call(
        share_kernel, parts, (core, before, keep, departed), flops=10**7, moved=2 * field, smem=(0,), mib=6
    )
    other = lax.ppermute(for_partner, "core", swap)
    summed = call(
        finish_kernel,
        shape(ROWS, COLS, LANES),
        (core, base, before, partner, other),
        scratch=[pltpu.VMEM((PAD, COLS, LANES), F32), pltpu.SemaphoreType.DMA((4,))],
        flops=10**7,
        moved=4 * field,
        smem=(0,),
        far_out=(0,),
        mib=10,
    )
    return summed.reshape(increment.shape), departure


def solution(mesh):
    split = Mesh(mesh.devices.reshape(GRID_Y, GRID_X, CORES, TILES), ("y", "x", "core", "tile"))
    win = ("y", "x", "core")
    return jax.shard_map(
        per_device,
        mesh=split,
        in_specs=(
            P(win, None, None, "tile", None),
            P(win, None, None, "tile", None),
            P(),
            P(win, None, None),
            P(win, None, "tile", None),
            P(None, win, "tile"),
            P(None, win, "tile"),
            P(win, "tile"),
            P(win, "tile"),
        ),
        out_specs=(P(win, None, None, "tile", None), P(win, "tile")),
        check_vma=False,
    )
```

```python
import jax
import jax.numpy as jnp
from jax import lax
from jax.experimental import pallas as pl
from jax.experimental.pallas import tpu as pltpu
from jax.sharding import Mesh, PartitionSpec as P

STEPS = 6
ROWS = 411
PAD = 416
COLS = 8
LANES = 128
GRID_Y = 4
GRID_X = 4
CORES = 2
PARTS = 16
PART = 104
TILES = 8
HALF = 208
STORE = 160
SLOTS = 512
CAP = 128
FIELDS = 8

F32 = jnp.float32
BF16 = jnp.bfloat16
HIGHEST = lax.Precision.HIGHEST
MIB = 1 << 20
WIDE = 56


def call(body, outs, ins, scratch=(), flops=0, moved=0, smem=(), far=(), far_out=(), mib=WIDE):
    specs = [
        pl.BlockSpec(memory_space=pltpu.SMEM if at in smem else pl.ANY if at in far else pltpu.VMEM)
        for at in range(len(ins))
    ]
    many = isinstance(outs, (list, tuple))
    out_specs = [
        pl.BlockSpec(memory_space=pl.ANY if at in far_out else pltpu.VMEM)
        for at in range(len(outs) if many else 1)
    ]
    return pl.pallas_call(
        body,
        out_shape=outs,
        in_specs=specs,
        out_specs=out_specs if many else out_specs[0],
        scratch_shapes=list(scratch),
        compiler_params=pltpu.CompilerParams(vmem_limit_bytes=mib * MIB),
        cost_estimate=pl.CostEstimate(flops=flops, bytes_accessed=moved, transcendentals=0),
    )(*ins)


def shape(*dims, dtype=F32):
    return jax.ShapeDtypeStruct(dims, dtype)


def two_parts(value):
    high = value.astype(BF16)
    low = (value - high.astype(F32)).astype(BF16)
    return high, low


def product(left_high, left_low, right):
    high, low = two_parts(right)
    total = jnp.dot(left_high, high, preferred_element_type=F32)
    total = total + jnp.dot(left_high, low, preferred_element_type=F32)
    return total + jnp.dot(left_low, high, preferred_element_type=F32)


def pack_kernel(inc_ref, rate_ref, west_ref, east_ref, sent_ref, held, rates, west, east, in_sems, out_sems):
    count = PAD // PART
    incoming = [pltpu.make_async_copy(rate_ref, rates, in_sems.at[count])]
    for b in range(count):
        rows = pl.ds(b * PART, min(PART, ROWS - b * PART))
        incoming.append(pltpu.make_async_copy(inc_ref.at[rows], held.at[rows], in_sems.at[b]))
    for copy in incoming:
        copy.start()
    sent_ref[...] = jnp.zeros((8, LANES), F32)
    flat = held.reshape(PAD * COLS, LANES)
    outgoing = []
    incoming[0].wait()
    for b in range(count):
        incoming[b + 1].wait()
        size = min(PART, ROWS - b * PART)
        for c in range(COLS):
            column = flat[pl.ds(b * PART * COLS + c, size, stride=COLS), :]
            if size < PART:
                weights = [rates[i, c : c + 1, :] for i in range(4)]
                column = jnp.concatenate([column] + weights + [jnp.zeros((1, LANES), F32)], 0)
            if c < STEPS:
                west[c, b * PART : (b + 1) * PART, :] = column
            if c >= COLS - STEPS:
                east[c - COLS + STEPS, b * PART : (b + 1) * PART, :] = column
        rows = pl.ds(b * PART, PART)
        outgoing.append(pltpu.make_async_copy(west.at[:, rows], west_ref.at[:, rows], out_sems.at[2 * b]))
        outgoing.append(pltpu.make_async_copy(east.at[:, rows], east_ref.at[:, rows], out_sems.at[2 * b + 1]))
        outgoing[-2].start()
        outgoing[-1].start()
    for copy in outgoing:
        copy.wait()


def pack(state, rates):
    halo = shape(STEPS, PAD, LANES)
    return call(
        pack_kernel,
        [halo, halo, shape(8, LANES)],
        (state, rates),
        scratch=[
            pltpu.VMEM((PAD, COLS, LANES), F32),
            pltpu.VMEM((4, COLS, LANES), F32),
            pltpu.VMEM((STEPS, PAD, LANES), F32),
            pltpu.VMEM((STEPS, PAD, LANES), F32),
            pltpu.SemaphoreType.DMA((PAD // PART + 1,)),
            pltpu.SemaphoreType.DMA((2 * PAD // PART,)),
        ],
        moved=3 * PAD * COLS * LANES * 4,
        far=(0, 1),
        far_out=(0, 1),
    )


def prepare_kernel(
    inc_ref, forcing_ref, root_ref, physics_ref, order_ref, base_ref, store_ref, ready_ref,
    start, force, root, square, drive, base, columns, powers, sems
):
    incoming = [
        pltpu.make_async_copy(root_ref, root, sems.at[0]),
        pltpu.make_async_copy(forcing_ref, force, sems.at[1]),
        pltpu.make_async_copy(inc_ref, start, sems.at[2]),
    ]
    for copy in incoming:
        copy.start()
    ready_ref[...] = jnp.zeros((8, LANES), F32)
    square[...] = jnp.zeros((PAD, PAD), F32)
    square[:ROWS, :ROWS] = 0.2 * physics_ref[...]
    once = square[...]
    twice = 2.0 * once + product(*two_parts(once), once)
    twice_parts = two_parts(twice)
    four = 2.0 * twice + product(*twice_parts, twice)
    six = twice + four + product(*twice_parts, four)
    powers[3] = jnp.zeros((PAD, LANES), F32)
    for p in range(4):
        width = min(LANES, PAD - p * LANES)
        powers[p, :, :width] = six[:, p * LANES : p * LANES + width]
    outgoing = [pltpu.make_async_copy(powers, store_ref.at[pl.ds(2 * COLS, 4)], sems.at[3])]
    outgoing[0].start()
    for copy in incoming:
        copy.wait()
    square[:ROWS, :ROWS] = root[...]
    root_high, root_low = two_parts(square[...])
    force_flat = force.reshape(ROWS * COLS, LANES)
    start_flat = start.reshape(ROWS * COLS, LANES)
    drive[ROWS - 3 :, :] = jnp.zeros((PAD - ROWS + 3, 2 * LANES), F32)
    for c in range(0, COLS, 2):
        drive[:ROWS, :LANES] = force_flat[pl.ds(c, ROWS, stride=COLS), :]
        drive[:ROWS, LANES:] = force_flat[pl.ds(c + 1, ROWS, stride=COLS), :]
        forced = product(root_high, root_low, drive[...])
        for k in range(2):
            column = start_flat[pl.ds(c + k, ROWS, stride=COLS), :]
            taken = forced[:, k * LANES : (k + 1) * LANES]
            columns[c + k, :ROWS, :] = column
            columns[c + k, ROWS:, :] = jnp.zeros((PAD - ROWS, LANES), F32)
            base[c + k, :ROWS, :] = column - taken[:ROWS]
            base[c + k, ROWS:, :] = taken[ROWS:]
        pair, beyond = pl.ds(c, 2), pl.ds(COLS + c, 2)
        outgoing.append(pltpu.make_async_copy(base.at[pair], base_ref.at[pair], sems.at[4 + c // 2]))
        outgoing.append(pltpu.make_async_copy(base.at[pair], store_ref.at[pair], sems.at[8 + c // 2]))
        outgoing.append(pltpu.make_async_copy(columns.at[pair], store_ref.at[beyond], sems.at[12 + c // 2]))
        for copy in outgoing[-3:]:
            copy.start()
    for copy in outgoing:
        copy.wait()


def rotated(j):
    return j % 5 in (0, 2)


def advance_kernel(
    rate_ref, west_ref, east_ref, core_ref, store_ref, order_ref,
    end_ref, keep_ref, send_ref, table, band, odd, even, end_held, base, powers, sems
):
    own = pltpu.make_async_copy(store_ref.at[pl.ds(COLS, COLS)], even.at[pl.ds(STEPS, COLS)], sems.at[0])
    own.start()
    later = [
        pltpu.make_async_copy(store_ref.at[pl.ds(2 * COLS, 4)], powers, sems.at[1]),
        pltpu.make_async_copy(store_ref.at[pl.ds(0, COLS)], base, sems.at[2]),
    ]
    for copy in later:
        copy.start()
    row = lax.broadcasted_iota(jnp.int32, (LANES, LANES), 0)
    lane = lax.broadcasted_iota(jnp.int32, (LANES, LANES), 1)
    wide = COLS + 2 * STEPS
    for j in range(1, wide - 1):
        if j < STEPS:
            rates = [west_ref[j, ROWS + i : ROWS + i + 1, :] for i in range(4)]
        elif j < STEPS + COLS:
            rates = [rate_ref[i, j - STEPS : j - STEPS + 1, :] for i in range(4)]
        else:
            rates = [east_ref[j - STEPS - COLS, ROWS + i : ROWS + i + 1, :] for i in range(4)]
        center = 1.0 - (rates[0] + rates[1] + rates[2] + rates[3])
        table[5 * j] = jnp.broadcast_to(rates[0], (8, LANES))
        table[5 * j + 1] = jnp.broadcast_to(rates[1], (8, LANES))
        if rotated(j):
            table[5 * j + 2] = jnp.broadcast_to(center, (8, LANES))
            table[5 * j + 3] = jnp.broadcast_to(jnp.where(lane[:1] == LANES - 1, 0.0, rates[2]), (8, LANES))
            table[5 * j + 4] = jnp.broadcast_to(jnp.where(lane[:1] == 0, 0.0, rates[3]), (8, LANES))
            continue
        along = jnp.where(row == lane, center, 0.0)
        along = jnp.where(row == lane + 1, rates[2], along)
        along = jnp.where(row == lane - 1, rates[3], along)
        along_high, along_low = two_parts(along)
        band[j, :LANES, :LANES] = along_high
        band[j, LANES:, :LANES] = along_high
        band[j, :LANES, LANES:] = along_low
        band[j, LANES:, LANES:] = jnp.zeros((LANES, LANES), BF16)
    own.wait()

    def load(step, j, rows):
        if step == 0 and j < STEPS:
            return west_ref[j, rows, :]
        if step == 0 and j >= STEPS + COLS:
            return east_ref[j - STEPS - COLS, rows, :]
        return (odd if step % 2 else even)[j, rows, :]

    def tiles(value):
        return value.reshape(value.shape[0] // 8, 8, LANES)

    def finish(step, j, rows, total):
        total = total + table[5 * j] * tiles(load(step - 1, j + 1, rows))
        total = total + table[5 * j + 1] * tiles(load(step - 1, j - 1, rows))
        total = total.reshape(total.shape[0] * 8, LANES)
        if step == STEPS:
            end_held[j - STEPS, rows, :] = total
        else:
            (odd if step % 2 else even)[j, rows, :] = total

    quarters = [slice(q * PART, (q + 1) * PART) for q in range(4)]
    for step in range(1, STEPS + 1):
        for j in range(step, wide - step):
            if rotated(j):
                for rows in quarters:
                    value = tiles(load(step - 1, j, rows))
                    total = table[5 * j + 2] * value
                    total = total + table[5 * j + 3] * pltpu.roll(value, LANES - 1, 2)
                    total = total + table[5 * j + 4] * pltpu.roll(value, 1, 2)
                    finish(step, j, rows, total)
            else:
                parts = jnp.concatenate(two_parts(load(step - 1, j, slice(None))), 1)
                along = jnp.dot(parts, band[j], preferred_element_type=F32)
                for rows in quarters:
                    finish(step, j, rows, tiles(along[rows, :LANES] + along[rows, LANES:]))

    for copy in later:
        copy.wait()
    high, low = two_parts(jnp.concatenate([powers[p] for p in range(4)], 1)[:, :PAD])
    core = core_ref[0]
    outgoing = []
    for kind, out_ref in ((1, send_ref), (0, keep_ref)):
        start = 4 * (core ^ kind)
        for i in (0, 2):
            c = start + i
            column = jnp.concatenate([end_held[c], end_held[c + 1]], 1)
            end = column + product(high, low, column)
            for k in range(2):
                column = end[:, k * LANES : (k + 1) * LANES]
                end_held[c + k] = column
                rest = base[c + k] - column
                for q in range(4):
                    out_ref[4 * (i + k) + q] = rest[q * PART : (q + 1) * PART]
            pair = pl.ds(c, 2)
            outgoing.append(pltpu.make_async_copy(end_held.at[pair], end_ref.at[pair], sems.at[3 + 2 * kind + i // 2]))
            outgoing[-1].start()
    for copy in outgoing:
        copy.wait()


def pair_kernel(keep_ref, partner_ref, pair_ref, ready_ref):
    pair_ref[...] = keep_ref[...] + partner_ref[...]
    ready_ref[...] = jnp.zeros((8, LANES), F32)


def scan_kernel(in_ref, order_ref, out_ref):
    def block(index, carry):
        here = pl.ds(pl.multiple_of(index * 8, 8), 8)
        total = jnp.zeros((8, LANES), F32)
        for k in range(PARTS):
            out_ref[k, here, :] = total
            total = total + in_ref[k, here, :]
        return carry

    lax.fori_loop(0, PART // 8, block, 0)


def share_kernel(core_ref, before_ref, keep_ref, order_ref, out_ref):
    first = (core_ref[0] == 0).astype(F32)
    out_ref[...] = before_ref[...] + first * keep_ref[...]


def finish_kernel(core_ref, base_ref, before_ref, partner_ref, other_ref, out_ref, out, sems):
    core = core_ref[0]
    flat = out.reshape(PAD * COLS, LANES)
    second = (core == 1).astype(F32)
    outgoing = []
    for q in range(4):
        for c in range(COLS):
            at = 4 * (c % 4) + q
            own = before_ref[at] + second * partner_ref[at]
            earlier = jnp.where(core == c // 4, own, other_ref[at])
            flat[pl.ds(q * PART * COLS + c, PART, stride=COLS), :] = (
                base_ref[c, q * PART : (q + 1) * PART, :] + earlier
            )
        rows = pl.ds(q * PART, min(PART, ROWS - q * PART))
        outgoing.append(pltpu.make_async_copy(out.at[rows], out_ref.at[rows], sems.at[q]))
        outgoing[-1].start()
    for copy in outgoing:
        copy.wait()


def spread_of(place):
    return (lax.broadcasted_iota(jnp.int32, (CAP, SLOTS), 0) == place.astype(jnp.int32)).astype(F32)


def sort_kernel(index_ref, frac_ref, order_ref, out_ref, place_ref):
    column_x = index_ref[0]
    bucket = lax.broadcasted_iota(jnp.int32, (TILES, SLOTS), 0)
    chosen = (bucket == (column_x >> 3)).astype(F32)
    before = lax.broadcasted_iota(jnp.int32, (SLOTS, SLOTS), 0) < lax.broadcasted_iota(jnp.int32, (SLOTS, SLOTS), 1)
    rank = jnp.dot(chosen.astype(BF16), before.astype(F32).astype(BF16), preferred_element_type=F32)
    place = jnp.sum(chosen * rank, axis=0, keepdims=True)
    spread = spread_of(place)
    place_ref[:TILES] = chosen
    place_ref[TILES:] = jnp.broadcast_to(place, (TILES, SLOTS))
    values = jnp.concatenate(
        [
            (column_x & (COLS - 1)).astype(F32),
            index_ref[1].astype(F32),
            index_ref[2].astype(F32),
            frac_ref[0],
            frac_ref[1],
            jnp.zeros((FIELDS - 5, SLOTS), F32),
        ],
        0,
    )
    for j in range(TILES):
        masked = values * chosen[j : j + 1, :]
        out_ref[j] = lax.dot_general(
            masked, spread, (((1,), (1,)), ((), ())), precision=HIGHEST, preferred_element_type=F32
        )


def observe_kernel(me_ref, obs_ref, end_ref, order_ref, out_ref, end_high, end_low, end, sems):
    copies = [pltpu.make_async_copy(end_ref.at[c], end.at[c], sems.at[c]) for c in range(COLS)]
    for copy in copies:
        copy.start()
    for c in range(COLS):
        copies[c].wait()
        high, low = two_parts(end[c])
        end_high[:, c * LANES : (c + 1) * LANES] = high
        end_low[:, c * LANES : (c + 1) * LANES] = low
    lanes = 2 * CAP
    for j in range(0, TILES, 2):
        tiles = [(me_ref[0] - j - k + TILES) & (TILES - 1) for k in range(2)]
        fields = [jnp.concatenate([obs_ref[t, i : i + 1] for t in tiles], 1) for i in range(5)]
        column, line, row = [(f + 0.5).astype(jnp.int32) for f in fields[:3]]
        across, upward = fields[3:]
        y = lax.broadcasted_iota(jnp.int32, (LANES, lanes), 0)
        here, after = y == line, y == line + 1
        highs, lows = [], []
        for c in range(COLS):
            mine = column == c
            near = jnp.where(mine, 1.0 - across, 0.0)
            far = jnp.where(mine, across, 0.0)
            weight = jnp.where(here, near, jnp.where(after, far, 0.0))
            high, low = two_parts(weight)
            highs.append(high)
            lows.append(low)
        high, low = jnp.concatenate(highs, 0), jnp.concatenate(lows, 0)
        taken = jnp.dot(end_high[...], high, preferred_element_type=F32)
        taken = taken + jnp.dot(end_high[...], low, preferred_element_type=F32)
        taken = taken + jnp.dot(end_low[...], high, preferred_element_type=F32)
        r = lax.broadcasted_iota(jnp.int32, (PAD, lanes), 0)
        weight = jnp.where(r == row, 1.0 - upward, jnp.where(r == row + 1, upward, 0.0))
        value = jnp.sum(weight * taken, axis=0, keepdims=True)
        out_ref[j : j + 1, :] = value[:, :CAP]
        out_ref[j + 1 : j + 2, :] = value[:, CAP:]


def depart_kernel(count_ref, me_ref, back_ref, place_ref, value_ref, out_ref, ready_ref):
    ready_ref[...] = jnp.zeros((8, LANES), F32)
    spread = jnp.dot(
        back_ref[...], spread_of(place_ref[TILES : TILES + 1]), precision=HIGHEST, preferred_element_type=F32
    )
    evolved = jnp.zeros((1, SLOTS), F32)
    for j in range(TILES):
        tile = (me_ref[0] + j) & (TILES - 1)
        evolved = evolved + spread[j : j + 1] * place_ref[pl.ds(tile, 1)]
    live = lax.broadcasted_iota(jnp.int32, (1, SLOTS), 1) < count_ref[0, 0]
    out_ref[...] = jnp.where(live, value_ref[...] - evolved, 0.0)


def ring_step(blocks, by, offsets):
    size = blocks[0].shape[0]
    parcel = jnp.concatenate([blocks[o] for o in offsets], 0)
    parcel = lax.ppermute(parcel, "tile", [(i, (i + by) % TILES) for i in range(TILES)])
    return {o: parcel[at * size : (at + 1) * size] for at, o in enumerate(offsets)}


def give_back(found):
    blocks = {o: found[-o % TILES : -o % TILES + 1] for o in range(-4, 4)}
    for width, forward, backward in ((3, (2, 3), (-4, -3, -2)), (1, (-2, 1), (-4, -1, 2))):
        arrived = {**ring_step(blocks, width, forward), **ring_step(blocks, -width, backward)}
        blocks = {**blocks, **arrived}
    return jnp.concatenate([blocks[-j if j <= 4 else TILES - j] for j in range(TILES)], 0)


def per_device(
    increment, forcing, error_root, physics, coefficients, obs_index, obs_frac, obs_value, obs_count
):
    state = increment.reshape(ROWS, COLS, LANES)
    drive = forcing.reshape(ROWS, COLS, LANES)
    rates = coefficients.reshape(4, COLS, LANES)
    core = jnp.reshape(lax.axis_index("core"), (1,)).astype(jnp.int32)
    me = jnp.reshape(lax.axis_index("tile"), (1,)).astype(jnp.int32)
    field = PAD * COLS * LANES * 4

    to_west = [(i + 1, i) for i in range(TILES - 1)]
    to_east = [(i, i + 1) for i in range(TILES - 1)]

    west, east, sent = pack(state, rates)
    from_west = lax.ppermute(east, "tile", to_east)
    from_east = lax.ppermute(west, "tile", to_west)
    store = shape(STORE, PAD, LANES)
    base, planes, ready = call(
        prepare_kernel,
        [shape(COLS, PAD, LANES), store, shape(8, LANES)],
        (state, drive, error_root, physics.reshape(ROWS, ROWS), sent),
        scratch=[
            pltpu.VMEM((ROWS, COLS, LANES), F32),
            pltpu.VMEM((ROWS, COLS, LANES), F32),
            pltpu.VMEM((ROWS, ROWS), F32),
            pltpu.VMEM((PAD, PAD), F32),
            pltpu.VMEM((PAD, 2 * LANES), F32),
            pltpu.VMEM((COLS, PAD, LANES), F32),
            pltpu.VMEM((COLS, PAD, LANES), F32),
            pltpu.VMEM((4, PAD, LANES), F32),
            pltpu.SemaphoreType.DMA((16,)),
        ],
        flops=10**8,
        moved=10**6,
        far=(0, 1, 2),
        far_out=(0, 1),
        mib=24,
    )
    queries, places = call(
        sort_kernel,
        [shape(TILES, FIELDS, CAP), shape(2 * TILES, SLOTS)],
        (obs_index, obs_frac, ready),
        flops=10**7,
        moved=10**5,
        mib=8,
    )
    arrived = lax.all_to_all(queries, "tile", 0, 0, tiled=True)
    parts = shape(PARTS, PART, LANES)
    wide = COLS + 2 * STEPS
    end, keep, send = call(
        advance_kernel,
        [store, parts, parts],
        (rates, from_west, from_east, core, planes, arrived),
        scratch=[
            pltpu.VMEM((5 * wide, 8, LANES), F32),
            pltpu.VMEM((wide, 2 * LANES, 2 * LANES), BF16),
            pltpu.VMEM((wide, PAD, LANES), F32),
            pltpu.VMEM((wide, PAD, LANES), F32),
            pltpu.VMEM((COLS, PAD, LANES), F32),
            pltpu.VMEM((COLS, PAD, LANES), F32),
            pltpu.VMEM((4, PAD, LANES), F32),
            pltpu.SemaphoreType.DMA((7,)),
        ],
        flops=15 * 10**9,
        moved=6 * field,
        smem=(3,),
        far=(4, 5),
        far_out=(0,),
        mib=36,
    )
    swap = [(0, 1), (1, 0)]
    partner = lax.ppermute(send, "core", swap)
    pair, paired = call(pair_kernel, [parts, shape(8, LANES)], (keep, partner), flops=10**6, moved=2 * field, mib=6)
    gathered = lax.all_to_all(pair, ("y", "x"), 0, 0, tiled=True)
    found = call(
        observe_kernel,
        shape(TILES, CAP),
        (me, arrived, end, paired),
        scratch=[
            pltpu.VMEM((PAD, COLS * LANES), BF16),
            pltpu.VMEM((PAD, COLS * LANES), BF16),
            pltpu.VMEM((COLS, PAD, LANES), F32),
            pltpu.SemaphoreType.DMA((COLS,)),
        ],
        flops=3 * 10**9,
        moved=field,
        smem=(0,),
        far=(2,),
        mib=10,
    )
    totals = call(scan_kernel, parts, (gathered, found), flops=10**7, moved=field, mib=6)
    before = lax.all_to_all(totals, ("y", "x"), 0, 0, tiled=True)
    departure, departed = call(
        depart_kernel,
        [shape(1, SLOTS), shape(8, LANES)],
        (obs_count, me, give_back(found), places, obs_value),
        flops=10**7,
        moved=10**6,
        smem=(0, 1),
        mib=4,
    )
    for_partner = call(
        share_kernel, parts, (core, before, keep, departed), flops=10**7, moved=2 * field, smem=(0,), mib=6
    )
    other = lax.ppermute(for_partner, "core", swap)
    summed = call(
        finish_kernel,
        shape(ROWS, COLS, LANES),
        (core, base, before, partner, other),
        scratch=[pltpu.VMEM((PAD, COLS, LANES), F32), pltpu.SemaphoreType.DMA((4,))],
        flops=10**7,
        moved=4 * field,
        smem=(0,),
        far_out=(0,),
        mib=10,
    )
    return summed.reshape(increment.shape), departure


def solution(mesh):
    split = Mesh(mesh.devices.reshape(GRID_Y, GRID_X, CORES, TILES), ("y", "x", "core", "tile"))
    win = ("y", "x", "core")
    return jax.shard_map(
        per_device,
        mesh=split,
        in_specs=(
            P(win, None, None, "tile", None),
            P(win, None, None, "tile", None),
            P(),
            P(win, None, None),
            P(win, None, "tile", None),
            P(None, win, "tile"),
            P(None, win, "tile"),
            P(win, "tile"),
            P(win, "tile"),
        ),
        out_specs=(P(win, None, None, "tile", None), P(win, "tile")),
        check_vma=False,
    )
```

```python
import jax
import jax.numpy as jnp
from jax import lax
from jax.experimental import pallas as pl
from jax.experimental.pallas import tpu as pltpu
from jax.sharding import Mesh, PartitionSpec as P

STEPS = 6
ROWS = 411
PAD = 416
COLS = 8
LANES = 128
GRID_Y = 4
GRID_X = 4
CORES = 2
PARTS = 16
PART = 104
TILES = 8
HALF = 208
STORE = 160
END_STORE = 320
SLOTS = 512
CAP = 128
FIELDS = 8

F32 = jnp.float32
BF16 = jnp.bfloat16
HIGHEST = lax.Precision.HIGHEST
MIB = 1 << 20
WIDE = 56


def call(body, outs, ins, scratch=(), flops=0, moved=0, smem=(), far=(), far_out=(), mib=WIDE):
    specs = [
        pl.BlockSpec(memory_space=pltpu.SMEM if at in smem else pl.ANY if at in far else pltpu.VMEM)
        for at in range(len(ins))
    ]
    many = isinstance(outs, (list, tuple))
    out_specs = [
        pl.BlockSpec(memory_space=pl.ANY if at in far_out else pltpu.VMEM)
        for at in range(len(outs) if many else 1)
    ]
    return pl.pallas_call(
        body,
        out_shape=outs,
        in_specs=specs,
        out_specs=out_specs if many else out_specs[0],
        scratch_shapes=list(scratch),
        compiler_params=pltpu.CompilerParams(vmem_limit_bytes=mib * MIB),
        cost_estimate=pl.CostEstimate(flops=flops, bytes_accessed=moved, transcendentals=0),
    )(*ins)


def shape(*dims, dtype=F32):
    return jax.ShapeDtypeStruct(dims, dtype)


def two_parts(value):
    high = value.astype(BF16)
    low = (value - high.astype(F32)).astype(BF16)
    return high, low


def product(left_high, left_low, right):
    high, low = two_parts(right)
    total = jnp.dot(left_high, high, preferred_element_type=F32)
    total = total + jnp.dot(left_high, low, preferred_element_type=F32)
    return total + jnp.dot(left_low, high, preferred_element_type=F32)


def pack_kernel(inc_ref, rate_ref, west_ref, east_ref, sent_ref, held, rates, west, east, in_sems, out_sems):
    count = PAD // PART
    incoming = [pltpu.make_async_copy(rate_ref, rates, in_sems.at[count])]
    for b in range(count):
        rows = pl.ds(b * PART, min(PART, ROWS - b * PART))
        incoming.append(pltpu.make_async_copy(inc_ref.at[rows], held.at[rows], in_sems.at[b]))
    for copy in incoming:
        copy.start()
    sent_ref[...] = jnp.zeros((8, LANES), F32)
    flat = held.reshape(PAD * COLS, LANES)
    outgoing = []
    incoming[0].wait()
    for b in range(count):
        incoming[b + 1].wait()
        size = min(PART, ROWS - b * PART)
        for c in range(COLS):
            column = flat[pl.ds(b * PART * COLS + c, size, stride=COLS), :]
            if size < PART:
                weights = [rates[i, c : c + 1, :] for i in range(4)]
                column = jnp.concatenate([column] + weights + [jnp.zeros((1, LANES), F32)], 0)
            if c < STEPS:
                west[c, b * PART : (b + 1) * PART, :] = column
            if c >= COLS - STEPS:
                east[c - COLS + STEPS, b * PART : (b + 1) * PART, :] = column
        rows = pl.ds(b * PART, PART)
        outgoing.append(pltpu.make_async_copy(west.at[:, rows], west_ref.at[:, rows], out_sems.at[2 * b]))
        outgoing.append(pltpu.make_async_copy(east.at[:, rows], east_ref.at[:, rows], out_sems.at[2 * b + 1]))
        outgoing[-2].start()
        outgoing[-1].start()
    for copy in outgoing:
        copy.wait()


def pack(state, rates):
    halo = shape(STEPS, PAD, LANES)
    return call(
        pack_kernel,
        [halo, halo, shape(8, LANES)],
        (state, rates),
        scratch=[
            pltpu.VMEM((PAD, COLS, LANES), F32),
            pltpu.VMEM((4, COLS, LANES), F32),
            pltpu.VMEM((STEPS, PAD, LANES), F32),
            pltpu.VMEM((STEPS, PAD, LANES), F32),
            pltpu.SemaphoreType.DMA((PAD // PART + 1,)),
            pltpu.SemaphoreType.DMA((2 * PAD // PART,)),
        ],
        moved=3 * PAD * COLS * LANES * 4,
        far=(0, 1),
        far_out=(0, 1),
    )


def prepare_kernel(
    inc_ref, forcing_ref, root_ref, physics_ref, order_ref, base_ref, store_ref, ready_ref,
    start, force, root, square, drive, base, columns, powers, sems
):
    incoming = [
        pltpu.make_async_copy(root_ref, root, sems.at[0]),
        pltpu.make_async_copy(forcing_ref, force, sems.at[1]),
        pltpu.make_async_copy(inc_ref, start, sems.at[2]),
    ]
    for copy in incoming:
        copy.start()
    ready_ref[...] = jnp.zeros((8, LANES), F32)
    square[...] = jnp.zeros((PAD, PAD), F32)
    square[:ROWS, :ROWS] = 0.2 * physics_ref[...]
    once = square[...]
    twice = 2.0 * once + product(*two_parts(once), once)
    twice_parts = two_parts(twice)
    four = 2.0 * twice + product(*twice_parts, twice)
    six = twice + four + product(*twice_parts, four)
    powers[3] = jnp.zeros((PAD, LANES), F32)
    for p in range(4):
        width = min(LANES, PAD - p * LANES)
        powers[p, :, :width] = six[:, p * LANES : p * LANES + width]
    outgoing = [pltpu.make_async_copy(powers, store_ref.at[pl.ds(2 * COLS, 4)], sems.at[3])]
    outgoing[0].start()
    for copy in incoming:
        copy.wait()
    square[:ROWS, :ROWS] = root[...]
    root_high, root_low = two_parts(square[...])
    force_flat = force.reshape(ROWS * COLS, LANES)
    start_flat = start.reshape(ROWS * COLS, LANES)
    drive[ROWS - 3 :, :] = jnp.zeros((PAD - ROWS + 3, 2 * LANES), F32)
    for c in range(0, COLS, 2):
        drive[:ROWS, :LANES] = force_flat[pl.ds(c, ROWS, stride=COLS), :]
        drive[:ROWS, LANES:] = force_flat[pl.ds(c + 1, ROWS, stride=COLS), :]
        forced = product(root_high, root_low, drive[...])
        for k in range(2):
            column = start_flat[pl.ds(c + k, ROWS, stride=COLS), :]
            taken = forced[:, k * LANES : (k + 1) * LANES]
            columns[c + k, :ROWS, :] = column
            columns[c + k, ROWS:, :] = jnp.zeros((PAD - ROWS, LANES), F32)
            base[c + k, :ROWS, :] = column - taken[:ROWS]
            base[c + k, ROWS:, :] = taken[ROWS:]
        pair, beyond = pl.ds(c, 2), pl.ds(COLS + c, 2)
        outgoing.append(pltpu.make_async_copy(base.at[pair], base_ref.at[pair], sems.at[4 + c // 2]))
        outgoing.append(pltpu.make_async_copy(base.at[pair], store_ref.at[pair], sems.at[8 + c // 2]))
        outgoing.append(pltpu.make_async_copy(columns.at[pair], store_ref.at[beyond], sems.at[12 + c // 2]))
        for copy in outgoing[-3:]:
            copy.start()
    for copy in outgoing:
        copy.wait()


def rotated(j):
    return j % 5 in (0, 2)


def advance_kernel(
    rate_ref, west_ref, east_ref, core_ref, store_ref, order_ref,
    end_ref, keep_ref, send_ref, table, band, odd, even, end_held, base, powers, sems
):
    own = pltpu.make_async_copy(store_ref.at[pl.ds(COLS, COLS)], even.at[pl.ds(STEPS, COLS)], sems.at[0])
    own.start()
    later = [
        pltpu.make_async_copy(store_ref.at[pl.ds(2 * COLS, 4)], powers, sems.at[1]),
        pltpu.make_async_copy(store_ref.at[pl.ds(0, COLS)], base, sems.at[2]),
    ]
    for copy in later:
        copy.start()
    row = lax.broadcasted_iota(jnp.int32, (LANES, LANES), 0)
    lane = lax.broadcasted_iota(jnp.int32, (LANES, LANES), 1)
    wide = COLS + 2 * STEPS
    for j in range(1, wide - 1):
        if j < STEPS:
            rates = [west_ref[j, ROWS + i : ROWS + i + 1, :] for i in range(4)]
        elif j < STEPS + COLS:
            rates = [rate_ref[i, j - STEPS : j - STEPS + 1, :] for i in range(4)]
        else:
            rates = [east_ref[j - STEPS - COLS, ROWS + i : ROWS + i + 1, :] for i in range(4)]
        center = 1.0 - (rates[0] + rates[1] + rates[2] + rates[3])
        table[5 * j] = jnp.broadcast_to(rates[0], (8, LANES))
        table[5 * j + 1] = jnp.broadcast_to(rates[1], (8, LANES))
        if rotated(j):
            table[5 * j + 2] = jnp.broadcast_to(center, (8, LANES))
            table[5 * j + 3] = jnp.broadcast_to(jnp.where(lane[:1] == LANES - 1, 0.0, rates[2]), (8, LANES))
            table[5 * j + 4] = jnp.broadcast_to(jnp.where(lane[:1] == 0, 0.0, rates[3]), (8, LANES))
            continue
        along = jnp.where(row == lane, center, 0.0)
        along = jnp.where(row == lane + 1, rates[2], along)
        along = jnp.where(row == lane - 1, rates[3], along)
        along_high, along_low = two_parts(along)
        band[j, :LANES, :LANES] = along_high
        band[j, LANES:, :LANES] = along_high
        band[j, :LANES, LANES:] = along_low
        band[j, LANES:, LANES:] = jnp.zeros((LANES, LANES), BF16)
    def load(step, j, rows):
        if step == 0 and j < STEPS:
            return west_ref[j, rows, :]
        if step == 0 and j >= STEPS + COLS:
            return east_ref[j - STEPS - COLS, rows, :]
        return (odd if step % 2 else even)[j, rows, :]

    def tiles(value):
        return value.reshape(value.shape[0] // 8, 8, LANES)

    def finish(step, j, rows, total):
        total = total + table[5 * j] * tiles(load(step - 1, j + 1, rows))
        total = total + table[5 * j + 1] * tiles(load(step - 1, j - 1, rows))
        total = total.reshape(total.shape[0] * 8, LANES)
        if step == STEPS:
            end_held[j - STEPS, rows, :] = total
        else:
            (odd if step % 2 else even)[j, rows, :] = total

    quarters = [slice(q * PART, (q + 1) * PART) for q in range(4)]
    for step in range(1, STEPS + 1):
        order = list(range(step, wide - step))
        if step == 1:
            apart = [j for j in order if j < STEPS - 1 or j > STEPS + COLS]
            order = apart + [j for j in order if j not in apart]
        for j in order:
            if step == 1 and j == STEPS - 1:
                own.wait()
            if rotated(j):
                for rows in quarters:
                    value = tiles(load(step - 1, j, rows))
                    total = table[5 * j + 2] * value
                    total = total + table[5 * j + 3] * pltpu.roll(value, LANES - 1, 2)
                    total = total + table[5 * j + 4] * pltpu.roll(value, 1, 2)
                    finish(step, j, rows, total)
            else:
                parts = jnp.concatenate(two_parts(load(step - 1, j, slice(None))), 1)
                along = jnp.dot(parts, band[j], preferred_element_type=F32)
                for rows in quarters:
                    finish(step, j, rows, tiles(along[rows, :LANES] + along[rows, LANES:]))

    for copy in later:
        copy.wait()
    high, low = two_parts(jnp.concatenate([powers[p] for p in range(4)], 1)[:, :PAD])
    core = core_ref[0]
    outgoing = []
    for kind, out_ref in ((1, send_ref), (0, keep_ref)):
        start = 4 * (core ^ kind)
        for i in (0, 2):
            c = start + i
            column = jnp.concatenate([end_held[c], end_held[c + 1]], 1)
            end = column + product(high, low, column)
            for k in range(2):
                column = end[:, k * LANES : (k + 1) * LANES]
                end_held[c + k] = column
                rest = base[c + k] - column
                for q in range(4):
                    out_ref[4 * (i + k) + q] = rest[q * PART : (q + 1) * PART]
            pair = pl.ds(c, 2)
            outgoing.append(pltpu.make_async_copy(end_held.at[pair], end_ref.at[pair], sems.at[3 + 2 * kind + i // 2]))
            outgoing[-1].start()
    for copy in outgoing:
        copy.wait()


def pair_kernel(keep_ref, partner_ref, pair_ref, ready_ref):
    pair_ref[...] = keep_ref[...] + partner_ref[...]
    ready_ref[...] = jnp.zeros((8, LANES), F32)


def scan_kernel(in_ref, order_ref, out_ref):
    def block(index, carry):
        here = pl.ds(pl.multiple_of(index * 8, 8), 8)
        total = jnp.zeros((8, LANES), F32)
        for k in range(PARTS):
            out_ref[k, here, :] = total
            total = total + in_ref[k, here, :]
        return carry

    lax.fori_loop(0, PART // 8, block, 0)


def share_kernel(core_ref, before_ref, keep_ref, order_ref, out_ref):
    first = (core_ref[0] == 0).astype(F32)
    out_ref[...] = before_ref[...] + first * keep_ref[...]


def finish_kernel(core_ref, base_ref, before_ref, partner_ref, other_ref, out_ref, out, sems):
    core = core_ref[0]
    flat = out.reshape(PAD * COLS, LANES)
    second = (core == 1).astype(F32)
    outgoing = []
    for q in range(4):
        for c in range(COLS):
            at = 4 * (c % 4) + q
            own = before_ref[at] + second * partner_ref[at]
            earlier = jnp.where(core == c // 4, own, other_ref[at])
            flat[pl.ds(q * PART * COLS + c, PART, stride=COLS), :] = (
                base_ref[c, q * PART : (q + 1) * PART, :] + earlier
            )
        rows = pl.ds(q * PART, min(PART, ROWS - q * PART))
        outgoing.append(pltpu.make_async_copy(out.at[rows], out_ref.at[rows], sems.at[q]))
        outgoing[-1].start()
    for copy in outgoing:
        copy.wait()


def spread_of(place):
    return (lax.broadcasted_iota(jnp.int32, (CAP, SLOTS), 0) == place.astype(jnp.int32)).astype(F32)


def sort_kernel(index_ref, frac_ref, order_ref, out_ref, place_ref):
    column_x = index_ref[0]
    bucket = lax.broadcasted_iota(jnp.int32, (TILES, SLOTS), 0)
    chosen = (bucket == (column_x >> 3)).astype(F32)
    before = lax.broadcasted_iota(jnp.int32, (SLOTS, SLOTS), 0) < lax.broadcasted_iota(jnp.int32, (SLOTS, SLOTS), 1)
    rank = jnp.dot(chosen.astype(BF16), before.astype(F32).astype(BF16), preferred_element_type=F32)
    place = jnp.sum(chosen * rank, axis=0, keepdims=True)
    spread = spread_of(place)
    place_ref[:TILES] = chosen
    place_ref[TILES:] = jnp.broadcast_to(place, (TILES, SLOTS))
    values = jnp.concatenate(
        [
            (column_x & (COLS - 1)).astype(F32),
            index_ref[1].astype(F32),
            index_ref[2].astype(F32),
            frac_ref[0],
            frac_ref[1],
            jnp.zeros((FIELDS - 5, SLOTS), F32),
        ],
        0,
    )
    for j in range(TILES):
        masked = values * chosen[j : j + 1, :]
        out_ref[j] = lax.dot_general(
            masked, spread, (((1,), (1,)), ((), ())), precision=HIGHEST, preferred_element_type=F32
        )


def observe_kernel(me_ref, obs_ref, end_ref, order_ref, out_ref, end_high, end_low, end, sems):
    copies = [pltpu.make_async_copy(end_ref.at[c], end.at[c], sems.at[c]) for c in range(COLS)]
    for copy in copies:
        copy.start()
    for c in range(COLS):
        copies[c].wait()
        high, low = two_parts(end[c])
        end_high[:, c * LANES : (c + 1) * LANES] = high
        end_low[:, c * LANES : (c + 1) * LANES] = low
    lanes = 2 * CAP
    for j in range(0, TILES, 2):
        tiles = [(me_ref[0] - j - k + TILES) & (TILES - 1) for k in range(2)]
        fields = [jnp.concatenate([obs_ref[t, i : i + 1] for t in tiles], 1) for i in range(5)]
        column, line, row = [(f + 0.5).astype(jnp.int32) for f in fields[:3]]
        across, upward = fields[3:]
        y = lax.broadcasted_iota(jnp.int32, (LANES, lanes), 0)
        here, after = y == line, y == line + 1
        highs, lows = [], []
        for c in range(COLS):
            mine = column == c
            near = jnp.where(mine, 1.0 - across, 0.0)
            far = jnp.where(mine, across, 0.0)
            weight = jnp.where(here, near, jnp.where(after, far, 0.0))
            high, low = two_parts(weight)
            highs.append(high)
            lows.append(low)
        high, low = jnp.concatenate(highs, 0), jnp.concatenate(lows, 0)
        taken = jnp.dot(end_high[...], high, preferred_element_type=F32)
        taken = taken + jnp.dot(end_high[...], low, preferred_element_type=F32)
        taken = taken + jnp.dot(end_low[...], high, preferred_element_type=F32)
        r = lax.broadcasted_iota(jnp.int32, (PAD, lanes), 0)
        weight = jnp.where(r == row, 1.0 - upward, jnp.where(r == row + 1, upward, 0.0))
        value = jnp.sum(weight * taken, axis=0, keepdims=True)
        out_ref[j : j + 1, :] = value[:, :CAP]
        out_ref[j + 1 : j + 2, :] = value[:, CAP:]


def depart_kernel(count_ref, me_ref, back_ref, place_ref, value_ref, out_ref, ready_ref):
    ready_ref[...] = jnp.zeros((8, LANES), F32)
    spread = jnp.dot(
        back_ref[...], spread_of(place_ref[TILES : TILES + 1]), precision=HIGHEST, preferred_element_type=F32
    )
    evolved = jnp.zeros((1, SLOTS), F32)
    for j in range(TILES):
        tile = (me_ref[0] + j) & (TILES - 1)
        evolved = evolved + spread[j : j + 1] * place_ref[pl.ds(tile, 1)]
    live = lax.broadcasted_iota(jnp.int32, (1, SLOTS), 1) < count_ref[0, 0]
    out_ref[...] = jnp.where(live, value_ref[...] - evolved, 0.0)


def ring_step(blocks, by, offsets):
    size = blocks[0].shape[0]
    parcel = jnp.concatenate([blocks[o] for o in offsets], 0)
    parcel = lax.ppermute(parcel, "tile", [(i, (i + by) % TILES) for i in range(TILES)])
    return {o: parcel[at * size : (at + 1) * size] for at, o in enumerate(offsets)}


def give_back(found):
    blocks = {o: found[-o % TILES : -o % TILES + 1] for o in range(-4, 4)}
    for width, forward, backward in ((3, (2, 3), (-4, -3, -2)), (1, (-2, 1), (-4, -1, 2))):
        arrived = {**ring_step(blocks, width, forward), **ring_step(blocks, -width, backward)}
        blocks = {**blocks, **arrived}
    return jnp.concatenate([blocks[-j if j <= 4 else TILES - j] for j in range(TILES)], 0)


def per_device(
    increment, forcing, error_root, physics, coefficients, obs_index, obs_frac, obs_value, obs_count
):
    state = increment.reshape(ROWS, COLS, LANES)
    drive = forcing.reshape(ROWS, COLS, LANES)
    rates = coefficients.reshape(4, COLS, LANES)
    core = jnp.reshape(lax.axis_index("core"), (1,)).astype(jnp.int32)
    me = jnp.reshape(lax.axis_index("tile"), (1,)).astype(jnp.int32)
    field = PAD * COLS * LANES * 4

    to_west = [(i + 1, i) for i in range(TILES - 1)]
    to_east = [(i, i + 1) for i in range(TILES - 1)]

    west, east, sent = pack(state, rates)
    from_west = lax.ppermute(east, "tile", to_east)
    from_east = lax.ppermute(west, "tile", to_west)
    store = shape(STORE, PAD, LANES)
    base, planes, ready = call(
        prepare_kernel,
        [shape(COLS, PAD, LANES), store, shape(8, LANES)],
        (state, drive, error_root, physics.reshape(ROWS, ROWS), sent),
        scratch=[
            pltpu.VMEM((ROWS, COLS, LANES), F32),
            pltpu.VMEM((ROWS, COLS, LANES), F32),
            pltpu.VMEM((ROWS, ROWS), F32),
            pltpu.VMEM((PAD, PAD), F32),
            pltpu.VMEM((PAD, 2 * LANES), F32),
            pltpu.VMEM((COLS, PAD, LANES), F32),
            pltpu.VMEM((COLS, PAD, LANES), F32),
            pltpu.VMEM((4, PAD, LANES), F32),
            pltpu.SemaphoreType.DMA((16,)),
        ],
        flops=10**8,
        moved=10**6,
        far=(0, 1, 2),
        far_out=(0, 1),
        mib=24,
    )
    queries, places = call(
        sort_kernel,
        [shape(TILES, FIELDS, CAP), shape(2 * TILES, SLOTS)],
        (obs_index, obs_frac, ready),
        flops=10**7,
        moved=10**5,
        mib=8,
    )
    arrived = lax.all_to_all(queries, "tile", 0, 0, tiled=True)
    parts = shape(PARTS, PART, LANES)
    wide = COLS + 2 * STEPS
    end, keep, send = call(
        advance_kernel,
        [shape(END_STORE, PAD, LANES), parts, parts],
        (rates, from_west, from_east, core, planes, arrived),
        scratch=[
            pltpu.VMEM((5 * wide, 8, LANES), F32),
            pltpu.VMEM((wide, 2 * LANES, 2 * LANES), BF16),
            pltpu.VMEM((wide, PAD, LANES), F32),
            pltpu.VMEM((wide, PAD, LANES), F32),
            pltpu.VMEM((COLS, PAD, LANES), F32),
            pltpu.VMEM((COLS, PAD, LANES), F32),
            pltpu.VMEM((4, PAD, LANES), F32),
            pltpu.SemaphoreType.DMA((7,)),
        ],
        flops=15 * 10**9,
        moved=6 * field,
        smem=(3,),
        far=(4, 5),
        far_out=(0,),
        mib=36,
    )
    swap = [(0, 1), (1, 0)]
    partner = lax.ppermute(send, "core", swap)
    pair, paired = call(pair_kernel, [parts, shape(8, LANES)], (keep, partner), flops=10**6, moved=2 * field, mib=6)
    gathered = lax.all_to_all(pair, ("y", "x"), 0, 0, tiled=True)
    found = call(
        observe_kernel,
        shape(TILES, CAP),
        (me, arrived, end, paired),
        scratch=[
            pltpu.VMEM((PAD, COLS * LANES), BF16),
            pltpu.VMEM((PAD, COLS * LANES), BF16),
            pltpu.VMEM((COLS, PAD, LANES), F32),
            pltpu.SemaphoreType.DMA((COLS,)),
        ],
        flops=3 * 10**9,
        moved=field,
        smem=(0,),
        far=(2,),
        mib=10,
    )
    totals = call(scan_kernel, parts, (gathered, found), flops=10**7, moved=field, mib=6)
    before = lax.all_to_all(totals, ("y", "x"), 0, 0, tiled=True)
    departure, departed = call(
        depart_kernel,
        [shape(1, SLOTS), shape(8, LANES)],
        (obs_count, me, give_back(found), places, obs_value),
        flops=10**7,
        moved=10**6,
        smem=(0, 1),
        mib=4,
    )
    for_partner = call(
        share_kernel, parts, (core, before, keep, departed), flops=10**7, moved=2 * field, smem=(0,), mib=6
    )
    other = lax.ppermute(for_partner, "core", swap)
    summed = call(
        finish_kernel,
        shape(ROWS, COLS, LANES),
        (core, base, before, partner, other),
        scratch=[pltpu.VMEM((PAD, COLS, LANES), F32), pltpu.SemaphoreType.DMA((4,))],
        flops=10**7,
        moved=4 * field,
        smem=(0,),
        far_out=(0,),
        mib=10,
    )
    return summed.reshape(increment.shape), departure


def solution(mesh):
    split = Mesh(mesh.devices.reshape(GRID_Y, GRID_X, CORES, TILES), ("y", "x", "core", "tile"))
    win = ("y", "x", "core")
    return jax.shard_map(
        per_device,
        mesh=split,
        in_specs=(
            P(win, None, None, "tile", None),
            P(win, None, None, "tile", None),
            P(),
            P(win, None, None),
            P(win, None, "tile", None),
            P(None, win, "tile"),
            P(None, win, "tile"),
            P(win, "tile"),
            P(win, "tile"),
        ),
        out_specs=(P(win, None, None, "tile", None), P(win, "tile")),
        check_vma=False,
    )
```

```python
import jax
import jax.numpy as jnp
from jax import lax
from jax.experimental import pallas as pl
from jax.experimental.pallas import tpu as pltpu
from jax.sharding import Mesh, PartitionSpec as P

STEPS = 6
ROWS = 411
PAD = 416
COLS = 8
LANES = 128
GRID_Y = 4
GRID_X = 4
CORES = 2
PARTS = 16
PART = 104
TILES = 8
HALF = 208
STORE = 160
END_STORE = 320
SLOTS = 512
CAP = 128
FIELDS = 8

F32 = jnp.float32
BF16 = jnp.bfloat16
HIGHEST = lax.Precision.HIGHEST
MIB = 1 << 20
WIDE = 56


def call(body, outs, ins, scratch=(), flops=0, moved=0, smem=(), far=(), far_out=(), mib=WIDE):
    specs = [
        pl.BlockSpec(memory_space=pltpu.SMEM if at in smem else pl.ANY if at in far else pltpu.VMEM)
        for at in range(len(ins))
    ]
    many = isinstance(outs, (list, tuple))
    out_specs = [
        pl.BlockSpec(memory_space=pl.ANY if at in far_out else pltpu.VMEM)
        for at in range(len(outs) if many else 1)
    ]
    return pl.pallas_call(
        body,
        out_shape=outs,
        in_specs=specs,
        out_specs=out_specs if many else out_specs[0],
        scratch_shapes=list(scratch),
        compiler_params=pltpu.CompilerParams(vmem_limit_bytes=mib * MIB),
        cost_estimate=pl.CostEstimate(flops=flops, bytes_accessed=moved, transcendentals=0),
    )(*ins)


def shape(*dims, dtype=F32):
    return jax.ShapeDtypeStruct(dims, dtype)


def two_parts(value):
    high = value.astype(BF16)
    low = (value - high.astype(F32)).astype(BF16)
    return high, low


def product(left_high, left_low, right):
    high, low = two_parts(right)
    total = jnp.dot(left_high, high, preferred_element_type=F32)
    total = total + jnp.dot(left_high, low, preferred_element_type=F32)
    return total + jnp.dot(left_low, high, preferred_element_type=F32)


def pack_kernel(inc_ref, rate_ref, west_ref, east_ref, sent_ref, held, rates, west, east, in_sems, out_sems):
    count = PAD // PART
    incoming = [pltpu.make_async_copy(rate_ref, rates, in_sems.at[count])]
    for b in range(count):
        rows = pl.ds(b * PART, min(PART, ROWS - b * PART))
        incoming.append(pltpu.make_async_copy(inc_ref.at[rows], held.at[rows], in_sems.at[b]))
    for copy in incoming:
        copy.start()
    sent_ref[...] = jnp.zeros((8, LANES), F32)
    flat = held.reshape(PAD * COLS, LANES)
    outgoing = []
    incoming[0].wait()
    for b in range(count):
        incoming[b + 1].wait()
        size = min(PART, ROWS - b * PART)
        for c in range(COLS):
            column = flat[pl.ds(b * PART * COLS + c, size, stride=COLS), :]
            if size < PART:
                weights = [rates[i, c : c + 1, :] for i in range(4)]
                column = jnp.concatenate([column] + weights + [jnp.zeros((1, LANES), F32)], 0)
            if c < STEPS:
                west[c, b * PART : (b + 1) * PART, :] = column
            if c >= COLS - STEPS:
                east[c - COLS + STEPS, b * PART : (b + 1) * PART, :] = column
        rows = pl.ds(b * PART, PART)
        outgoing.append(pltpu.make_async_copy(west.at[:, rows], west_ref.at[:, rows], out_sems.at[2 * b]))
        outgoing.append(pltpu.make_async_copy(east.at[:, rows], east_ref.at[:, rows], out_sems.at[2 * b + 1]))
        outgoing[-2].start()
        outgoing[-1].start()
    for copy in outgoing:
        copy.wait()


def pack(state, rates):
    halo = shape(STEPS, PAD, LANES)
    return call(
        pack_kernel,
        [halo, halo, shape(8, LANES)],
        (state, rates),
        scratch=[
            pltpu.VMEM((PAD, COLS, LANES), F32),
            pltpu.VMEM((4, COLS, LANES), F32),
            pltpu.VMEM((STEPS, PAD, LANES), F32),
            pltpu.VMEM((STEPS, PAD, LANES), F32),
            pltpu.SemaphoreType.DMA((PAD // PART + 1,)),
            pltpu.SemaphoreType.DMA((2 * PAD // PART,)),
        ],
        moved=3 * PAD * COLS * LANES * 4,
        far=(0, 1),
        far_out=(0, 1),
    )


def prepare_kernel(
    inc_ref, forcing_ref, root_ref, physics_ref, order_ref, base_ref, store_ref, ready_ref,
    start, force, root, square, drive, base, columns, powers, sems
):
    incoming = [
        pltpu.make_async_copy(root_ref, root, sems.at[0]),
        pltpu.make_async_copy(forcing_ref, force, sems.at[1]),
        pltpu.make_async_copy(inc_ref, start, sems.at[2]),
    ]
    for copy in incoming:
        copy.start()
    ready_ref[...] = jnp.zeros((8, LANES), F32)
    square[...] = jnp.zeros((PAD, PAD), F32)
    square[:ROWS, :ROWS] = 0.2 * physics_ref[...]
    once = square[...]
    twice = 2.0 * once + product(*two_parts(once), once)
    twice_parts = two_parts(twice)
    four = 2.0 * twice + product(*twice_parts, twice)
    six = twice + four + product(*twice_parts, four)
    powers[3] = jnp.zeros((PAD, LANES), F32)
    for p in range(4):
        width = min(LANES, PAD - p * LANES)
        powers[p, :, :width] = six[:, p * LANES : p * LANES + width]
    outgoing = [pltpu.make_async_copy(powers, store_ref.at[pl.ds(2 * COLS, 4)], sems.at[3])]
    outgoing[0].start()
    for copy in incoming:
        copy.wait()
    square[:ROWS, :ROWS] = root[...]
    root_high, root_low = two_parts(square[...])
    force_flat = force.reshape(ROWS * COLS, LANES)
    start_flat = start.reshape(ROWS * COLS, LANES)
    drive[ROWS - 3 :, :] = jnp.zeros((PAD - ROWS + 3, 2 * LANES), F32)
    for c in range(0, COLS, 2):
        drive[:ROWS, :LANES] = force_flat[pl.ds(c, ROWS, stride=COLS), :]
        drive[:ROWS, LANES:] = force_flat[pl.ds(c + 1, ROWS, stride=COLS), :]
        forced = product(root_high, root_low, drive[...])
        for k in range(2):
            column = start_flat[pl.ds(c + k, ROWS, stride=COLS), :]
            taken = forced[:, k * LANES : (k + 1) * LANES]
            columns[c + k, :ROWS, :] = column
            columns[c + k, ROWS:, :] = jnp.zeros((PAD - ROWS, LANES), F32)
            base[c + k, :ROWS, :] = column - taken[:ROWS]
            base[c + k, ROWS:, :] = taken[ROWS:]
        pair, beyond = pl.ds(c, 2), pl.ds(COLS + c, 2)
        outgoing.append(pltpu.make_async_copy(base.at[pair], base_ref.at[pair], sems.at[4 + c // 2]))
        outgoing.append(pltpu.make_async_copy(base.at[pair], store_ref.at[pair], sems.at[8 + c // 2]))
        outgoing.append(pltpu.make_async_copy(columns.at[pair], store_ref.at[beyond], sems.at[12 + c // 2]))
        for copy in outgoing[-3:]:
            copy.start()
    for copy in outgoing:
        copy.wait()


def advance_kernel(
    rate_ref, west_ref, east_ref, core_ref, store_ref, order_ref,
    end_ref, keep_ref, send_ref, table, band, odd, even, end_held, base, powers, sems
):
    own = pltpu.make_async_copy(store_ref.at[pl.ds(COLS, COLS)], even.at[pl.ds(STEPS, COLS)], sems.at[0])
    own.start()
    later = [
        pltpu.make_async_copy(store_ref.at[pl.ds(2 * COLS, 4)], powers, sems.at[1]),
        pltpu.make_async_copy(store_ref.at[pl.ds(0, COLS)], base, sems.at[2]),
    ]
    for copy in later:
        copy.start()
    row = lax.broadcasted_iota(jnp.int32, (LANES, LANES), 0)
    lane = lax.broadcasted_iota(jnp.int32, (LANES, LANES), 1)
    wide = COLS + 2 * STEPS
    for j in range(1, wide - 1):
        if j < STEPS:
            rates = [west_ref[j, ROWS + i : ROWS + i + 1, :] for i in range(4)]
        elif j < STEPS + COLS:
            rates = [rate_ref[i, j - STEPS : j - STEPS + 1, :] for i in range(4)]
        else:
            rates = [east_ref[j - STEPS - COLS, ROWS + i : ROWS + i + 1, :] for i in range(4)]
        center = 1.0 - (rates[0] + rates[1] + rates[2] + rates[3])
        table[2 * j] = jnp.broadcast_to(rates[0], (8, LANES))
        table[2 * j + 1] = jnp.broadcast_to(rates[1], (8, LANES))
        along = jnp.where(row == lane, center, 0.0)
        along = jnp.where(row == lane + 1, rates[2], along)
        along = jnp.where(row == lane - 1, rates[3], along)
        along_high, along_low = two_parts(along)
        band[j, :LANES, :LANES] = along_high
        band[j, LANES:, :LANES] = along_high
        band[j, :LANES, LANES:] = along_low
        band[j, LANES:, LANES:] = jnp.zeros((LANES, LANES), BF16)
    def load(step, j, rows):
        if step == 0 and j < STEPS:
            return west_ref[j, rows, :]
        if step == 0 and j >= STEPS + COLS:
            return east_ref[j - STEPS - COLS, rows, :]
        return (odd if step % 2 else even)[j, rows, :]

    def tiles(value):
        return value.reshape(value.shape[0] // 8, 8, LANES)

    def finish(step, j, rows, total):
        total = total + table[2 * j] * tiles(load(step - 1, j + 1, rows))
        total = total + table[2 * j + 1] * tiles(load(step - 1, j - 1, rows))
        total = total.reshape(total.shape[0] * 8, LANES)
        if step == STEPS:
            end_held[j - STEPS, rows, :] = total
        else:
            (odd if step % 2 else even)[j, rows, :] = total

    quarters = [slice(q * PART, (q + 1) * PART) for q in range(4)]
    for step in range(1, STEPS + 1):
        order = list(range(step, wide - step))
        if step == 1:
            apart = [j for j in order if j < STEPS - 1 or j > STEPS + COLS]
            order = apart + [j for j in order if j not in apart]
        for j in order:
            if step == 1 and j == STEPS - 1:
                own.wait()
            parts = jnp.concatenate(two_parts(load(step - 1, j, slice(None))), 1)
            along = jnp.dot(parts, band[j], preferred_element_type=F32)
            for rows in quarters:
                finish(step, j, rows, tiles(along[rows, :LANES] + along[rows, LANES:]))

    for copy in later:
        copy.wait()
    high, low = two_parts(jnp.concatenate([powers[p] for p in range(4)], 1)[:, :PAD])
    core = core_ref[0]
    outgoing = []
    for kind, out_ref in ((1, send_ref), (0, keep_ref)):
        start = 4 * (core ^ kind)
        for i in (0, 2):
            c = start + i
            column = jnp.concatenate([end_held[c], end_held[c + 1]], 1)
            end = column + product(high, low, column)
            for k in range(2):
                column = end[:, k * LANES : (k + 1) * LANES]
                end_held[c + k] = column
                rest = base[c + k] - column
                for q in range(4):
                    out_ref[4 * (i + k) + q] = rest[q * PART : (q + 1) * PART]
            pair = pl.ds(c, 2)
            outgoing.append(pltpu.make_async_copy(end_held.at[pair], end_ref.at[pair], sems.at[3 + 2 * kind + i // 2]))
            outgoing[-1].start()
    for copy in outgoing:
        copy.wait()


def pair_kernel(keep_ref, partner_ref, pair_ref, ready_ref):
    pair_ref[...] = keep_ref[...] + partner_ref[...]
    ready_ref[...] = jnp.zeros((8, LANES), F32)


def scan_kernel(in_ref, order_ref, out_ref):
    def block(index, carry):
        here = pl.ds(pl.multiple_of(index * 8, 8), 8)
        total = jnp.zeros((8, LANES), F32)
        for k in range(PARTS):
            out_ref[k, here, :] = total
            total = total + in_ref[k, here, :]
        return carry

    lax.fori_loop(0, PART // 8, block, 0)


def share_kernel(core_ref, before_ref, keep_ref, order_ref, out_ref):
    first = (core_ref[0] == 0).astype(F32)
    out_ref[...] = before_ref[...] + first * keep_ref[...]


def finish_kernel(core_ref, base_ref, before_ref, partner_ref, other_ref, out_ref, out, sems):
    core = core_ref[0]
    flat = out.reshape(PAD * COLS, LANES)
    second = (core == 1).astype(F32)
    outgoing = []
    for q in range(4):
        for c in range(COLS):
            at = 4 * (c % 4) + q
            own = before_ref[at] + second * partner_ref[at]
            earlier = jnp.where(core == c // 4, own, other_ref[at])
            flat[pl.ds(q * PART * COLS + c, PART, stride=COLS), :] = (
                base_ref[c, q * PART : (q + 1) * PART, :] + earlier
            )
        rows = pl.ds(q * PART, min(PART, ROWS - q * PART))
        outgoing.append(pltpu.make_async_copy(out.at[rows], out_ref.at[rows], sems.at[q]))
        outgoing[-1].start()
    for copy in outgoing:
        copy.wait()


def spread_of(place):
    return (lax.broadcasted_iota(jnp.int32, (CAP, SLOTS), 0) == place.astype(jnp.int32)).astype(F32)


def sort_kernel(index_ref, frac_ref, order_ref, out_ref, place_ref):
    column_x = index_ref[0]
    bucket = lax.broadcasted_iota(jnp.int32, (TILES, SLOTS), 0)
    chosen = (bucket == (column_x >> 3)).astype(F32)
    before = lax.broadcasted_iota(jnp.int32, (SLOTS, SLOTS), 0) < lax.broadcasted_iota(jnp.int32, (SLOTS, SLOTS), 1)
    rank = jnp.dot(chosen.astype(BF16), before.astype(F32).astype(BF16), preferred_element_type=F32)
    place = jnp.sum(chosen * rank, axis=0, keepdims=True)
    spread = spread_of(place)
    place_ref[:TILES] = chosen
    place_ref[TILES:] = jnp.broadcast_to(place, (TILES, SLOTS))
    values = jnp.concatenate(
        [
            (column_x & (COLS - 1)).astype(F32),
            index_ref[1].astype(F32),
            index_ref[2].astype(F32),
            frac_ref[0],
            frac_ref[1],
            jnp.zeros((FIELDS - 5, SLOTS), F32),
        ],
        0,
    )
    for j in range(TILES):
        masked = values * chosen[j : j + 1, :]
        out_ref[j] = lax.dot_general(
            masked, spread, (((1,), (1,)), ((), ())), precision=HIGHEST, preferred_element_type=F32
        )


def observe_kernel(me_ref, obs_ref, end_ref, order_ref, out_ref, end_high, end_low, end, sems):
    copies = [pltpu.make_async_copy(end_ref.at[c], end.at[c], sems.at[c]) for c in range(COLS)]
    for copy in copies:
        copy.start()
    for c in range(COLS):
        copies[c].wait()
        high, low = two_parts(end[c])
        end_high[:, c * LANES : (c + 1) * LANES] = high
        end_low[:, c * LANES : (c + 1) * LANES] = low
    lanes = 2 * CAP
    for j in range(0, TILES, 2):
        tiles = [(me_ref[0] - j - k + TILES) & (TILES - 1) for k in range(2)]
        fields = [jnp.concatenate([obs_ref[t, i : i + 1] for t in tiles], 1) for i in range(5)]
        column, line, row = [(f + 0.5).astype(jnp.int32) for f in fields[:3]]
        across, upward = fields[3:]
        y = lax.broadcasted_iota(jnp.int32, (LANES, lanes), 0)
        here, after = y == line, y == line + 1
        highs, lows = [], []
        for c in range(COLS):
            mine = column == c
            near = jnp.where(mine, 1.0 - across, 0.0)
            far = jnp.where(mine, across, 0.0)
            weight = jnp.where(here, near, jnp.where(after, far, 0.0))
            high, low = two_parts(weight)
            highs.append(high)
            lows.append(low)
        high, low = jnp.concatenate(highs, 0), jnp.concatenate(lows, 0)
        taken = jnp.dot(end_high[...], high, preferred_element_type=F32)
        taken = taken + jnp.dot(end_high[...], low, preferred_element_type=F32)
        taken = taken + jnp.dot(end_low[...], high, preferred_element_type=F32)
        r = lax.broadcasted_iota(jnp.int32, (PAD, lanes), 0)
        weight = jnp.where(r == row, 1.0 - upward, jnp.where(r == row + 1, upward, 0.0))
        value = jnp.sum(weight * taken, axis=0, keepdims=True)
        out_ref[j : j + 1, :] = value[:, :CAP]
        out_ref[j + 1 : j + 2, :] = value[:, CAP:]


def depart_kernel(count_ref, me_ref, back_ref, place_ref, value_ref, out_ref, ready_ref):
    ready_ref[...] = jnp.zeros((8, LANES), F32)
    spread = jnp.dot(
        back_ref[...], spread_of(place_ref[TILES : TILES + 1]), precision=HIGHEST, preferred_element_type=F32
    )
    evolved = jnp.zeros((1, SLOTS), F32)
    for j in range(TILES):
        tile = (me_ref[0] + j) & (TILES - 1)
        evolved = evolved + spread[j : j + 1] * place_ref[pl.ds(tile, 1)]
    live = lax.broadcasted_iota(jnp.int32, (1, SLOTS), 1) < count_ref[0, 0]
    out_ref[...] = jnp.where(live, value_ref[...] - evolved, 0.0)


def ring_step(blocks, by, offsets):
    size = blocks[0].shape[0]
    parcel = jnp.concatenate([blocks[o] for o in offsets], 0)
    parcel = lax.ppermute(parcel, "tile", [(i, (i + by) % TILES) for i in range(TILES)])
    return {o: parcel[at * size : (at + 1) * size] for at, o in enumerate(offsets)}


def give_back(found):
    blocks = {o: found[-o % TILES : -o % TILES + 1] for o in range(-4, 4)}
    for width, forward, backward in ((3, (2, 3), (-4, -3, -2)), (1, (-2, 1), (-4, -1, 2))):
        arrived = {**ring_step(blocks, width, forward), **ring_step(blocks, -width, backward)}
        blocks = {**blocks, **arrived}
    return jnp.concatenate([blocks[-j if j <= 4 else TILES - j] for j in range(TILES)], 0)


def per_device(
    increment, forcing, error_root, physics, coefficients, obs_index, obs_frac, obs_value, obs_count
):
    state = increment.reshape(ROWS, COLS, LANES)
    drive = forcing.reshape(ROWS, COLS, LANES)
    rates = coefficients.reshape(4, COLS, LANES)
    core = jnp.reshape(lax.axis_index("core"), (1,)).astype(jnp.int32)
    me = jnp.reshape(lax.axis_index("tile"), (1,)).astype(jnp.int32)
    field = PAD * COLS * LANES * 4

    to_west = [(i + 1, i) for i in range(TILES - 1)]
    to_east = [(i, i + 1) for i in range(TILES - 1)]

    west, east, sent = pack(state, rates)
    from_west = lax.ppermute(east, "tile", to_east)
    from_east = lax.ppermute(west, "tile", to_west)
    store = shape(STORE, PAD, LANES)
    base, planes, ready = call(
        prepare_kernel,
        [shape(COLS, PAD, LANES), store, shape(8, LANES)],
        (state, drive, error_root, physics.reshape(ROWS, ROWS), sent),
        scratch=[
            pltpu.VMEM((ROWS, COLS, LANES), F32),
            pltpu.VMEM((ROWS, COLS, LANES), F32),
            pltpu.VMEM((ROWS, ROWS), F32),
            pltpu.VMEM((PAD, PAD), F32),
            pltpu.VMEM((PAD, 2 * LANES), F32),
            pltpu.VMEM((COLS, PAD, LANES), F32),
            pltpu.VMEM((COLS, PAD, LANES), F32),
            pltpu.VMEM((4, PAD, LANES), F32),
            pltpu.SemaphoreType.DMA((16,)),
        ],
        flops=10**8,
        moved=10**6,
        far=(0, 1, 2),
        far_out=(0, 1),
        mib=24,
    )
    queries, places = call(
        sort_kernel,
        [shape(TILES, FIELDS, CAP), shape(2 * TILES, SLOTS)],
        (obs_index, obs_frac, ready),
        flops=10**7,
        moved=10**5,
        mib=8,
    )
    arrived = lax.all_to_all(queries, "tile", 0, 0, tiled=True)
    parts = shape(PARTS, PART, LANES)
    wide = COLS + 2 * STEPS
    end, keep, send = call(
        advance_kernel,
        [shape(END_STORE, PAD, LANES), parts, parts],
        (rates, from_west, from_east, core, planes, arrived),
        scratch=[
            pltpu.VMEM((2 * wide, 8, LANES), F32),
            pltpu.VMEM((wide, 2 * LANES, 2 * LANES), BF16),
            pltpu.VMEM((wide, PAD, LANES), F32),
            pltpu.VMEM((wide, PAD, LANES), F32),
            pltpu.VMEM((COLS, PAD, LANES), F32),
            pltpu.VMEM((COLS, PAD, LANES), F32),
            pltpu.VMEM((4, PAD, LANES), F32),
            pltpu.SemaphoreType.DMA((7,)),
        ],
        flops=15 * 10**9,
        moved=6 * field,
        smem=(3,),
        far=(4, 5),
        far_out=(0,),
        mib=36,
    )
    swap = [(0, 1), (1, 0)]
    partner = lax.ppermute(send, "core", swap)
    pair, paired = call(pair_kernel, [parts, shape(8, LANES)], (keep, partner), flops=10**6, moved=2 * field, mib=6)
    gathered = lax.all_to_all(pair, ("y", "x"), 0, 0, tiled=True)
    found = call(
        observe_kernel,
        shape(TILES, CAP),
        (me, arrived, end, paired),
        scratch=[
            pltpu.VMEM((PAD, COLS * LANES), BF16),
            pltpu.VMEM((PAD, COLS * LANES), BF16),
            pltpu.VMEM((COLS, PAD, LANES), F32),
            pltpu.SemaphoreType.DMA((COLS,)),
        ],
        flops=3 * 10**9,
        moved=field,
        smem=(0,),
        far=(2,),
        mib=10,
    )
    totals = call(scan_kernel, parts, (gathered, found), flops=10**7, moved=field, mib=6)
    before = lax.all_to_all(totals, ("y", "x"), 0, 0, tiled=True)
    departure, departed = call(
        depart_kernel,
        [shape(1, SLOTS), shape(8, LANES)],
        (obs_count, me, give_back(found), places, obs_value),
        flops=10**7,
        moved=10**6,
        smem=(0, 1),
        mib=4,
    )
    for_partner = call(
        share_kernel, parts, (core, before, keep, departed), flops=10**7, moved=2 * field, smem=(0,), mib=6
    )
    other = lax.ppermute(for_partner, "core", swap)
    summed = call(
        finish_kernel,
        shape(ROWS, COLS, LANES),
        (core, base, before, partner, other),
        scratch=[pltpu.VMEM((PAD, COLS, LANES), F32), pltpu.SemaphoreType.DMA((4,))],
        flops=10**7,
        moved=4 * field,
        smem=(0,),
        far_out=(0,),
        mib=10,
    )
    return summed.reshape(increment.shape), departure


def solution(mesh):
    split = Mesh(mesh.devices.reshape(GRID_Y, GRID_X, CORES, TILES), ("y", "x", "core", "tile"))
    win = ("y", "x", "core")
    return jax.shard_map(
        per_device,
        mesh=split,
        in_specs=(
            P(win, None, None, "tile", None),
            P(win, None, None, "tile", None),
            P(),
            P(win, None, None),
            P(win, None, "tile", None),
            P(None, win, "tile"),
            P(None, win, "tile"),
            P(win, "tile"),
            P(win, "tile"),
        ),
        out_specs=(P(win, None, None, "tile", None), P(win, "tile")),
        check_vma=False,
    )
```
